32 devices in a mesh: dp: 16 (over z, x, core), tensor: 2 (over y).
Axes of the slice: x: 2, y: 2, z: 4, core: 2. Of those that a mesh axis runs over, the one named last changes fastest.
Arguments:
- inputs: bfloat16 [16, 2, 320, 2048], P(None, 'tensor', 'dp'), may hold values from -6 to 6
- lengths: int32 [16], replicated, may hold values from 160 to 640, as said below
- dealing: int32 [16], replicated, may hold values from 0 to 15, each once
- w_query: bfloat16 [2048, 2048], P('dp', 'tensor'), may hold values from -0.125 to 0.125
- w_key: bfloat16 [2048, 2048], P('dp', 'tensor'), may hold values from -0.125 to 0.125
- w_value: bfloat16 [2048, 2048], P('dp', 'tensor'), may hold values from -0.125 to 0.125
- b_query: float32 [2048], replicated, may hold values from -3 to 3
- b_value: float32 [2048], replicated, may hold values from -3 to 3
- w_out: bfloat16 [2048, 2048], P('tensor', 'dp'), may hold values from -0.5 to 0.5
- b_out: float32 [2048], replicated, may hold values from -3 to 3
- gain_first: float32 [2048], replicated, may hold values from 0.5 to 1.5
- shift_first: float32 [2048], replicated, may hold values from -3 to 3
- w_up: bfloat16 [2048, 8192], P('dp', 'tensor'), may hold values from -0.125 to 0.125
- b_up: float32 [8192], replicated, may hold values from -3 to 3
- w_down: bfloat16 [8192, 2048], P('tensor', 'dp'), may hold values from -0.0625 to 0.0625
- b_down: float32 [2048], replicated, may hold values from -3 to 3
- gain_second: float32 [2048], replicated, may hold values from 0.5 to 1.5
- shift_second: float32 [2048], replicated, may hold values from -3 to 3
- cotangent: bfloat16 [16, 640, 2048], P('dp', 'tensor'), may hold values from -6 to 6
Outputs:
- output: bfloat16 [16, 640, 2048], P('dp', 'tensor')
- grad_inputs: bfloat16 [16, 2, 320, 2048], P(None, 'tensor', 'dp')
- grad_w_query: float32 [2048, 2048], P('dp', 'tensor')
- grad_w_key: float32 [2048, 2048], P('dp', 'tensor')
- grad_w_value: float32 [2048, 2048], P('dp', 'tensor')
- grad_b_query: float32 [2048], replicated
- grad_b_value: float32 [2048], replicated
- grad_w_out: float32 [2048, 2048], P('tensor', 'dp')
- grad_b_out: float32 [2048], replicated
- grad_gain_first: float32 [2048], replicated
- grad_shift_first: float32 [2048], replicated
- grad_w_up: float32 [2048, 8192], P('dp', 'tensor')
- grad_b_up: float32 [8192], replicated
- grad_w_down: float32 [8192, 2048], P('tensor', 'dp')
- grad_b_down: float32 [2048], replicated
- grad_gain_second: float32 [2048], replicated
- grad_shift_second: float32 [2048], replicated
The draws below stay inside these ranges and needn't reach their ends.
Inputs may be any that keep to these rules, and one draw needn't show every extreme that they name: `lengths`: every sequence has 160 live tokens or more; one sequence has all 640.
All inputs are finite; a program needn't handle non-finite values.
Results may differ from the reference program's by a relative error of at most 0.017.
Values may be sent and summed in bfloat16 or wider, within the bound.
A program may use at most 256 MiB of HBM per device.

```python
import jax
import jax.numpy as jnp
from jax import lax

D = 2048
HEADS = 16
HEAD_DIM = 128
FF = 8192
L = 640
NSEQ = 16
HALF = 320
N_TENSOR = 2


def draw_lengths(key, part):
    key = jax.random.fold_in(key, 11)
    first_key, second_key = jax.random.split(key)
    drawn = jax.random.randint(first_key, (NSEQ,), L // 4, L + 1)
    longest = jax.random.randint(second_key, (), 0, NSEQ)
    return jnp.where(jnp.arange(NSEQ) == longest, L, drawn).astype(jnp.int32)


def block_levels(key, extent, cuts, low, largest):
    loudness, own = 1.0, jax.random.fold_in(key, 6)
    for axis_at, shards_of in cuts:
        heights = jnp.exp(jax.random.uniform(jax.random.fold_in(own, axis_at), (shards_of,), jnp.float32, low / len(cuts), largest / len(cuts)))
        loudness = loudness * jnp.repeat(heights, extent[axis_at] // shards_of).reshape([-1 if axis == axis_at else 1 for axis in range(len(extent))])
    return loudness


def noise(key, dims, scale, limit, pieces=(), dtype=jnp.bfloat16):
    loudness = block_levels(key, dims, pieces, -0.22, 0.18) if pieces else 1.0
    values = jax.random.normal(key, dims, jnp.float32) * scale * loudness
    return jnp.minimum(jnp.maximum(values, -limit), limit).astype(dtype)


def setup_inputs(seed: int = 0) -> dict:
    arg_keys = jax.random.split(jax.random.key(seed), 20)
    return {
        "inputs": noise(arg_keys[0], (NSEQ, N_TENSOR, HALF, D), 1.0, 6.0, ((1, 2), (2, 16))),
        "lengths": draw_lengths(jax.random.fold_in(arg_keys[19], 71), 0),
        "dealing": jax.random.permutation(arg_keys[2], NSEQ).astype(jnp.int32),
        "w_query": noise(arg_keys[3], (D, D), D ** -0.5, 0.125, ((0, 16), (1, 2))),
        "w_key": noise(arg_keys[4], (D, D), D ** -0.5, 0.125, ((0, 16), (1, 2))),
        "w_value": noise(arg_keys[5], (D, D), D ** -0.5, 0.125, ((0, 16), (1, 2))),
        "b_query": noise(arg_keys[6], (D,), 0.5, 3.0, (), jnp.float32),
        "b_value": noise(arg_keys[7], (D,), 0.5, 3.0, (), jnp.float32),
        "w_out": noise(arg_keys[8], (D, D), (D // 16) ** -0.5, 0.5, ((0, 2), (1, 16))),
        "b_out": noise(arg_keys[9], (D,), 0.5, 3.0, (), jnp.float32),
        "gain_first": jnp.clip(1.0 + 0.1 * jax.random.normal(arg_keys[10], (D,), jnp.float32), 0.5, 1.5),
        "shift_first": noise(arg_keys[11], (D,), 0.5, 3.0, (), jnp.float32),
        "w_up": noise(arg_keys[12], (D, FF), D ** -0.5, 0.125, ((0, 16), (1, 2))),
        "b_up": noise(arg_keys[13], (FF,), 0.5, 3.0, (), jnp.float32),
        "w_down": noise(arg_keys[14], (FF, D), FF ** -0.5, 0.0625, ((0, 2), (1, 16))),
        "b_down": noise(arg_keys[15], (D,), 0.5, 3.0, (), jnp.float32),
        "gain_second": jnp.clip(1.0 + 0.1 * jax.random.normal(arg_keys[16], (D,), jnp.float32), 0.5, 1.5),
        "shift_second": noise(arg_keys[17], (D,), 0.5, 3.0, (), jnp.float32),
        "cotangent": noise(arg_keys[18], (NSEQ, L, D), 1.0, 6.0, ((0, 16), (1, 2))),
    }


@jax.custom_vjp
def low(v):
    return lax.optimization_barrier(v.astype(jnp.bfloat16)).astype(jnp.float32)

@jax.custom_vjp
def low_back(v):
    return v

def low_keep(v):
    return (low(v), None)

def low_pass(kept, grad):
    return (grad,)

def back_keep(v):
    return (v, None)

def back_low(kept, grad):
    return (low(grad),)
low.defvjp(low_keep, low_pass)
low_back.defvjp(back_keep, back_low)
EPSILON = 1e-05
MASKED = -1e+30
BEST_PRECISION = lax.Precision.HIGHEST

def matmul(left, right):
    return jnp.dot(left, right, precision=BEST_PRECISION, preferred_element_type=jnp.float32)

def layer_norm(values, scale_gain, bias_shift):
    center = values - lax.optimization_barrier(jnp.mean(values, axis=-1, keepdims=True))
    spread = lax.optimization_barrier(jnp.mean(center * center, axis=-1, keepdims=True))
    return center * lax.rsqrt(spread + EPSILON) * scale_gain + bias_shift

def round_both(values):
    return low_back(low(values))

def forward_seq(params, sequence, length):
    w_query, w_key, w_value, b_query, b_value, w_out, b_out, gain_first, shift_first, w_up, b_up, w_down, b_down, gain_second, shift_second = params
    seq_len = sequence.shape[0]
    query_rows = round_both(matmul(sequence, w_query) + b_query).reshape(seq_len, HEADS, HEAD_DIM)
    key_rows = round_both(matmul(sequence, w_key)).reshape(seq_len, HEADS, HEAD_DIM)
    value_rows = round_both(matmul(sequence, w_value) + b_value).reshape(seq_len, HEADS, HEAD_DIM)
    scores = jnp.einsum('qhd,khd->hqk', query_rows, key_rows, precision=BEST_PRECISION) * HEAD_DIM ** (-0.5)
    key_valid = jnp.arange(seq_len) < length
    scores = low_back(jnp.where(key_valid[None, None, :], scores, MASKED))
    softmax_out = jax.nn.softmax(scores, axis=-1)
    mixed_heads = jnp.einsum('hqk,khd->qhd', low(softmax_out), value_rows, precision=BEST_PRECISION)
    mixed_heads = round_both(mixed_heads.reshape(seq_len, HEADS * HEAD_DIM))
    attended = low_back(matmul(mixed_heads, w_out) + b_out)
    hidden = layer_norm(sequence + attended, gain_first, shift_first)
    upward = low_back(matmul(low(hidden), w_up) + b_up)
    active = low(jax.nn.gelu(upward, approximate=True))
    downward = low_back(matmul(active, w_down) + b_down)
    return layer_norm(hidden + downward, gain_second, shift_second)

def reference(inputs, lengths, dealing, w_query, w_key, w_value, b_query, b_value, w_out, b_out, gain_first, shift_first, w_up, b_up, w_down, b_down, gain_second, shift_second, cotangent):
    params = tuple((array.astype(jnp.float32) for array in (w_query, w_key, w_value, b_query, b_value, w_out, b_out, gain_first, shift_first, w_up, b_up, w_down, b_down, gain_second, shift_second)))
    sequences = inputs.astype(jnp.float32).reshape(NSEQ, L, D)[dealing]
    seq_lengths = lengths[dealing]
    cotangents = cotangent.astype(jnp.float32)
    zero_grads = tuple((jnp.zeros_like(array) for array in params))

    def scan_step(totals, scan_item):
        sequence, length, seq_cotangent = scan_item

        def apply_layer(param_set, values):
            return forward_seq(param_set, values, length)
        result, pullback = jax.vjp(apply_layer, params, sequence)
        grad_params, grad_sequence = pullback(seq_cotangent)
        totals = tuple((first + second for first, second in zip(totals, grad_params)))
        return (totals, (result, grad_sequence))
    totals, (results, grad_sequences) = lax.scan(scan_step, zero_grads, (sequences, seq_lengths, cotangents))
    grad_given = jnp.zeros_like(grad_sequences).at[dealing].set(grad_sequences)
    grad_given = grad_given.reshape(NSEQ, N_TENSOR, HALF, D).astype(jnp.bfloat16)
    return (results.astype(jnp.bfloat16), grad_given, totals[0], totals[1], totals[2], totals[3], totals[4], totals[5], totals[6], totals[7], totals[8], totals[9], totals[10], totals[11], totals[12], totals[13], totals[14])
```

```python
from functools import partial

import jax
import jax.numpy as jnp
from jax import lax
from jax.sharding import PartitionSpec as P

HEAD_DIM = 128


EPSILON = 1e-05
MASKED = -1e30


def norm_forward(values, scale_gain, bias_shift):
    center = values - jnp.mean(values, axis=-1, keepdims=True)
    inverse = lax.rsqrt(jnp.mean(center * center, axis=-1, keepdims=True) + EPSILON)
    normed = center * inverse
    return (normed * scale_gain + bias_shift, normed, inverse)


def norm_backward(grad_out, scale_gain, normed, inverse):
    scaled = grad_out * scale_gain
    grad_in = inverse * (
        scaled
        - jnp.mean(scaled, axis=-1, keepdims=True)
        - normed * jnp.mean(scaled * normed, axis=-1, keepdims=True)
    )
    return (grad_in, jnp.sum(grad_out * normed, axis=0), jnp.sum(grad_out, axis=0))


def contract_rows(left, right):
    return lax.dot_general(
        left, right, (((0,), (0,)), ((), ())), preferred_element_type=jnp.float32
    )


def contract_cols(left, right):
    return lax.dot_general(
        left, right, (((1,), (1,)), ((), ())), preferred_element_type=jnp.float32
    )


def attention_scores(query_rows, key_rows, key_valid, factor):
    scores = (
        jnp.einsum("qhd,khd->hqk", query_rows, key_rows, preferred_element_type=jnp.float32)
        * factor
    )
    return jnp.where(key_valid[None, None, :], scores, MASKED)


def place_slice(local_sum, full_size, offset):
    return lax.dynamic_update_slice_in_dim(
        jnp.zeros((full_size,), jnp.float32), local_sum, offset, 0
    )


def shards(
    inputs,
    lengths,
    dealing,
    w_query,
    w_key,
    w_value,
    b_query,
    b_value,
    w_out,
    b_out,
    gain_first,
    shift_first,
    w_up,
    b_up,
    w_down,
    b_down,
    gain_second,
    shift_second,
    cotangent,
):
    group_index = lax.axis_index("dp")
    tensor_index = lax.axis_index("tensor")
    ordered = jnp.take(inputs, dealing, axis=0)
    arrived = lax.all_to_all(ordered, "dp", split_axis=0, concat_axis=2, tiled=True)
    features = arrived.shape[3]
    half_rows = arrived.shape[2]
    own_rows = arrived.reshape(half_rows, features)
    seq_len = half_rows * lax.axis_size("tensor")
    length = lengths[dealing[group_index]]
    key_valid = jnp.arange(seq_len) < length
    factor = HEAD_DIM ** (-0.5)
    gathered = (
        lax.all_gather(w_query, "dp", axis=0, tiled=True),
        lax.all_gather(w_key, "dp", axis=0, tiled=True),
        lax.all_gather(w_value, "dp", axis=0, tiled=True),
        lax.all_gather(w_out, "dp", axis=1, tiled=True),
        lax.all_gather(w_up, "dp", axis=0, tiled=True),
        lax.all_gather(w_down, "dp", axis=1, tiled=True),
    )
    query_full, key_full, value_full, out_full, up_full, down_full = gathered
    head_cols = query_full.shape[1]
    heads_local = head_cols // HEAD_DIM
    up_cols = up_full.shape[1]
    query_bias = lax.dynamic_slice_in_dim(b_query, tensor_index * head_cols, head_cols)
    value_bias = lax.dynamic_slice_in_dim(b_value, tensor_index * head_cols, head_cols)
    up_bias = lax.dynamic_slice_in_dim(b_up, tensor_index * up_cols, up_cols)
    full_in = lax.all_gather(own_rows, "tensor", axis=0, tiled=True)
    query_rows = (
        jnp.dot(full_in, query_full, preferred_element_type=jnp.float32) + query_bias
    ).astype(jnp.bfloat16)
    key_rows = jnp.dot(full_in, key_full, preferred_element_type=jnp.float32).astype(jnp.bfloat16)
    value_rows = (
        jnp.dot(full_in, value_full, preferred_element_type=jnp.float32) + value_bias
    ).astype(jnp.bfloat16)
    query_rows = query_rows.reshape(seq_len, heads_local, HEAD_DIM)
    key_rows = key_rows.reshape(seq_len, heads_local, HEAD_DIM)
    value_rows = value_rows.reshape(seq_len, heads_local, HEAD_DIM)
    scores = attention_scores(query_rows, key_rows, key_valid, factor)
    row_max = jnp.max(scores, axis=-1, keepdims=True)
    expanded = jnp.exp(scores - row_max)
    row_sum = jnp.sum(expanded, axis=-1, keepdims=True)
    log_norm = row_max + jnp.log(row_sum)
    softmax_low = (expanded / row_sum).astype(jnp.bfloat16)
    mixed_heads = jnp.einsum(
        "hqk,khd->qhd", softmax_low, value_rows, preferred_element_type=jnp.float32
    )
    mixed_heads = mixed_heads.astype(jnp.bfloat16).reshape(seq_len, head_cols)
    attn_part = jnp.dot(mixed_heads, out_full, preferred_element_type=jnp.float32)
    attended = (
        lax.psum_scatter(
            attn_part.astype(jnp.bfloat16), "tensor", scatter_dimension=0, tiled=True
        ).astype(jnp.float32)
        + b_out
    )
    hidden, normed_first, inverse_first = norm_forward(
        own_rows.astype(jnp.float32) + attended, gain_first, shift_first
    )
    full_hidden = lax.all_gather(hidden.astype(jnp.bfloat16), "tensor", axis=0, tiled=True)
    upward = jnp.dot(full_hidden, up_full, preferred_element_type=jnp.float32) + up_bias
    active = jax.nn.gelu(upward, approximate=True).astype(jnp.bfloat16)
    down_part = jnp.dot(active, down_full, preferred_element_type=jnp.float32)
    downward = (
        lax.psum_scatter(
            down_part.astype(jnp.bfloat16), "tensor", scatter_dimension=0, tiled=True
        ).astype(jnp.float32)
        + b_down
    )
    result, normed_second, inverse_second = norm_forward(
        hidden + downward, gain_second, shift_second
    )
    output = result.astype(jnp.bfloat16).reshape(cotangent.shape)
    gathered = (
        lax.all_gather(w_query, "dp", axis=0, tiled=True),
        lax.all_gather(w_key, "dp", axis=0, tiled=True),
        lax.all_gather(w_value, "dp", axis=0, tiled=True),
        lax.all_gather(w_out, "dp", axis=1, tiled=True),
        lax.all_gather(w_up, "dp", axis=0, tiled=True),
        lax.all_gather(w_down, "dp", axis=1, tiled=True),
    )
    query_full, key_full, value_full, out_full, up_full, down_full = gathered
    grad_result = cotangent.reshape(half_rows, features).astype(jnp.float32)
    grad_second, grad_gain_second, grad_shift_second = norm_backward(
        grad_result, gain_second, normed_second, inverse_second
    )
    grad_down = grad_second.astype(jnp.bfloat16)
    grad_b_down = jnp.sum(grad_down.astype(jnp.float32), axis=0)
    full_grad_down = lax.all_gather(grad_down, "tensor", axis=0, tiled=True)
    grad_active = contract_cols(full_grad_down, down_full)
    grad_w_down = contract_rows(active, full_grad_down)
    _, gelu_pull = jax.vjp(partial(jax.nn.gelu, approximate=True), upward)
    grad_up = gelu_pull(grad_active)[0].astype(jnp.bfloat16)
    grad_up_bias = jnp.sum(grad_up.astype(jnp.float32), axis=0)
    grad_w_up = contract_rows(full_hidden, grad_up)
    hidden_part = contract_cols(grad_up, up_full)
    grad_hidden = grad_second + lax.psum_scatter(
        hidden_part.astype(jnp.bfloat16), "tensor", scatter_dimension=0, tiled=True
    ).astype(jnp.float32)
    grad_first, grad_gain_first, grad_shift_first = norm_backward(
        grad_hidden, gain_first, normed_first, inverse_first
    )
    grad_attended = grad_first.astype(jnp.bfloat16)
    grad_b_out = jnp.sum(grad_attended.astype(jnp.float32), axis=0)
    full_grad_attended = lax.all_gather(grad_attended, "tensor", axis=0, tiled=True)
    grad_mixed = contract_cols(full_grad_attended, out_full).astype(jnp.bfloat16)
    grad_w_out = contract_rows(mixed_heads, full_grad_attended)
    grad_mixed = grad_mixed.reshape(seq_len, heads_local, HEAD_DIM)
    scores = attention_scores(query_rows, key_rows, key_valid, factor)
    softmax_again = jnp.exp(scores - log_norm)
    grad_values = jnp.einsum(
        "hqk,qhd->khd",
        softmax_again.astype(jnp.bfloat16),
        grad_mixed,
        preferred_element_type=jnp.float32,
    ).astype(jnp.bfloat16)
    grad_softmax = jnp.einsum(
        "qhd,khd->hqk", grad_mixed, value_rows, preferred_element_type=jnp.float32
    )
    row_inner = jnp.sum(softmax_again * grad_softmax, axis=-1, keepdims=True)
    grad_scores = (softmax_again * (grad_softmax - row_inner)).astype(jnp.bfloat16)
    grad_queries = (
        (
            jnp.einsum("hqk,khd->qhd", grad_scores, key_rows, preferred_element_type=jnp.float32)
            * factor
        )
        .astype(jnp.bfloat16)
        .reshape(seq_len, head_cols)
    )
    grad_keys = (
        (
            jnp.einsum("hqk,qhd->khd", grad_scores, query_rows, preferred_element_type=jnp.float32)
            * factor
        )
        .astype(jnp.bfloat16)
        .reshape(seq_len, head_cols)
    )
    grad_values = grad_values.reshape(seq_len, head_cols)
    grad_w_query = contract_rows(full_in, grad_queries)
    grad_w_key = contract_rows(full_in, grad_keys)
    grad_w_value = contract_rows(full_in, grad_values)
    grad_query_bias = jnp.sum(grad_queries.astype(jnp.float32), axis=0)
    grad_value_bias = jnp.sum(grad_values.astype(jnp.float32), axis=0)
    input_part = (
        contract_cols(grad_queries, query_full)
        + contract_cols(grad_keys, key_full)
        + contract_cols(grad_values, value_full)
    )
    grad_own = grad_first + lax.psum_scatter(
        input_part.astype(jnp.bfloat16), "tensor", scatter_dimension=0, tiled=True
    ).astype(jnp.float32)
    grad_sent = grad_own.astype(jnp.bfloat16).reshape(1, 1, half_rows, features)
    returned = lax.all_to_all(grad_sent, "dp", split_axis=2, concat_axis=0, tiled=True)
    grad_inputs = jnp.zeros_like(returned).at[dealing].set(returned)
    weight_sums = (
        lax.psum_scatter(grad_w_query.astype(jnp.bfloat16), "dp", scatter_dimension=0, tiled=True).astype(jnp.float32),
        lax.psum_scatter(grad_w_key.astype(jnp.bfloat16), "dp", scatter_dimension=0, tiled=True).astype(jnp.float32),
        lax.psum_scatter(grad_w_value.astype(jnp.bfloat16), "dp", scatter_dimension=0, tiled=True).astype(jnp.float32),
        lax.psum_scatter(grad_w_out.astype(jnp.bfloat16), "dp", scatter_dimension=1, tiled=True).astype(jnp.float32),
        lax.psum_scatter(grad_w_up.astype(jnp.bfloat16), "dp", scatter_dimension=0, tiled=True).astype(jnp.float32),
        lax.psum_scatter(grad_w_down.astype(jnp.bfloat16), "dp", scatter_dimension=1, tiled=True).astype(jnp.float32),
    )
    full_cols = b_query.shape[0]
    full_up = b_up.shape[0]
    small_sums = lax.psum(
        (
            place_slice(grad_query_bias, full_cols, tensor_index * head_cols),
            place_slice(grad_value_bias, full_cols, tensor_index * head_cols),
            grad_b_out,
            place_slice(grad_up_bias, full_up, tensor_index * up_cols),
            grad_b_down,
            grad_gain_first,
            grad_shift_first,
            grad_gain_second,
            grad_shift_second,
        ),
        ("dp", "tensor"),
    )
    return (
        output,
        grad_inputs,
        weight_sums[0],
        weight_sums[1],
        weight_sums[2],
        small_sums[0],
        small_sums[1],
        weight_sums[3],
        small_sums[2],
        small_sums[5],
        small_sums[6],
        weight_sums[4],
        small_sums[3],
        weight_sums[5],
        small_sums[4],
        small_sums[7],
        small_sums[8],
    )


def solution(mesh):
    in_specs = (
        P(None, "tensor", "dp", None),
        P(),
        P(),
        P("dp", "tensor"),
        P("dp", "tensor"),
        P("dp", "tensor"),
        P(),
        P(),
        P("tensor", "dp"),
        P(),
        P(),
        P(),
        P("dp", "tensor"),
        P(),
        P("tensor", "dp"),
        P(),
        P(),
        P(),
        P("dp", "tensor", None),
    )
    out_specs = (
        P("dp", "tensor", None),
        P(None, "tensor", "dp", None),
        P("dp", "tensor"),
        P("dp", "tensor"),
        P("dp", "tensor"),
        P(),
        P(),
        P("tensor", "dp"),
        P(),
        P(),
        P(),
        P("dp", "tensor"),
        P(),
        P("tensor", "dp"),
        P(),
        P(),
        P(),
    )
    return jax.shard_map(shards, mesh=mesh, in_specs=in_specs, out_specs=out_specs, check_vma=False)
```

```python
from functools import partial

import jax
import jax.numpy as jnp
from jax import lax
from jax.experimental import pallas as pl
from jax.experimental.pallas import tpu as pltpu
from jax.sharding import PartitionSpec as P

HEAD_DIM = 128


EPSILON = 1e-05
MASKED = -1e30


def norm_forward(values, scale_gain, bias_shift):
    center = values - jnp.mean(values, axis=-1, keepdims=True)
    inverse = lax.rsqrt(jnp.mean(center * center, axis=-1, keepdims=True) + EPSILON)
    normed = center * inverse
    return (normed * scale_gain + bias_shift, normed, inverse)


def norm_backward(grad_out, scale_gain, normed, inverse):
    scaled = grad_out * scale_gain
    grad_in = inverse * (
        scaled
        - jnp.mean(scaled, axis=-1, keepdims=True)
        - normed * jnp.mean(scaled * normed, axis=-1, keepdims=True)
    )
    return (grad_in, jnp.sum(grad_out * normed, axis=0), jnp.sum(grad_out, axis=0))


def contract_rows(left, right):
    return lax.dot_general(
        left, right, (((0,), (0,)), ((), ())), preferred_element_type=jnp.float32
    )


def contract_cols(left, right):
    return lax.dot_general(
        left, right, (((1,), (1,)), ((), ())), preferred_element_type=jnp.float32
    )


def attention_scores(query_rows, key_rows, key_valid, factor):
    scores = (
        jnp.einsum("qhd,khd->hqk", query_rows, key_rows, preferred_element_type=jnp.float32)
        * factor
    )
    return jnp.where(key_valid[None, None, :], scores, MASKED)


def place_slice(local_sum, full_size, offset):
    return lax.dynamic_update_slice_in_dim(
        jnp.zeros((full_size,), jnp.float32), local_sum, offset, 0
    )

MESH = pl.DeviceIdType.MESH
TILE = 1024


def place():
    dp, tensor = lax.axis_index("dp"), lax.axis_index("tensor")
    return dp // 4, (dp // 2) % 2, dp % 2, tensor


def device_of(plane, across, core, tensor):
    return ((plane * 2 + across) * 2 + core, tensor)


def enter(peers):
    barrier = pltpu.get_barrier_semaphore()
    for peer in peers:
        pl.semaphore_signal(barrier, inc=1, device_id=peer, device_id_type=MESH)
    pl.semaphore_wait(barrier, len(peers))


def gather_kernel(planes, widths, *refs):
    count = len(widths)
    shard_refs, full_refs = refs[:count], refs[count : 2 * count]
    local_sem, plane_send, plane_recv, x_send, x_recv, core_send, core_recv = refs[2 * count :]
    plane, across, core, tensor = place()
    far = [lax.rem(plane + k, planes) for k in range(planes)]
    near = [lax.rem(plane + planes - k, planes) for k in range(planes)]
    x_peer = device_of(plane, 1 - across, core, tensor)
    core_peer = device_of(plane, across, 1 - core, tensor)
    enter([device_of(far[k], across, core, tensor) for k in range(1, planes)] + [x_peer, core_peer])
    tiles = [(i, start) for i, width in enumerate(widths) for start in range(0, width, TILE)]
    total = len(tiles)

    def view(c, *at):
        i, start = tiles[c]
        return full_refs[i].at[(*at, slice(None), pl.ds(start, TILE))]

    def own(c):
        i, start = tiles[c]
        return shard_refs[i].at[:, pl.ds(start, TILE)]

    def to_plane(c, k):
        return pltpu.make_async_remote_copy(
            own(c), view(c, plane, across, core), plane_send.at[c, k - 1], plane_recv.at[c, k - 1],
            device_id=device_of(far[k], across, core, tensor), device_id_type=MESH,
        )

    def from_plane(c, k):
        return pltpu.make_async_remote_copy(
            own(c), view(c, near[k], across, core), plane_send.at[c, k - 1], plane_recv.at[c, k - 1],
            device_id=device_of(far[k], across, core, tensor), device_id_type=MESH,
        )

    def keep(c):
        return pltpu.make_async_copy(own(c), view(c, plane, across, core), local_sem.at[c])

    def to_x(c, side):
        part = view(c, slice(None), side, core)
        return pltpu.make_async_remote_copy(
            part, part, x_send.at[c], x_recv.at[c], device_id=x_peer, device_id_type=MESH
        )

    def to_core(c, side):
        part = view(c, slice(None), slice(None), side)
        return pltpu.make_async_remote_copy(
            part, part, core_send.at[c], core_recv.at[c], device_id=core_peer, device_id_type=MESH
        )

    def begin(c):
        keep(c).start()
        for k in range(1, planes):
            to_plane(c, k).start()

    ahead = 3
    for c in range(min(ahead, total)):
        begin(c)
    for c in range(total):
        keep(c).wait()
        for k in range(1, planes):
            from_plane(c, k).wait_recv()
        to_x(c, across).start()
        if c + ahead < total:
            begin(c + ahead)
        if c > 0:
            to_x(c - 1, 1 - across).wait_recv()
            to_core(c - 1, core).start()
    to_x(total - 1, 1 - across).wait_recv()
    to_core(total - 1, core).start()
    for c in range(total):
        for k in range(1, planes):
            to_plane(c, k).wait_send()
        to_x(c, across).wait_send()
        to_core(c, core).wait_send()
        to_core(c, 1 - core).wait_recv()


def gather_weights(shard_list):
    planes = lax.axis_size("dp") // 4
    widths = [shard.shape[1] for shard in shard_list]
    total = sum(width // TILE for width in widths)
    sem = pltpu.SemaphoreType.DMA
    full = pl.pallas_call(
        partial(gather_kernel, planes, widths),
        out_shape=[
            jax.ShapeDtypeStruct((planes, 2, 2, *shard.shape), jnp.bfloat16) for shard in shard_list
        ],
        in_specs=[pl.BlockSpec(memory_space=pl.ANY)] * len(shard_list),
        out_specs=[pl.BlockSpec(memory_space=pl.ANY)] * len(shard_list),
        scratch_shapes=[
            sem((total,)), sem((total, planes - 1)), sem((total, planes - 1)),
            sem((total,)), sem((total,)), sem((total,)), sem((total,)),
        ],
        compiler_params=pltpu.CompilerParams(collective_id=0, has_side_effects=True),
        name="gather_weights",
    )(*shard_list)
    return [array.reshape(-1, array.shape[-1]) for array in full]


def scatter_kernel(planes, jobs, widths, *refs):
    lefts, rights = 4, len(widths)
    left_ref, right_refs, small_ref = refs[0], refs[1 : 1 + rights], refs[1 + rights]
    outs = refs[2 + rights :]
    grad_refs, small_out = outs[:rights], outs[rights]
    left_far, right_fars = outs[rights + 1], outs[rights + 2 : rights + 2 + rights]
    (
        left_buf, right_buf, stage, x_land, plane_land, out_buf, small_land,
        left_sem, right_sem, out_sem, core_send, core_recv, left_send, left_recv,
        x_send, x_recv, plane_send, plane_recv, small_send, small_recv,
    ) = outs[2 * rights + 2 :]
    plane, across, core, tensor = place()
    tokens = left_ref.shape[-1]
    far = [lax.rem(plane + k, planes) for k in range(planes)]
    x_peer = device_of(plane, 1 - across, core, tensor)
    core_peer = device_of(plane, across, 1 - core, tensor)
    y_peer = device_of(plane, across, core, 1 - tensor)
    plane_peers = [device_of(far[k], across, core, tensor) for k in range(1, planes)]
    enter(plane_peers + [x_peer, core_peer, y_peer])
    total = len(jobs)

    def left_out(a):
        return pltpu.make_async_remote_copy(
            left_ref.at[a, :, :, 1 - core], left_far.at[a], left_send.at[a], left_recv.at[a],
            device_id=core_peer, device_id_type=MESH,
        )

    def right_out(c):
        _, i, start = jobs[c]
        return pltpu.make_async_remote_copy(
            right_refs[i].at[:, pl.ds(start, TILE)], right_fars[i].at[:, pl.ds(start, TILE)],
            core_send.at[c], core_recv.at[c], device_id=core_peer, device_id_type=MESH,
        )

    def left_load(a, slot):
        mine = [
            pltpu.make_async_copy(
                left_ref.at[a, :, side, core], left_buf.at[slot, side, :, :, pl.ds(0, tokens)],
                left_sem.at[slot, 0, side],
            )
            for side in range(2)
        ]
        theirs = [
            pltpu.make_async_copy(
                left_far.at[a, :, side], left_buf.at[slot, side, :, :, pl.ds(tokens, tokens)],
                left_sem.at[slot, 1, side],
            )
            for side in range(2)
        ]
        return mine + theirs

    def right_load(c):
        _, i, start = jobs[c]
        slot = c % 2
        cols = pl.ds(start, TILE)
        return [
            pltpu.make_async_copy(
                right_refs[i].at[:, cols], right_buf.at[slot, pl.ds(0, tokens)], right_sem.at[slot, 0]
            ),
            pltpu.make_async_copy(
                right_fars[i].at[:, cols], right_buf.at[slot, pl.ds(tokens, tokens)], right_sem.at[slot, 1]
            ),
        ]

    def x_out(c):
        return pltpu.make_async_remote_copy(
            stage.at[c % 3, 1 - across], x_land.at[c], x_send.at[c], x_recv.at[c],
            device_id=x_peer, device_id_type=MESH,
        )

    def plane_out(c, k):
        return pltpu.make_async_remote_copy(
            x_land.at[c, far[k]], plane_land.at[c, k - 1], plane_send.at[c, k - 1], plane_recv.at[c, k - 1],
            device_id=plane_peers[k - 1], device_id_type=MESH,
        )

    def grad_out(c):
        _, i, start = jobs[c]
        return pltpu.make_async_copy(
            out_buf.at[c % 2], grad_refs[i].at[:, pl.ds(start, TILE)], out_sem.at[c % 2]
        )

    order = []
    for a, _, _ in jobs:
        if a not in order:
            order.append(a)
    seen = set()
    for c in range(total):
        a = jobs[c][0]
        if a not in seen:
            seen.add(a)
            left_out(a).start()
        right_out(c).start()

    def fetch(c):
        a = jobs[c][0]
        if c == 0 or jobs[c - 1][0] != a:
            left_out(a).wait_recv()
            for copy in left_load(a, order.index(a) % 2):
                copy.start()
        right_out(c).wait_recv()
        for copy in right_load(c):
            copy.start()

    def multiply(c):
        a = jobs[c][0]
        slot = order.index(a) % 2
        if c == 0 or jobs[c - 1][0] != a:
            for copy in left_load(a, slot):
                copy.wait()
        for copy in right_load(c):
            copy.wait()
        if c + 1 < total:
            fetch(c + 1)
        if c >= 3:
            x_out(c - 3).wait_send()

        @pl.loop(0, TILE // 256)
        def _(n):
            cols = pl.ds(pl.multiple_of(n * 256, 256), 256)
            left = left_buf[slot]
            result = jnp.dot(
                left.reshape(-1, left.shape[-1]), right_buf[c % 2, :, cols],
                preferred_element_type=jnp.float32,
            ).astype(jnp.bfloat16)
            stage[c % 3, :, :, :, cols] = result.reshape(*left.shape[:-1], 256)

        x_out(c).start()

    def fold(c):
        x_out(c).wait_recv()

        @pl.loop(0, planes)
        def _(p):
            x_land[c, p] = (
                x_land[c, p].astype(jnp.float32) + stage[c % 3, across, p].astype(jnp.float32)
            ).astype(jnp.bfloat16)

        for k in range(1, planes):
            plane_out(c, k).start()

    def finish(c):
        for k in range(1, planes):
            plane_out(c, k).wait_recv()
        if c >= 2:
            grad_out(c - 2).wait()
        value = x_land[c, plane].astype(jnp.float32)
        for k in range(1, planes):
            value += plane_land[c, k - 1].astype(jnp.float32)
        out_buf[c % 2] = value
        grad_out(c).start()

    def small_copy(step, peer, slot):
        return pltpu.make_async_remote_copy(
            small_land.at[0], small_land.at[slot], small_send.at[step], small_recv.at[step],
            device_id=peer, device_id_type=MESH,
        )

    def small_begin(step):
        if step < 3:
            if step == 0:
                pltpu.sync_copy(small_ref, small_land.at[0])
            small_copy(step, (core_peer, x_peer, y_peer)[step], 1 + step).start()
        else:
            for k in range(1, planes):
                small_copy(2 + k, plane_peers[k - 1], 3 + k).start()

    def small_end(step):
        if step < 3:
            small_copy(step, core_peer, 1 + step).wait()
            small_land[0] = small_land[0] + small_land[1 + step]
        else:
            for k in range(1, planes):
                small_copy(2 + k, core_peer, 3 + k).wait()
            value = jnp.zeros(small_land.shape[1:], jnp.float32)
            for p in range(planes):
                back = lax.rem(plane + planes - p, planes)
                value += small_land[jnp.where(back == 0, 0, 3 + back)]
            small_land[1] = value
            pltpu.sync_copy(small_land.at[1], small_out)

    fetch(0)
    for c in range(total + 2):
        if c < total:
            multiply(c)
        if 1 <= c <= total:
            fold(c - 1)
        if c >= 2:
            finish(c - 2)
        if c in (1, 2, 3, 4):
            small_end(c - 1)
        if c in (0, 1, 2, 3):
            small_begin(c)
    for a in order:
        left_out(a).wait_send()
    for c in range(total):
        right_out(c).wait_send()
        if c >= total - 3:
            x_out(c).wait_send()
        for k in range(1, planes):
            plane_out(c, k).wait_send()
    for c in range(total - 2, total):
        grad_out(c).wait()


def scatter_grads(lefts, rights, smalls):
    size = lax.axis_size("dp")
    planes = size // 4
    tokens, features = lefts[0].shape
    rows = features // size
    left = jnp.stack([array.T for array in lefts]).reshape(4, planes, 2, 2, rows, tokens)
    arrays = [array for array, _ in rights]
    widths = [array.shape[1] for array in arrays]
    jobs = [
        (which, i, start)
        for i, (array, which) in enumerate(rights)
        for start in range(0, array.shape[1], TILE)
    ]
    total = len(jobs)
    sem = pltpu.SemaphoreType.DMA
    hbm = pl.BlockSpec(memory_space=pl.ANY)
    results = pl.pallas_call(
        partial(scatter_kernel, planes, jobs, widths),
        out_shape=[jax.ShapeDtypeStruct((rows, width), jnp.float32) for width in widths]
        + [jax.ShapeDtypeStruct(smalls.shape, jnp.float32)]
        + [jax.ShapeDtypeStruct((4, planes, 2, rows, tokens), jnp.bfloat16)]
        + [jax.ShapeDtypeStruct(array.shape, jnp.bfloat16) for array in arrays],
        in_specs=[hbm] * (2 + len(arrays)),
        out_specs=[hbm] * (2 + 2 * len(arrays)),
        scratch_shapes=[
            pltpu.VMEM((2, 2, planes, rows, 2 * tokens), jnp.bfloat16),
            pltpu.VMEM((2, 2 * tokens, TILE), jnp.bfloat16),
            pltpu.VMEM((3, 2, planes, rows, TILE), jnp.bfloat16),
            pltpu.VMEM((total, planes, rows, TILE), jnp.bfloat16),
            pltpu.VMEM((total, planes - 1, rows, TILE), jnp.bfloat16),
            pltpu.VMEM((2, rows, TILE), jnp.float32),
            pltpu.VMEM((3 + planes, *smalls.shape), jnp.float32),
            sem((2, 2, 2)), sem((2, 2)), sem((2,)), sem((total,)), sem((total,)), sem((4,)), sem((4,)),
            sem((total,)), sem((total,)), sem((total, planes - 1)), sem((total, planes - 1)),
            sem((2 + planes,)), sem((2 + planes,)),
        ],
        compiler_params=pltpu.CompilerParams(
            collective_id=1, has_side_effects=True, vmem_limit_bytes=60 * 2**20
        ),
        name="scatter_grads",
    )(left, *arrays, smalls)
    return results[: len(arrays)], results[len(arrays)]


def shards(
    inputs,
    lengths,
    dealing,
    w_query,
    w_key,
    w_value,
    b_query,
    b_value,
    w_out,
    b_out,
    gain_first,
    shift_first,
    w_up,
    b_up,
    w_down,
    b_down,
    gain_second,
    shift_second,
    cotangent,
):
    group_index = lax.axis_index("dp")
    tensor_index = lax.axis_index("tensor")
    ordered = jnp.take(inputs, dealing, axis=0)
    arrived = lax.all_to_all(ordered, "dp", split_axis=0, concat_axis=2, tiled=True)
    features = arrived.shape[3]
    half_rows = arrived.shape[2]
    own_rows = arrived.reshape(half_rows, features)
    seq_len = half_rows * lax.axis_size("tensor")
    length = lengths[dealing[group_index]]
    key_valid = jnp.arange(seq_len) < length
    factor = HEAD_DIM ** (-0.5)
    query_full, key_full, value_full, out_turned, up_full, down_turned = gather_weights(
        [w_query, w_key, w_value, w_out.T, w_up, w_down.T]
    )
    head_cols = query_full.shape[1]
    heads_local = head_cols // HEAD_DIM
    up_cols = up_full.shape[1]
    query_bias = lax.dynamic_slice_in_dim(b_query, tensor_index * head_cols, head_cols)
    value_bias = lax.dynamic_slice_in_dim(b_value, tensor_index * head_cols, head_cols)
    up_bias = lax.dynamic_slice_in_dim(b_up, tensor_index * up_cols, up_cols)
    full_in = lax.all_gather(own_rows, "tensor", axis=0, tiled=True)
    query_rows = (
        jnp.dot(full_in, query_full, preferred_element_type=jnp.float32) + query_bias
    ).astype(jnp.bfloat16)
    key_rows = jnp.dot(full_in, key_full, preferred_element_type=jnp.float32).astype(jnp.bfloat16)
    value_rows = (
        jnp.dot(full_in, value_full, preferred_element_type=jnp.float32) + value_bias
    ).astype(jnp.bfloat16)
    query_rows = query_rows.reshape(seq_len, heads_local, HEAD_DIM)
    key_rows = key_rows.reshape(seq_len, heads_local, HEAD_DIM)
    value_rows = value_rows.reshape(seq_len, heads_local, HEAD_DIM)
    scores = attention_scores(query_rows, key_rows, key_valid, factor)
    row_max = jnp.max(scores, axis=-1, keepdims=True)
    expanded = jnp.exp(scores - row_max)
    row_sum = jnp.sum(expanded, axis=-1, keepdims=True)
    log_norm = row_max + jnp.log(row_sum)
    softmax_low = (expanded / row_sum).astype(jnp.bfloat16)
    mixed_heads = jnp.einsum(
        "hqk,khd->qhd", softmax_low, value_rows, preferred_element_type=jnp.float32
    )
    mixed_heads = mixed_heads.astype(jnp.bfloat16).reshape(seq_len, head_cols)
    attn_part = contract_cols(mixed_heads, out_turned)
    attended = (
        lax.psum_scatter(
            attn_part.astype(jnp.bfloat16), "tensor", scatter_dimension=0, tiled=True
        ).astype(jnp.float32)
        + b_out
    )
    hidden, normed_first, inverse_first = norm_forward(
        own_rows.astype(jnp.float32) + attended, gain_first, shift_first
    )
    full_hidden = lax.all_gather(hidden.astype(jnp.bfloat16), "tensor", axis=0, tiled=True)
    upward = jnp.dot(full_hidden, up_full, preferred_element_type=jnp.float32) + up_bias
    active = jax.nn.gelu(upward, approximate=True).astype(jnp.bfloat16)
    down_part = contract_cols(active, down_turned)
    downward = (
        lax.psum_scatter(
            down_part.astype(jnp.bfloat16), "tensor", scatter_dimension=0, tiled=True
        ).astype(jnp.float32)
        + b_down
    )
    result, normed_second, inverse_second = norm_forward(
        hidden + downward, gain_second, shift_second
    )
    output = result.astype(jnp.bfloat16).reshape(cotangent.shape)
    grad_result = cotangent.reshape(half_rows, features).astype(jnp.float32)
    grad_second, grad_gain_second, grad_shift_second = norm_backward(
        grad_result, gain_second, normed_second, inverse_second
    )
    grad_down = grad_second.astype(jnp.bfloat16)
    grad_b_down = jnp.sum(grad_down.astype(jnp.float32), axis=0)
    full_grad_down = lax.all_gather(grad_down, "tensor", axis=0, tiled=True)
    grad_active = jnp.dot(full_grad_down, down_turned, preferred_element_type=jnp.float32)
    _, gelu_pull = jax.vjp(partial(jax.nn.gelu, approximate=True), upward)
    grad_up = gelu_pull(grad_active)[0].astype(jnp.bfloat16)
    grad_up_bias = jnp.sum(grad_up.astype(jnp.float32), axis=0)
    hidden_part = contract_cols(grad_up, up_full)
    grad_hidden = grad_second + lax.psum_scatter(
        hidden_part.astype(jnp.bfloat16), "tensor", scatter_dimension=0, tiled=True
    ).astype(jnp.float32)
    grad_first, grad_gain_first, grad_shift_first = norm_backward(
        grad_hidden, gain_first, normed_first, inverse_first
    )
    grad_attended = grad_first.astype(jnp.bfloat16)
    grad_b_out = jnp.sum(grad_attended.astype(jnp.float32), axis=0)
    full_grad_attended = lax.all_gather(grad_attended, "tensor", axis=0, tiled=True)
    grad_mixed = jnp.dot(
        full_grad_attended, out_turned, preferred_element_type=jnp.float32
    ).astype(jnp.bfloat16)
    grad_mixed = grad_mixed.reshape(seq_len, heads_local, HEAD_DIM)
    scores = attention_scores(query_rows, key_rows, key_valid, factor)
    softmax_again = jnp.exp(scores - log_norm)
    grad_values = jnp.einsum(
        "hqk,qhd->khd",
        softmax_again.astype(jnp.bfloat16),
        grad_mixed,
        preferred_element_type=jnp.float32,
    ).astype(jnp.bfloat16)
    grad_softmax = jnp.einsum(
        "qhd,khd->hqk", grad_mixed, value_rows, preferred_element_type=jnp.float32
    )
    row_inner = jnp.sum(softmax_again * grad_softmax, axis=-1, keepdims=True)
    grad_scores = (softmax_again * (grad_softmax - row_inner)).astype(jnp.bfloat16)
    grad_queries = (
        (
            jnp.einsum("hqk,khd->qhd", grad_scores, key_rows, preferred_element_type=jnp.float32)
            * factor
        )
        .astype(jnp.bfloat16)
        .reshape(seq_len, head_cols)
    )
    grad_keys = (
        (
            jnp.einsum("hqk,qhd->khd", grad_scores, query_rows, preferred_element_type=jnp.float32)
            * factor
        )
        .astype(jnp.bfloat16)
        .reshape(seq_len, head_cols)
    )
    grad_values = grad_values.reshape(seq_len, head_cols)
    grad_query_bias = jnp.sum(grad_queries.astype(jnp.float32), axis=0)
    grad_value_bias = jnp.sum(grad_values.astype(jnp.float32), axis=0)
    input_part = (
        contract_cols(grad_queries, query_full)
        + contract_cols(grad_keys, key_full)
        + contract_cols(grad_values, value_full)
    )
    grad_own = grad_first + lax.psum_scatter(
        input_part.astype(jnp.bfloat16), "tensor", scatter_dimension=0, tiled=True
    ).astype(jnp.float32)
    grad_sent = grad_own.astype(jnp.bfloat16).reshape(1, 1, half_rows, features)
    returned = lax.all_to_all(grad_sent, "dp", split_axis=2, concat_axis=0, tiled=True)
    grad_inputs = jnp.zeros_like(returned).at[dealing].set(returned)
    full_cols = b_query.shape[0]
    full_up = b_up.shape[0]
    smalls = (
        place_slice(grad_query_bias, full_cols, tensor_index * head_cols),
        place_slice(grad_value_bias, full_cols, tensor_index * head_cols),
        grad_b_out,
        place_slice(grad_up_bias, full_up, tensor_index * up_cols),
        grad_b_down,
        grad_gain_first,
        grad_shift_first,
        grad_gain_second,
        grad_shift_second,
    )
    sums, small_total = scatter_grads(
        [full_in, full_grad_attended, full_hidden, full_grad_down],
        [(active, 3), (grad_up, 2), (mixed_heads, 1), (grad_queries, 0), (grad_keys, 0), (grad_values, 0)],
        jnp.concatenate(smalls).reshape(-1, 128),
    )
    weight_sums = (sums[3], sums[4], sums[5], sums[2].T, sums[1], sums[0].T)
    small_total = small_total.reshape(-1)
    small_sums, at = [], 0
    for small in smalls:
        small_sums.append(small_total[at : at + small.shape[0]])
        at += small.shape[0]
    return (
        output,
        grad_inputs,
        weight_sums[0],
        weight_sums[1],
        weight_sums[2],
        small_sums[0],
        small_sums[1],
        weight_sums[3],
        small_sums[2],
        small_sums[5],
        small_sums[6],
        weight_sums[4],
        small_sums[3],
        weight_sums[5],
        small_sums[4],
        small_sums[7],
        small_sums[8],
    )


def solution(mesh):
    in_specs = (
        P(None, "tensor", "dp", None),
        P(),
        P(),
        P("dp", "tensor"),
        P("dp", "tensor"),
        P("dp", "tensor"),
        P(),
        P(),
        P("tensor", "dp"),
        P(),
        P(),
        P(),
        P("dp", "tensor"),
        P(),
        P("tensor", "dp"),
        P(),
        P(),
        P(),
        P("dp", "tensor", None),
    )
    out_specs = (
        P("dp", "tensor", None),
        P(None, "tensor", "dp", None),
        P("dp", "tensor"),
        P("dp", "tensor"),
        P("dp", "tensor"),
        P(),
        P(),
        P("tensor", "dp"),
        P(),
        P(),
        P(),
        P("dp", "tensor"),
        P(),
        P("tensor", "dp"),
        P(),
        P(),
        P(),
    )
    return jax.shard_map(shards, mesh=mesh, in_specs=in_specs, out_specs=out_specs, check_vma=False)
```

```python
from functools import partial

import jax
import jax.numpy as jnp
from jax import lax
from jax.experimental import pallas as pl
from jax.experimental.pallas import tpu as pltpu
from jax.sharding import PartitionSpec as P

HEAD_DIM = 128


EPSILON = 1e-05
MASKED = -1e30


def norm_forward(values, scale_gain, bias_shift):
    center = values - jnp.mean(values, axis=-1, keepdims=True)
    inverse = lax.rsqrt(jnp.mean(center * center, axis=-1, keepdims=True) + EPSILON)
    normed = center * inverse
    return (normed * scale_gain + bias_shift, normed, inverse)


def norm_backward(grad_out, scale_gain, normed, inverse):
    scaled = grad_out * scale_gain
    grad_in = inverse * (
        scaled
        - jnp.mean(scaled, axis=-1, keepdims=True)
        - normed * jnp.mean(scaled * normed, axis=-1, keepdims=True)
    )
    return (grad_in, jnp.sum(grad_out * normed, axis=0), jnp.sum(grad_out, axis=0))


def contract_rows(left, right):
    return lax.dot_general(
        left, right, (((0,), (0,)), ((), ())), preferred_element_type=jnp.float32
    )


def contract_cols(left, right):
    return lax.dot_general(
        left, right, (((1,), (1,)), ((), ())), preferred_element_type=jnp.float32
    )


def attention_scores(query_rows, key_rows, key_valid, factor):
    scores = (
        jnp.einsum("qhd,khd->hqk", query_rows, key_rows, preferred_element_type=jnp.float32)
        * factor
    )
    return jnp.where(key_valid[None, None, :], scores, MASKED)


def place_slice(local_sum, full_size, offset):
    return lax.dynamic_update_slice_in_dim(
        jnp.zeros((full_size,), jnp.float32), local_sum, offset, 0
    )

MESH = pl.DeviceIdType.MESH
TILE = 1024
SLOPE = 0.7978845608028654


def place():
    dp, tensor = lax.axis_index("dp"), lax.axis_index("tensor")
    return dp // 4, (dp // 2) % 2, dp % 2, tensor


def device_of(plane, across, core, tensor):
    return ((plane * 2 + across) * 2 + core, tensor)


def enter(peers):
    barrier = pltpu.get_barrier_semaphore()
    for peer in peers:
        pl.semaphore_signal(barrier, inc=1, device_id=peer, device_id_type=MESH)
    pl.semaphore_wait(barrier, len(peers))


def gather_tiles(widths):
    return [(i, start) for i, width in enumerate(widths) for start in range(0, width, TILE)]


def forward_kernel(planes, widths, *refs):
    count = len(widths)
    shard_refs = refs[:count]
    own_ref, cot_ref, mask_ref, vec_ref = refs[count : count + 4]
    outs = refs[count + 4 :]
    full_refs = outs[:count]
    (
        x_full, cot_full, qkv_out, mixed_out, normed_out, inverse_out, hidden_out, active_out, slope_out,
        result_out, down_out, second_out, sums_out,
    ) = outs[count : count + 13]
    (
        w_buf, x_buf, qkv_buf, mixed_buf, attn_acc, attn_land, send_buf, hidden_buf, active_buf, slope_buf,
        down_acc, down_land, inverse_buf, result_buf, sums_buf,
        plane_send, plane_recv, x_send, x_recv, core_send, core_recv, w_sem, in_send, in_recv,
        attn_send, attn_recv, down_send, down_recv, load_sem, store_sem,
    ) = outs[count + 13 :]
    plane, across, core, tensor = place()
    far = [lax.rem(plane + k, planes) for k in range(planes)]
    near = [lax.rem(plane + planes - k, planes) for k in range(planes)]
    x_peer = device_of(plane, 1 - across, core, tensor)
    core_peer = device_of(plane, across, 1 - core, tensor)
    y_peer = device_of(plane, across, core, 1 - tensor)
    plane_peers = [device_of(far[k], across, core, tensor) for k in range(planes)]
    tiles = gather_tiles(widths)
    half, features = own_ref.shape
    tokens = 2 * half
    block = features // planes
    head_cols = mixed_buf.shape[1]
    factor = HEAD_DIM ** (-0.5)
    own_rows = pl.ds(pl.multiple_of(tensor * half, half), half)

    vec_at = {}
    at = 0
    for key, size in (
        ("b_query", head_cols), ("b_value", head_cols), ("b_out", features), ("gain_first", features),
        ("shift_first", features), ("b_up", widths[4]), ("b_down", features), ("gain_second", features),
        ("shift_second", features),
    ):
        vec_at[key] = at
        at += size

    def vector(key, start, size):
        return vec_ref[:, pl.ds(vec_at[key] + start, size)]

    first_down = len(tiles) - widths[5] // TILE
    units = [(c, k) for c in range(first_down) for k in range(planes)]
    units += [(c, k) for k in range(planes) for c in range(first_down, len(tiles))]
    ahead, lag = 6, 2

    def view(c, *where):
        i, start = tiles[c]
        return full_refs[i].at[(*where, slice(None), pl.ds(start, TILE))]

    def own(c):
        i, start = tiles[c]
        return shard_refs[i].at[:, pl.ds(start, TILE)]

    def unit_z(u, source):
        c, k = units[u]
        if k == 0:
            return pltpu.make_async_copy(own(c), view(c, plane, across, core), plane_recv.at[c, 0])
        return pltpu.make_async_remote_copy(
            own(c), view(c, source, across, core), plane_send.at[c, k], plane_recv.at[c, k],
            device_id=plane_peers[k], device_id_type=MESH,
        )

    def unit_x(u, side):
        c, k = units[u]
        part = view(c, near[k], side, core)
        return pltpu.make_async_remote_copy(
            part, part, x_send.at[c, k], x_recv.at[c, k], device_id=x_peer, device_id_type=MESH
        )

    def unit_core(u, side):
        c, k = units[u]
        part = view(c, near[k], slice(None), side)
        return pltpu.make_async_remote_copy(
            part, part, core_send.at[c, k], core_recv.at[c, k], device_id=core_peer, device_id_type=MESH
        )

    def z_start(u):
        unit_z(u, plane).start()

    def z_wait(u):
        c, k = units[u]
        if k == 0:
            unit_z(u, plane).wait()
        else:
            unit_z(u, near[k]).wait_recv()

    def pump(n):
        if n < len(units):
            z_wait(n)
            unit_x(n, across).start()
            if n + ahead < len(units):
                z_start(n + ahead)
        if n >= lag:
            unit_x(n - lag, 1 - across).wait_recv()
            unit_core(n - lag, core).start()

    def landed(u):
        unit_core(u, 1 - core).wait_recv()

    def tile_copies(c):
        i, start = tiles[c]
        return [
            pltpu.make_async_copy(
                full_refs[i].at[p, :, :, :, pl.ds(start, TILE)], w_buf.at[c % 2, p], w_sem.at[c % 2, p]
            )
            for p in range(planes)
        ]

    def load_tile(c):
        for u, (tile, _) in enumerate(units):
            if tile == c:
                landed(u)
        for copy in tile_copies(c):
            copy.start()

    def wait_tile(c):
        for copy in tile_copies(c):
            copy.wait()

    def down_copy(k, j):
        c = first_down + j
        return pltpu.make_async_copy(
            view(c, near[k], slice(None), slice(None)), w_buf.at[k % 2, j], w_sem.at[k % 2, j]
        )

    down_parts = widths[5] // TILE

    def load_down(k):
        for j in range(down_parts):
            landed(units.index((first_down + j, k)))
            down_copy(k, j).start()

    def flat(value):
        return value.reshape(-1, value.shape[-1])

    def load_x():
        exchange(0, own_ref, x_full).wait_recv()
        keep(0, own_ref, x_full).wait()
        copy = pltpu.make_async_copy(x_full, x_buf, load_sem.at[2])
        copy.start()
        copy.wait()

    def exchange(which, source, target):
        return pltpu.make_async_remote_copy(
            source, target.at[own_rows], in_send.at[which], in_recv.at[which],
            device_id=y_peer, device_id_type=MESH,
        )

    def keep(which, source, target):
        return pltpu.make_async_copy(source, target.at[own_rows], load_sem.at[which])

    def project(c, bias):
        wait_tile(c)

        @pl.loop(0, TILE // 512)
        def _(n):
            cols = pl.ds(pl.multiple_of(n * 512, 512), 512)
            value = jnp.dot(
                x_buf[...], flat(w_buf[c % 2, :, :, :, :, cols]), preferred_element_type=jnp.float32
            )
            if bias is not None:
                value += vec_ref[:, pl.ds(pl.multiple_of(vec_at[bias] + n * 512, 128), 512)]
            qkv_buf[:, pl.ds(pl.multiple_of(c * TILE + n * 512, 512), 512)] = value.astype(jnp.bfloat16)

    def attend(first, last):
        @pl.loop(first, last)
        def _(h):
            def cols(which):
                return pl.ds(pl.multiple_of(which * head_cols + h * HEAD_DIM, HEAD_DIM), HEAD_DIM)

            scores = contract_cols(qkv_buf[:, cols(0)], qkv_buf[:, cols(1)]) * factor
            scores = jnp.where(mask_ref[0:1, :] > 0.0, scores, MASKED)
            expanded = jnp.exp(scores - jnp.max(scores, axis=1, keepdims=True))
            weight = (expanded / jnp.sum(expanded, axis=1, keepdims=True)).astype(jnp.bfloat16)
            mixed_buf[:, cols(0)] = jnp.dot(
                weight, qkv_buf[:, cols(2)], preferred_element_type=jnp.float32
            ).astype(jnp.bfloat16)

    def block_cols(p):
        return pl.ds(pl.multiple_of(p * block, block), block)

    def attn_share(p):
        return pltpu.make_async_remote_copy(
            send_buf.at[:, block_cols(p)], attn_land.at[:, block_cols(p)], attn_send.at[p], attn_recv.at[p],
            device_id=y_peer, device_id_type=MESH,
        )

    def project_out():
        wait_tile(3)

        @pl.loop(0, planes)
        def _(p):
            value = contract_cols(mixed_buf[...], flat(w_buf[1, p]))
            attn_acc[:, block_cols(p)] = value
            send_buf[:, block_cols(p)] = value.astype(jnp.bfloat16)
            attn_share(p).start()

    def first_norm():
        @pl.loop(0, planes)
        def _(p):
            attn_share(p).wait()

        @pl.loop(0, tokens // 16)
        def _(i):
            rows = pl.ds(pl.multiple_of(i * 16, 16), 16)
            value = (
                x_buf[rows, :].astype(jnp.float32)
                + (attn_acc[rows, :] + attn_land[rows, :].astype(jnp.float32))
                + vector("b_out", 0, features)
            )
            hidden, normed, inverse = norm_forward(
                value, vector("gain_first", 0, features), vector("shift_first", 0, features)
            )
            attn_acc[rows, :] = normed
            inverse_buf[rows, :] = jnp.broadcast_to(inverse, (16, 128))
            hidden_buf[rows, :] = hidden.astype(jnp.bfloat16)

        store(0, attn_acc, normed_out).start()
        store(1, inverse_buf, inverse_out).start()
        store(2, hidden_buf, hidden_out).start()
        exchange(1, cot_ref, cot_full).wait_recv()
        keep(1, cot_ref, cot_full).wait()
        pltpu.make_async_copy(cot_full, x_buf, load_sem.at[2]).start()

    def store(which, source, target):
        return pltpu.make_async_copy(source, target, store_sem.at[which])

    def slope_store(j):
        return pltpu.make_async_copy(
            slope_buf.at[j % 2], slope_out.at[:, pl.ds(j * TILE, TILE)], store_sem.at[5 + j % 2]
        )

    def raise_up(j):
        c = 4 + j
        wait_tile(c)
        if j >= 2:
            slope_store(j - 2).wait()

        @pl.loop(0, TILE // 256)
        def _(n):
            cols = pl.ds(pl.multiple_of(n * 256, 256), 256)
            value = jnp.dot(
                hidden_buf[...], flat(w_buf[c % 2, :, :, :, :, cols]), preferred_element_type=jnp.float32
            )
            value += vec_ref[:, pl.ds(pl.multiple_of(vec_at["b_up"] + j * TILE + n * 256, 128), 256)]
            square = value * value
            bend = jnp.tanh(SLOPE * value * (1.0 + 0.044715 * square))
            rise = 0.5 * (1.0 + bend)
            active_buf[:, pl.ds(pl.multiple_of(j * TILE + n * 256, 256), 256)] = (value * rise).astype(
                jnp.bfloat16
            )
            slope_buf[j % 2, :, cols] = (
                rise + 0.5 * value * (1.0 - bend * bend) * (SLOPE * (1.0 + 3.0 * 0.044715 * square))
            ).astype(jnp.bfloat16)

        slope_store(j).start()

    def down_share(k):
        cols = block_cols(near[k])
        return pltpu.make_async_remote_copy(
            send_buf.at[:, cols], down_land.at[:, cols], down_send.at[k], down_recv.at[k],
            device_id=y_peer, device_id_type=MESH,
        )

    def lower(k):
        cols = block_cols(near[k])
        value = None
        for j in range(down_parts):
            down_copy(k, j).wait()
            part = contract_cols(active_buf[:, j * TILE : (j + 1) * TILE], flat(w_buf[k % 2, j]))
            value = part if value is None else value + part
        down_acc[:, cols] = value
        send_buf[:, cols] = value.astype(jnp.bfloat16)
        down_share(k).start()

    def second_norm():
        for k in range(planes):
            down_share(k).wait()
        pltpu.make_async_copy(cot_full, x_buf, load_sem.at[2]).wait()
        store(2, hidden_buf, hidden_out).wait()
        sums_buf[...] = jnp.zeros_like(sums_buf)
        gain = vector("gain_second", 0, features)

        def rows_of(which, i):
            base = tensor if which == 0 else 1 - tensor
            return pl.ds(pl.multiple_of(base * half + i * 16, 16), 16)

        for which in (0, 1):
            @pl.loop(0, half // 16)
            def _(i):
                rows = rows_of(which, i)
                hidden = attn_acc[rows, :] * vector("gain_first", 0, features) + vector(
                    "shift_first", 0, features
                )
                value = (
                    hidden
                    + (down_acc[rows, :] + down_land[rows, :].astype(jnp.float32))
                    + vector("b_down", 0, features)
                )
                result, normed, inverse = norm_forward(value, gain, vector("shift_second", 0, features))
                grad_out = x_buf[rows, :].astype(jnp.float32)
                scaled = grad_out * gain
                grad = inverse * (
                    scaled
                    - jnp.mean(scaled, axis=-1, keepdims=True)
                    - normed * jnp.mean(scaled * normed, axis=-1, keepdims=True)
                )
                down_acc[rows, :] = grad
                low = grad.astype(jnp.bfloat16)
                hidden_buf[rows, :] = low
                if which == 0:
                    result_buf[pl.ds(pl.multiple_of(i * 16, 16), 16), :] = result.astype(jnp.bfloat16)
                    sums_buf[0] += grad_out * normed
                    sums_buf[1] += grad_out
                    sums_buf[2] += low.astype(jnp.float32)

        for which, source, target in (
            (2, hidden_buf, down_out), (3, down_acc, second_out), (4, result_buf, result_out), (9, sums_buf, sums_out),
        ):
            store(which, source, target).start()

    enter(plane_peers[1:] + [x_peer, core_peer, y_peer])
    for u in range(ahead):
        z_start(u)
    for which, source, target in ((0, own_ref, x_full), (1, cot_ref, cot_full)):
        exchange(which, source, target).start()
        keep(which, source, target).start()

    plan = {}

    def at_slot(n, step, *args):
        plan.setdefault(n, []).append((step, args))

    def ready(c):
        return planes * (c + 1) + 2

    heads = head_cols // HEAD_DIM
    at_slot(ready(0), load_x)
    for c in range(3):
        at_slot(ready(c), load_tile, c)
        at_slot(ready(c) + 1, project, c, ("b_query", None, "b_value")[c])
    begin = ready(2) + 2
    for q in range(4):
        at_slot(begin + q, attend, q * heads // 4, (q + 1) * heads // 4)
    at_slot(begin + 3, load_tile, 3)
    at_slot(begin + 4, project_out)
    norm_slot = begin + 4 + 10 * planes // 4
    at_slot(norm_slot, first_norm)
    at_slot(max(ready(4), begin), load_tile, 4)
    at_slot(max(ready(5), begin + 4), load_tile, 5)
    for j in range(4):
        slot = max(norm_slot + 1 + j, ready(4 + j) + 1)
        at_slot(slot, raise_up, j)
        if j >= 2:
            plan.setdefault(max(norm_slot + 1 + j - 2, ready(4 + j)), []).append((load_tile, (4 + j,)))
    for k in range(planes):
        slot = planes * first_down + down_parts * (k + 1) + 2
        at_slot(slot, load_down, k)
        at_slot(slot + 1, lower, k)
    last = max(max(plan), len(units) + lag - 1)
    for n in range(last + 1):
        if n < len(units) + lag:
            pump(n)
        for step, args in plan.get(n, []):
            step(*args)
        if n == begin + 3:
            store(7, qkv_buf, qkv_out).start()
            store(8, mixed_buf, mixed_out).start()
    store(10, active_buf, active_out).start()
    second_norm()
    for which, source, target in (
        (0, attn_acc, normed_out), (1, inverse_buf, inverse_out), (2, hidden_buf, down_out),
        (3, down_acc, second_out), (4, result_buf, result_out), (7, qkv_buf, qkv_out),
        (8, mixed_buf, mixed_out), (9, sums_buf, sums_out), (10, active_buf, active_out),
    ):
        store(which, source, target).wait()
    for j in range(2, 4):
        slope_store(j).wait()
    for which, source, target in ((0, own_ref, x_full), (1, cot_ref, cot_full)):
        exchange(which, source, target).wait_send()
    for u, (c, k) in enumerate(units):
        if k > 0:
            unit_z(u, plane).wait_send()
        unit_x(u, across).wait_send()
        unit_core(u, core).wait_send()


def forward(shard_list, own, cot, mask, vectors):
    planes = lax.axis_size("dp") // 4
    widths = [shard.shape[1] for shard in shard_list]
    total = sum(width // TILE for width in widths)
    half, features = own.shape
    tokens, rows = 2 * half, shard_list[0].shape[0]
    head_cols, up_cols = widths[0], widths[4]
    sem, low, high = pltpu.SemaphoreType.DMA, jnp.bfloat16, jnp.float32
    hbm, vmem = pl.BlockSpec(memory_space=pl.ANY), pl.BlockSpec(memory_space=pltpu.VMEM)
    shapes = [((planes, 2, 2, *shard.shape), low) for shard in shard_list] + [
        ((tokens, features), low), ((tokens, features), low), ((tokens, 3 * head_cols), low),
        ((tokens, head_cols), low), ((tokens, features), high), ((tokens, 128), high),
        ((tokens, features), low), ((tokens, up_cols), low), ((tokens, up_cols), low),
        ((half, features), low), ((tokens, features), low), ((tokens, features), high),
        ((3, 16, features), high),
    ]
    results = pl.pallas_call(
        partial(forward_kernel, planes, widths),
        out_shape=[jax.ShapeDtypeStruct(*shape) for shape in shapes],
        in_specs=[hbm] * (len(shard_list) + 2) + [vmem] * 2,
        out_specs=[hbm] * len(shapes),
        scratch_shapes=[
            pltpu.VMEM((2, planes, 2, 2, rows, TILE), low),
            pltpu.VMEM((tokens, features), low),
            pltpu.VMEM((tokens, 3 * head_cols), low),
            pltpu.VMEM((tokens, head_cols), low),
            pltpu.VMEM((tokens, features), high),
            pltpu.VMEM((tokens, features), low),
            pltpu.VMEM((tokens, features), low),
            pltpu.VMEM((tokens, features), low),
            pltpu.VMEM((tokens, up_cols), low),
            pltpu.VMEM((2, tokens, TILE), low),
            pltpu.VMEM((tokens, features), high),
            pltpu.VMEM((tokens, features), low),
            pltpu.VMEM((tokens, 128), high),
            pltpu.VMEM((half, features), low),
            pltpu.VMEM((3, 16, features), high),
            *[sem((total, planes))] * 6,
            sem((2, max(planes, 4))), sem((2,)), sem((2,)),
            sem((planes,)), sem((planes,)), sem((planes,)), sem((planes,)), sem((3,)), sem((11,)),
        ],
        compiler_params=pltpu.CompilerParams(
            collective_id=0, has_side_effects=True, vmem_limit_bytes=62 * 2**20
        ),
        name="forward_gather",
    )(*shard_list, own, cot, mask, vectors)
    weights = [array.reshape(-1, array.shape[-1]) for array in results[: len(shard_list)]]
    return weights, results[len(shard_list) :]


def scatter_kernel(planes, jobs, widths, *refs):
    lefts, rights = 4, len(widths)
    left_ref, right_refs, small_ref = refs[0], refs[1 : 1 + rights], refs[1 + rights]
    outs = refs[2 + rights :]
    grad_refs, small_out = outs[:rights], outs[rights]
    left_far, right_fars = outs[rights + 1], outs[rights + 2 : rights + 2 + rights]
    (
        left_buf, right_buf, stage, x_land, plane_land, out_buf, small_land,
        left_sem, right_sem, out_sem, core_send, core_recv, left_send, left_recv,
        x_send, x_recv, plane_send, plane_recv, small_send, small_recv,
    ) = outs[2 * rights + 2 :]
    plane, across, core, tensor = place()
    tokens = left_ref.shape[-1]
    far = [lax.rem(plane + k, planes) for k in range(planes)]
    x_peer = device_of(plane, 1 - across, core, tensor)
    core_peer = device_of(plane, across, 1 - core, tensor)
    y_peer = device_of(plane, across, core, 1 - tensor)
    plane_peers = [device_of(far[k], across, core, tensor) for k in range(1, planes)]
    enter(plane_peers + [x_peer, core_peer, y_peer])
    total = len(jobs)

    def left_out(a):
        return pltpu.make_async_remote_copy(
            left_ref.at[a, :, :, 1 - core], left_far.at[a], left_send.at[a], left_recv.at[a],
            device_id=core_peer, device_id_type=MESH,
        )

    def right_out(c):
        _, i, start = jobs[c]
        return pltpu.make_async_remote_copy(
            right_refs[i].at[:, pl.ds(start, TILE)], right_fars[i].at[:, pl.ds(start, TILE)],
            core_send.at[c], core_recv.at[c], device_id=core_peer, device_id_type=MESH,
        )

    def left_load(a, slot):
        mine = [
            pltpu.make_async_copy(
                left_ref.at[a, :, side, core], left_buf.at[slot, side, :, :, pl.ds(0, tokens)],
                left_sem.at[slot, 0, side],
            )
            for side in range(2)
        ]
        theirs = [
            pltpu.make_async_copy(
                left_far.at[a, :, side], left_buf.at[slot, side, :, :, pl.ds(tokens, tokens)],
                left_sem.at[slot, 1, side],
            )
            for side in range(2)
        ]
        return mine + theirs

    def right_load(c):
        _, i, start = jobs[c]
        slot = c % 2
        cols = pl.ds(start, TILE)
        return [
            pltpu.make_async_copy(
                right_refs[i].at[:, cols], right_buf.at[slot, pl.ds(0, tokens)], right_sem.at[slot, 0]
            ),
            pltpu.make_async_copy(
                right_fars[i].at[:, cols], right_buf.at[slot, pl.ds(tokens, tokens)], right_sem.at[slot, 1]
            ),
        ]

    def x_out(c):
        return pltpu.make_async_remote_copy(
            stage.at[c % 3, 1 - across], x_land.at[c], x_send.at[c], x_recv.at[c],
            device_id=x_peer, device_id_type=MESH,
        )

    def plane_out(c, k):
        return pltpu.make_async_remote_copy(
            x_land.at[c, far[k]], plane_land.at[c, k - 1], plane_send.at[c, k - 1], plane_recv.at[c, k - 1],
            device_id=plane_peers[k - 1], device_id_type=MESH,
        )

    def grad_out(c):
        _, i, start = jobs[c]
        return pltpu.make_async_copy(
            out_buf.at[c % 2], grad_refs[i].at[:, pl.ds(start, TILE)], out_sem.at[c % 2]
        )

    order = []
    for a, _, _ in jobs:
        if a not in order:
            order.append(a)
    seen = set()
    for c in range(total):
        a = jobs[c][0]
        if a not in seen:
            seen.add(a)
            left_out(a).start()
        right_out(c).start()

    def fetch(c):
        a = jobs[c][0]
        if c == 0 or jobs[c - 1][0] != a:
            left_out(a).wait_recv()
            for copy in left_load(a, order.index(a) % 2):
                copy.start()
        right_out(c).wait_recv()
        for copy in right_load(c):
            copy.start()

    def multiply(c):
        a = jobs[c][0]
        slot = order.index(a) % 2
        if c == 0 or jobs[c - 1][0] != a:
            for copy in left_load(a, slot):
                copy.wait()
        for copy in right_load(c):
            copy.wait()
        if c + 1 < total:
            fetch(c + 1)
        if c >= 3:
            x_out(c - 3).wait_send()

        @pl.loop(0, TILE // 256)
        def _(n):
            cols = pl.ds(pl.multiple_of(n * 256, 256), 256)
            left = left_buf[slot]
            result = jnp.dot(
                left.reshape(-1, left.shape[-1]), right_buf[c % 2, :, cols],
                preferred_element_type=jnp.float32,
            ).astype(jnp.bfloat16)
            stage[c % 3, :, :, :, cols] = result.reshape(*left.shape[:-1], 256)

        x_out(c).start()

    def fold(c):
        x_out(c).wait_recv()

        @pl.loop(0, planes)
        def _(p):
            x_land[c, p] = (
                x_land[c, p].astype(jnp.float32) + stage[c % 3, across, p].astype(jnp.float32)
            ).astype(jnp.bfloat16)

        for k in range(1, planes):
            plane_out(c, k).start()

    def finish(c):
        for k in range(1, planes):
            plane_out(c, k).wait_recv()
        if c >= 2:
            grad_out(c - 2).wait()
        value = x_land[c, plane].astype(jnp.float32)
        for k in range(1, planes):
            value += plane_land[c, k - 1].astype(jnp.float32)
        out_buf[c % 2] = value
        grad_out(c).start()

    def small_copy(step, peer, slot):
        return pltpu.make_async_remote_copy(
            small_land.at[0], small_land.at[slot], small_send.at[step], small_recv.at[step],
            device_id=peer, device_id_type=MESH,
        )

    def small_begin(step):
        if step < 3:
            if step == 0:
                pltpu.sync_copy(small_ref, small_land.at[0])
            small_copy(step, (core_peer, x_peer, y_peer)[step], 1 + step).start()
        else:
            for k in range(1, planes):
                small_copy(2 + k, plane_peers[k - 1], 3 + k).start()

    def small_end(step):
        if step < 3:
            small_copy(step, core_peer, 1 + step).wait()
            small_land[0] = small_land[0] + small_land[1 + step]
        else:
            for k in range(1, planes):
                small_copy(2 + k, core_peer, 3 + k).wait()
            value = jnp.zeros(small_land.shape[1:], jnp.float32)
            for p in range(planes):
                back = lax.rem(plane + planes - p, planes)
                value += small_land[jnp.where(back == 0, 0, 3 + back)]
            small_land[1] = value
            pltpu.sync_copy(small_land.at[1], small_out)

    fetch(0)
    for c in range(total + 2):
        if c < total:
            multiply(c)
        if 1 <= c <= total:
            fold(c - 1)
        if c >= 2:
            finish(c - 2)
        if c in (1, 2, 3, 4):
            small_end(c - 1)
        if c in (0, 1, 2, 3):
            small_begin(c)
    for a in order:
        left_out(a).wait_send()
    for c in range(total):
        right_out(c).wait_send()
        if c >= total - 3:
            x_out(c).wait_send()
        for k in range(1, planes):
            plane_out(c, k).wait_send()
    for c in range(total - 2, total):
        grad_out(c).wait()


def scatter_grads(lefts, rights, smalls):
    size = lax.axis_size("dp")
    planes = size // 4
    tokens, features = lefts[0].shape
    rows = features // size
    left = jnp.stack([array.T for array in lefts]).reshape(4, planes, 2, 2, rows, tokens)
    arrays = [array for array, _ in rights]
    widths = [array.shape[1] for array in arrays]
    jobs = [
        (which, i, start)
        for i, (array, which) in enumerate(rights)
        for start in range(0, array.shape[1], TILE)
    ]
    total = len(jobs)
    sem = pltpu.SemaphoreType.DMA
    hbm = pl.BlockSpec(memory_space=pl.ANY)
    results = pl.pallas_call(
        partial(scatter_kernel, planes, jobs, widths),
        out_shape=[jax.ShapeDtypeStruct((rows, width), jnp.float32) for width in widths]
        + [jax.ShapeDtypeStruct(smalls.shape, jnp.float32)]
        + [jax.ShapeDtypeStruct((4, planes, 2, rows, tokens), jnp.bfloat16)]
        + [jax.ShapeDtypeStruct(array.shape, jnp.bfloat16) for array in arrays],
        in_specs=[hbm] * (2 + len(arrays)),
        out_specs=[hbm] * (2 + 2 * len(arrays)),
        scratch_shapes=[
            pltpu.VMEM((2, 2, planes, rows, 2 * tokens), jnp.bfloat16),
            pltpu.VMEM((2, 2 * tokens, TILE), jnp.bfloat16),
            pltpu.VMEM((3, 2, planes, rows, TILE), jnp.bfloat16),
            pltpu.VMEM((total, planes, rows, TILE), jnp.bfloat16),
            pltpu.VMEM((total, planes - 1, rows, TILE), jnp.bfloat16),
            pltpu.VMEM((2, rows, TILE), jnp.float32),
            pltpu.VMEM((3 + planes, *smalls.shape), jnp.float32),
            sem((2, 2, 2)), sem((2, 2)), sem((2,)), sem((total,)), sem((total,)), sem((4,)), sem((4,)),
            sem((total,)), sem((total,)), sem((total, planes - 1)), sem((total, planes - 1)),
            sem((2 + planes,)), sem((2 + planes,)),
        ],
        compiler_params=pltpu.CompilerParams(
            collective_id=1, has_side_effects=True, vmem_limit_bytes=60 * 2**20
        ),
        name="scatter_grads",
    )(left, *arrays, smalls)
    return results[: len(arrays)], results[len(arrays)]


def shards(
    inputs,
    lengths,
    dealing,
    w_query,
    w_key,
    w_value,
    b_query,
    b_value,
    w_out,
    b_out,
    gain_first,
    shift_first,
    w_up,
    b_up,
    w_down,
    b_down,
    gain_second,
    shift_second,
    cotangent,
):
    group_index = lax.axis_index("dp")
    tensor_index = lax.axis_index("tensor")
    ordered = jnp.take(inputs, dealing, axis=0)
    arrived = lax.all_to_all(ordered, "dp", split_axis=0, concat_axis=2, tiled=True)
    features = arrived.shape[3]
    half_rows = arrived.shape[2]
    own_rows = arrived.reshape(half_rows, features)
    seq_len = half_rows * lax.axis_size("tensor")
    length = lengths[dealing[group_index]]
    key_valid = jnp.arange(seq_len) < length
    factor = HEAD_DIM ** (-0.5)
    head_cols = w_query.shape[1]
    heads_local = head_cols // HEAD_DIM
    up_cols = w_up.shape[1]
    query_bias = lax.dynamic_slice_in_dim(b_query, tensor_index * head_cols, head_cols)
    value_bias = lax.dynamic_slice_in_dim(b_value, tensor_index * head_cols, head_cols)
    up_bias = lax.dynamic_slice_in_dim(b_up, tensor_index * up_cols, up_cols)
    vectors = jnp.concatenate(
        (query_bias, value_bias, b_out, gain_first, shift_first, up_bias, b_down, gain_second, shift_second)
    ).reshape(1, -1)
    mask = jnp.broadcast_to(key_valid.astype(jnp.float32), (8, seq_len))
    weights, saved = forward(
        [w_query, w_key, w_value, w_out.T, w_up, w_down.T],
        own_rows, cotangent.reshape(half_rows, features), mask, vectors,
    )
    query_full, key_full, value_full, out_turned, up_full, down_turned = weights
    (
        full_in, _, qkv, mixed_heads, normed_full, inverse_full, full_hidden, active, slope,
        result, full_grad_down, second_full, second_sums,
    ) = saved
    output = result.reshape(cotangent.shape)
    own = partial(lax.dynamic_slice_in_dim, start_index=tensor_index * half_rows, slice_size=half_rows)
    normed_first, inverse_first, grad_second = own(normed_full), own(inverse_full)[:, :1], own(second_full)
    grad_gain_second, grad_shift_second, grad_b_down = jnp.sum(second_sums, axis=1)
    query_rows, key_rows, value_rows = (
        qkv[:, i * head_cols : (i + 1) * head_cols].reshape(seq_len, heads_local, HEAD_DIM) for i in range(3)
    )
    scores = attention_scores(query_rows, key_rows, key_valid, factor)
    row_max = jnp.max(scores, axis=-1, keepdims=True)
    log_norm = row_max + jnp.log(jnp.sum(jnp.exp(scores - row_max), axis=-1, keepdims=True))
    grad_active = jnp.dot(full_grad_down, down_turned, preferred_element_type=jnp.float32)
    grad_up = (grad_active * slope.astype(jnp.float32)).astype(jnp.bfloat16)
    grad_up_bias = jnp.sum(grad_up.astype(jnp.float32), axis=0)
    hidden_part = contract_cols(grad_up, up_full)
    grad_hidden = grad_second + lax.psum_scatter(
        hidden_part.astype(jnp.bfloat16), "tensor", scatter_dimension=0, tiled=True
    ).astype(jnp.float32)
    grad_first, grad_gain_first, grad_shift_first = norm_backward(
        grad_hidden, gain_first, normed_first, inverse_first
    )
    grad_attended = grad_first.astype(jnp.bfloat16)
    grad_b_out = jnp.sum(grad_attended.astype(jnp.float32), axis=0)
    full_grad_attended = lax.all_gather(grad_attended, "tensor", axis=0, tiled=True)
    grad_mixed = jnp.dot(
        full_grad_attended, out_turned, preferred_element_type=jnp.float32
    ).astype(jnp.bfloat16)
    grad_mixed = grad_mixed.reshape(seq_len, heads_local, HEAD_DIM)
    scores = attention_scores(query_rows, key_rows, key_valid, factor)
    softmax_again = jnp.exp(scores - log_norm)
    grad_values = jnp.einsum(
        "hqk,qhd->khd",
        softmax_again.astype(jnp.bfloat16),
        grad_mixed,
        preferred_element_type=jnp.float32,
    ).astype(jnp.bfloat16)
    grad_softmax = jnp.einsum(
        "qhd,khd->hqk", grad_mixed, value_rows, preferred_element_type=jnp.float32
    )
    row_inner = jnp.sum(softmax_again * grad_softmax, axis=-1, keepdims=True)
    grad_scores = (softmax_again * (grad_softmax - row_inner)).astype(jnp.bfloat16)
    grad_queries = (
        (
            jnp.einsum("hqk,khd->qhd", grad_scores, key_rows, preferred_element_type=jnp.float32)
            * factor
        )
        .astype(jnp.bfloat16)
        .reshape(seq_len, head_cols)
    )
    grad_keys = (
        (
            jnp.einsum("hqk,qhd->khd", grad_scores, query_rows, preferred_element_type=jnp.float32)
            * factor
        )
        .astype(jnp.bfloat16)
        .reshape(seq_len, head_cols)
    )
    grad_values = grad_values.reshape(seq_len, head_cols)
    grad_query_bias = jnp.sum(grad_queries.astype(jnp.float32), axis=0)
    grad_value_bias = jnp.sum(grad_values.astype(jnp.float32), axis=0)
    input_part = (
        contract_cols(grad_queries, query_full)
        + contract_cols(grad_keys, key_full)
        + contract_cols(grad_values, value_full)
    )
    grad_own = grad_first + lax.psum_scatter(
        input_part.astype(jnp.bfloat16), "tensor", scatter_dimension=0, tiled=True
    ).astype(jnp.float32)
    grad_sent = grad_own.astype(jnp.bfloat16).reshape(1, 1, half_rows, features)
    returned = lax.all_to_all(grad_sent, "dp", split_axis=2, concat_axis=0, tiled=True)
    grad_inputs = jnp.zeros_like(returned).at[dealing].set(returned)
    full_cols = b_query.shape[0]
    full_up = b_up.shape[0]
    smalls = (
        place_slice(grad_query_bias, full_cols, tensor_index * head_cols),
        place_slice(grad_value_bias, full_cols, tensor_index * head_cols),
        grad_b_out,
        place_slice(grad_up_bias, full_up, tensor_index * up_cols),
        grad_b_down,
        grad_gain_first,
        grad_shift_first,
        grad_gain_second,
        grad_shift_second,
    )
    sums, small_total = scatter_grads(
        [full_in, full_grad_attended, full_hidden, full_grad_down],
        [(active, 3), (grad_up, 2), (mixed_heads, 1), (grad_queries, 0), (grad_keys, 0), (grad_values, 0)],
        jnp.concatenate(smalls).reshape(-1, 128),
    )
    weight_sums = (sums[3], sums[4], sums[5], sums[2].T, sums[1], sums[0].T)
    small_total = small_total.reshape(-1)
    small_sums, at = [], 0
    for small in smalls:
        small_sums.append(small_total[at : at + small.shape[0]])
        at += small.shape[0]
    return (
        output,
        grad_inputs,
        weight_sums[0],
        weight_sums[1],
        weight_sums[2],
        small_sums[0],
        small_sums[1],
        weight_sums[3],
        small_sums[2],
        small_sums[5],
        small_sums[6],
        weight_sums[4],
        small_sums[3],
        weight_sums[5],
        small_sums[4],
        small_sums[7],
        small_sums[8],
    )


def solution(mesh):
    in_specs = (
        P(None, "tensor", "dp", None),
        P(),
        P(),
        P("dp", "tensor"),
        P("dp", "tensor"),
        P("dp", "tensor"),
        P(),
        P(),
        P("tensor", "dp"),
        P(),
        P(),
        P(),
        P("dp", "tensor"),
        P(),
        P("tensor", "dp"),
        P(),
        P(),
        P(),
        P("dp", "tensor", None),
    )
    out_specs = (
        P("dp", "tensor", None),
        P(None, "tensor", "dp", None),
        P("dp", "tensor"),
        P("dp", "tensor"),
        P("dp", "tensor"),
        P(),
        P(),
        P("tensor", "dp"),
        P(),
        P(),
        P(),
        P("dp", "tensor"),
        P(),
        P("tensor", "dp"),
        P(),
        P(),
        P(),
    )
    return jax.shard_map(shards, mesh=mesh, in_specs=in_specs, out_specs=out_specs, check_vma=False)
```

```python
from functools import partial

import jax
import jax.numpy as jnp
from jax import lax
from jax.experimental import pallas as pl
from jax.experimental.pallas import tpu as pltpu
from jax.sharding import PartitionSpec as P

HEAD_DIM = 128


EPSILON = 1e-05
MASKED = -1e30


def norm_forward(values, scale_gain, bias_shift):
    center = values - jnp.mean(values, axis=-1, keepdims=True)
    inverse = lax.rsqrt(jnp.mean(center * center, axis=-1, keepdims=True) + EPSILON)
    normed = center * inverse
    return (normed * scale_gain + bias_shift, normed, inverse)


def contract_rows(left, right):
    return lax.dot_general(
        left, right, (((0,), (0,)), ((), ())), preferred_element_type=jnp.float32
    )


def contract_cols(left, right):
    return lax.dot_general(
        left, right, (((1,), (1,)), ((), ())), preferred_element_type=jnp.float32
    )


MESH = pl.DeviceIdType.MESH
TILE = 1024
SLOPE = 0.7978845608028654


def place():
    dp, tensor = lax.axis_index("dp"), lax.axis_index("tensor")
    return dp // 4, (dp // 2) % 2, dp % 2, tensor


def device_of(plane, across, core, tensor):
    return ((plane * 2 + across) * 2 + core, tensor)


def enter(peers):
    barrier = pltpu.get_barrier_semaphore()
    for peer in peers:
        pl.semaphore_signal(barrier, inc=1, device_id=peer, device_id_type=MESH)
    pl.semaphore_wait(barrier, len(peers))


def gather_tiles(widths):
    return [(i, start) for i, width in enumerate(widths) for start in range(0, width, TILE)]


def forward_kernel(planes, widths, *refs):
    count = len(widths)
    shard_refs = refs[:count]
    own_ref, cot_ref, mask_ref, vec_ref = refs[count : count + 4]
    outs = refs[count + 4 :]
    full_refs = outs[:count]
    (
        x_full, cot_full, qkv_out, mixed_out, normed_out, inverse_out, hidden_out, active_out, slope_out,
        result_out, down_out, second_out, sums_out,
    ) = outs[count : count + 13]
    (
        w_buf, x_buf, qkv_buf, mixed_buf, attn_acc, attn_land, send_buf, hidden_buf, active_buf, slope_buf,
        down_acc, down_land, inverse_buf, result_buf, sums_buf,
        plane_send, plane_recv, x_send, x_recv, core_send, core_recv, w_sem, in_send, in_recv,
        attn_send, attn_recv, down_send, down_recv, load_sem, store_sem,
    ) = outs[count + 13 :]
    plane, across, core, tensor = place()
    far = [lax.rem(plane + k, planes) for k in range(planes)]
    near = [lax.rem(plane + planes - k, planes) for k in range(planes)]
    x_peer = device_of(plane, 1 - across, core, tensor)
    core_peer = device_of(plane, across, 1 - core, tensor)
    y_peer = device_of(plane, across, core, 1 - tensor)
    plane_peers = [device_of(far[k], across, core, tensor) for k in range(planes)]
    tiles = gather_tiles(widths)
    half, features = own_ref.shape
    tokens = 2 * half
    block = features // planes
    head_cols = mixed_buf.shape[1]
    factor = HEAD_DIM ** (-0.5)
    own_rows = pl.ds(pl.multiple_of(tensor * half, half), half)

    vec_at = {}
    at = 0
    for key, size in (
        ("b_query", head_cols), ("b_value", head_cols), ("b_out", features), ("gain_first", features),
        ("shift_first", features), ("b_up", widths[4]), ("b_down", features), ("gain_second", features),
        ("shift_second", features),
    ):
        vec_at[key] = at
        at += size

    def vector(key, start, size):
        return vec_ref[:, pl.ds(vec_at[key] + start, size)]

    first_down = len(tiles) - widths[5] // TILE
    units = [(c, k) for c in range(first_down) for k in range(planes)]
    units += [(c, k) for k in range(planes) for c in range(first_down, len(tiles))]
    ahead, lag = 6, 2

    def view(c, *where):
        i, start = tiles[c]
        return full_refs[i].at[(*where, slice(None), pl.ds(start, TILE))]

    def own(c):
        i, start = tiles[c]
        return shard_refs[i].at[:, pl.ds(start, TILE)]

    def unit_z(u, source):
        c, k = units[u]
        if k == 0:
            return pltpu.make_async_copy(own(c), view(c, plane, across, core), plane_recv.at[c, 0])
        return pltpu.make_async_remote_copy(
            own(c), view(c, source, across, core), plane_send.at[c, k], plane_recv.at[c, k],
            device_id=plane_peers[k], device_id_type=MESH,
        )

    def unit_x(u, side):
        c, k = units[u]
        part = view(c, near[k], side, core)
        return pltpu.make_async_remote_copy(
            part, part, x_send.at[c, k], x_recv.at[c, k], device_id=x_peer, device_id_type=MESH
        )

    def unit_core(u, side):
        c, k = units[u]
        part = view(c, near[k], slice(None), side)
        return pltpu.make_async_remote_copy(
            part, part, core_send.at[c, k], core_recv.at[c, k], device_id=core_peer, device_id_type=MESH
        )

    def z_start(u):
        unit_z(u, plane).start()

    def z_wait(u):
        c, k = units[u]
        if k == 0:
            unit_z(u, plane).wait()
        else:
            unit_z(u, near[k]).wait_recv()

    def pump(n):
        if n < len(units):
            z_wait(n)
            unit_x(n, across).start()
            if n + ahead < len(units):
                z_start(n + ahead)
        if n >= lag:
            unit_x(n - lag, 1 - across).wait_recv()
            unit_core(n - lag, core).start()

    def landed(u):
        unit_core(u, 1 - core).wait_recv()

    def tile_copies(c):
        i, start = tiles[c]
        return [
            pltpu.make_async_copy(
                full_refs[i].at[p, :, :, :, pl.ds(start, TILE)], w_buf.at[c % 2, p], w_sem.at[c % 2, p]
            )
            for p in range(planes)
        ]

    def load_tile(c):
        for u, (tile, _) in enumerate(units):
            if tile == c:
                landed(u)
        for copy in tile_copies(c):
            copy.start()

    def wait_tile(c):
        for copy in tile_copies(c):
            copy.wait()

    def down_copy(k, j):
        c = first_down + j
        return pltpu.make_async_copy(
            view(c, near[k], slice(None), slice(None)), w_buf.at[k % 2, j], w_sem.at[k % 2, j]
        )

    down_parts = widths[5] // TILE

    def load_down(k):
        for j in range(down_parts):
            landed(units.index((first_down + j, k)))
            down_copy(k, j).start()

    def flat(value):
        return value.reshape(-1, value.shape[-1])

    def load_x():
        exchange(0, own_ref, x_full).wait_recv()
        keep(0, own_ref, x_full).wait()
        copy = pltpu.make_async_copy(x_full, x_buf, load_sem.at[2])
        copy.start()
        copy.wait()

    def exchange(which, source, target):
        return pltpu.make_async_remote_copy(
            source, target.at[own_rows], in_send.at[which], in_recv.at[which],
            device_id=y_peer, device_id_type=MESH,
        )

    def keep(which, source, target):
        return pltpu.make_async_copy(source, target.at[own_rows], load_sem.at[which])

    def project(c, bias):
        wait_tile(c)

        @pl.loop(0, TILE // 512)
        def _(n):
            cols = pl.ds(pl.multiple_of(n * 512, 512), 512)
            value = jnp.dot(
                x_buf[...], flat(w_buf[c % 2, :, :, :, :, cols]), preferred_element_type=jnp.float32
            )
            if bias is not None:
                value += vec_ref[:, pl.ds(pl.multiple_of(vec_at[bias] + n * 512, 128), 512)]
            qkv_buf[:, pl.ds(pl.multiple_of(c * TILE + n * 512, 512), 512)] = value.astype(jnp.bfloat16)

    def attend(first, last):
        @pl.loop(first, last)
        def _(h):
            def cols(which):
                return pl.ds(pl.multiple_of(which * head_cols + h * HEAD_DIM, HEAD_DIM), HEAD_DIM)

            scores = contract_cols(qkv_buf[:, cols(0)], qkv_buf[:, cols(1)]) * factor
            scores = jnp.where(mask_ref[0:1, :] > 0.0, scores, MASKED)
            expanded = jnp.exp(scores - jnp.max(scores, axis=1, keepdims=True))
            weight = (expanded / jnp.sum(expanded, axis=1, keepdims=True)).astype(jnp.bfloat16)
            mixed_buf[:, cols(0)] = jnp.dot(
                weight, qkv_buf[:, cols(2)], preferred_element_type=jnp.float32
            ).astype(jnp.bfloat16)

    def block_cols(p):
        return pl.ds(pl.multiple_of(p * block, block), block)

    def attn_share(p):
        return pltpu.make_async_remote_copy(
            send_buf.at[:, block_cols(p)], attn_land.at[:, block_cols(p)], attn_send.at[p], attn_recv.at[p],
            device_id=y_peer, device_id_type=MESH,
        )

    def project_out():
        wait_tile(3)

        @pl.loop(0, planes)
        def _(p):
            value = contract_cols(mixed_buf[...], flat(w_buf[1, p]))
            attn_acc[:, block_cols(p)] = value
            send_buf[:, block_cols(p)] = value.astype(jnp.bfloat16)
            attn_share(p).start()

    def first_norm():
        @pl.loop(0, planes)
        def _(p):
            attn_share(p).wait()

        @pl.loop(0, tokens // 16)
        def _(i):
            rows = pl.ds(pl.multiple_of(i * 16, 16), 16)
            value = (
                x_buf[rows, :].astype(jnp.float32)
                + (attn_acc[rows, :] + attn_land[rows, :].astype(jnp.float32))
                + vector("b_out", 0, features)
            )
            hidden, normed, inverse = norm_forward(
                value, vector("gain_first", 0, features), vector("shift_first", 0, features)
            )
            attn_acc[rows, :] = normed
            inverse_buf[rows, :] = jnp.broadcast_to(inverse, (16, 128))
            hidden_buf[rows, :] = hidden.astype(jnp.bfloat16)

        store(0, attn_acc, normed_out).start()
        store(1, inverse_buf, inverse_out).start()
        store(2, hidden_buf, hidden_out).start()
        exchange(1, cot_ref, cot_full).wait_recv()
        keep(1, cot_ref, cot_full).wait()
        pltpu.make_async_copy(cot_full, x_buf, load_sem.at[2]).start()

    def store(which, source, target):
        return pltpu.make_async_copy(source, target, store_sem.at[which])

    def slope_store(j):
        return pltpu.make_async_copy(
            slope_buf.at[j % 2], slope_out.at[:, pl.ds(j * TILE, TILE)], store_sem.at[5 + j % 2]
        )

    def raise_up(j):
        c = 4 + j
        wait_tile(c)
        if j >= 2:
            slope_store(j - 2).wait()

        @pl.loop(0, TILE // 256)
        def _(n):
            cols = pl.ds(pl.multiple_of(n * 256, 256), 256)
            value = jnp.dot(
                hidden_buf[...], flat(w_buf[c % 2, :, :, :, :, cols]), preferred_element_type=jnp.float32
            )
            value += vec_ref[:, pl.ds(pl.multiple_of(vec_at["b_up"] + j * TILE + n * 256, 128), 256)]
            square = value * value
            bend = jnp.tanh(SLOPE * value * (1.0 + 0.044715 * square))
            rise = 0.5 * (1.0 + bend)
            active_buf[:, pl.ds(pl.multiple_of(j * TILE + n * 256, 256), 256)] = (value * rise).astype(
                jnp.bfloat16
            )
            slope_buf[j % 2, :, cols] = (
                rise + 0.5 * value * (1.0 - bend * bend) * (SLOPE * (1.0 + 3.0 * 0.044715 * square))
            ).astype(jnp.bfloat16)

        slope_store(j).start()

    def down_share(k):
        cols = block_cols(near[k])
        return pltpu.make_async_remote_copy(
            send_buf.at[:, cols], down_land.at[:, cols], down_send.at[k], down_recv.at[k],
            device_id=y_peer, device_id_type=MESH,
        )

    def lower(k):
        cols = block_cols(near[k])
        value = None
        for j in range(down_parts):
            down_copy(k, j).wait()
            part = contract_cols(active_buf[:, j * TILE : (j + 1) * TILE], flat(w_buf[k % 2, j]))
            value = part if value is None else value + part
        down_acc[:, cols] = value
        send_buf[:, cols] = value.astype(jnp.bfloat16)
        down_share(k).start()

    def second_norm():
        for k in range(planes):
            down_share(k).wait()
        pltpu.make_async_copy(cot_full, x_buf, load_sem.at[2]).wait()
        store(2, hidden_buf, hidden_out).wait()
        sums_buf[...] = jnp.zeros_like(sums_buf)
        gain = vector("gain_second", 0, features)

        def rows_of(which, i):
            base = tensor if which == 0 else 1 - tensor
            return pl.ds(pl.multiple_of(base * half + i * 16, 16), 16)

        for which in (0, 1):
            @pl.loop(0, half // 16)
            def _(i):
                rows = rows_of(which, i)
                hidden = attn_acc[rows, :] * vector("gain_first", 0, features) + vector(
                    "shift_first", 0, features
                )
                value = (
                    hidden
                    + (down_acc[rows, :] + down_land[rows, :].astype(jnp.float32))
                    + vector("b_down", 0, features)
                )
                result, normed, inverse = norm_forward(value, gain, vector("shift_second", 0, features))
                grad_out = x_buf[rows, :].astype(jnp.float32)
                scaled = grad_out * gain
                grad = inverse * (
                    scaled
                    - jnp.mean(scaled, axis=-1, keepdims=True)
                    - normed * jnp.mean(scaled * normed, axis=-1, keepdims=True)
                )
                down_acc[rows, :] = grad
                low = grad.astype(jnp.bfloat16)
                hidden_buf[rows, :] = low
                if which == 0:
                    result_buf[pl.ds(pl.multiple_of(i * 16, 16), 16), :] = result.astype(jnp.bfloat16)
                    sums_buf[0] += grad_out * normed
                    sums_buf[1] += grad_out
                    sums_buf[2] += low.astype(jnp.float32)

        for which, source, target in (
            (2, hidden_buf, down_out), (3, down_acc, second_out), (4, result_buf, result_out), (9, sums_buf, sums_out),
        ):
            store(which, source, target).start()

    enter(plane_peers[1:] + [x_peer, core_peer, y_peer])
    for u in range(ahead):
        z_start(u)
    for which, source, target in ((0, own_ref, x_full), (1, cot_ref, cot_full)):
        exchange(which, source, target).start()
        keep(which, source, target).start()

    plan = {}

    def at_slot(n, step, *args):
        plan.setdefault(n, []).append((step, args))

    def ready(c):
        return planes * (c + 1) + 2

    heads = head_cols // HEAD_DIM
    at_slot(ready(0), load_x)
    for c in range(3):
        at_slot(ready(c), load_tile, c)
        at_slot(ready(c) + 1, project, c, ("b_query", None, "b_value")[c])
    begin = ready(2) + 2
    for q in range(4):
        at_slot(begin + q, attend, q * heads // 4, (q + 1) * heads // 4)
    at_slot(begin + 3, load_tile, 3)
    at_slot(begin + 4, project_out)
    norm_slot = begin + 4 + 10 * planes // 4
    at_slot(norm_slot, first_norm)
    at_slot(max(ready(4), begin), load_tile, 4)
    at_slot(max(ready(5), begin + 4), load_tile, 5)
    for j in range(4):
        slot = max(norm_slot + 1 + j, ready(4 + j) + 1)
        at_slot(slot, raise_up, j)
        if j >= 2:
            plan.setdefault(max(norm_slot + 1 + j - 2, ready(4 + j)), []).append((load_tile, (4 + j,)))
    for k in range(planes):
        slot = planes * first_down + down_parts * (k + 1) + 2
        at_slot(slot, load_down, k)
        at_slot(slot + 1, lower, k)
    last = max(max(plan), len(units) + lag - 1)
    for n in range(last + 1):
        if n < len(units) + lag:
            pump(n)
        for step, args in plan.get(n, []):
            step(*args)
        if n == begin + 3:
            store(7, qkv_buf, qkv_out).start()
            store(8, mixed_buf, mixed_out).start()
    store(10, active_buf, active_out).start()
    second_norm()
    for which, source, target in (
        (0, attn_acc, normed_out), (1, inverse_buf, inverse_out), (2, hidden_buf, down_out),
        (3, down_acc, second_out), (4, result_buf, result_out), (7, qkv_buf, qkv_out),
        (8, mixed_buf, mixed_out), (9, sums_buf, sums_out), (10, active_buf, active_out),
    ):
        store(which, source, target).wait()
    for j in range(2, 4):
        slope_store(j).wait()
    for which, source, target in ((0, own_ref, x_full), (1, cot_ref, cot_full)):
        exchange(which, source, target).wait_send()
    for u, (c, k) in enumerate(units):
        if k > 0:
            unit_z(u, plane).wait_send()
        unit_x(u, across).wait_send()
        unit_core(u, core).wait_send()


def forward(shard_list, own, cot, mask, vectors):
    planes = lax.axis_size("dp") // 4
    widths = [shard.shape[1] for shard in shard_list]
    total = sum(width // TILE for width in widths)
    half, features = own.shape
    tokens, rows = 2 * half, shard_list[0].shape[0]
    head_cols, up_cols = widths[0], widths[4]
    sem, low, high = pltpu.SemaphoreType.DMA, jnp.bfloat16, jnp.float32
    hbm, vmem = pl.BlockSpec(memory_space=pl.ANY), pl.BlockSpec(memory_space=pltpu.VMEM)
    shapes = [((planes, 2, 2, *shard.shape), low) for shard in shard_list] + [
        ((tokens, features), low), ((tokens, features), low), ((tokens, 3 * head_cols), low),
        ((tokens, head_cols), low), ((tokens, features), high), ((tokens, 128), high),
        ((tokens, features), low), ((tokens, up_cols), low), ((tokens, up_cols), low),
        ((half, features), low), ((tokens, features), low), ((tokens, features), high),
        ((3, 16, features), high),
    ]
    results = pl.pallas_call(
        partial(forward_kernel, planes, widths),
        out_shape=[jax.ShapeDtypeStruct(*shape) for shape in shapes],
        in_specs=[hbm] * (len(shard_list) + 2) + [vmem] * 2,
        out_specs=[hbm] * len(shapes),
        scratch_shapes=[
            pltpu.VMEM((2, planes, 2, 2, rows, TILE), low),
            pltpu.VMEM((tokens, features), low),
            pltpu.VMEM((tokens, 3 * head_cols), low),
            pltpu.VMEM((tokens, head_cols), low),
            pltpu.VMEM((tokens, features), high),
            pltpu.VMEM((tokens, features), low),
            pltpu.VMEM((tokens, features), low),
            pltpu.VMEM((tokens, features), low),
            pltpu.VMEM((tokens, up_cols), low),
            pltpu.VMEM((2, tokens, TILE), low),
            pltpu.VMEM((tokens, features), high),
            pltpu.VMEM((tokens, features), low),
            pltpu.VMEM((tokens, 128), high),
            pltpu.VMEM((half, features), low),
            pltpu.VMEM((3, 16, features), high),
            *[sem((total, planes))] * 6,
            sem((2, max(planes, 4))), sem((2,)), sem((2,)),
            sem((planes,)), sem((planes,)), sem((planes,)), sem((planes,)), sem((3,)), sem((11,)),
        ],
        compiler_params=pltpu.CompilerParams(
            collective_id=0, has_side_effects=True, vmem_limit_bytes=62 * 2**20
        ),
        name="forward_gather",
    )(*shard_list, own, cot, mask, vectors)
    return results[: len(shard_list)], results[len(shard_list) :]


JOB = 512


def backward_kernel(planes, *refs):
    (
        query_w, key_w, value_w, out_w, up_w, down_w,
        x_in, qkv_in, mixed_in, normed_in, inverse_in, hidden_in, active_in, slope_in, down_in, second_in,
        sums_in, mask_ref, gain_ref,
    ) = refs[:19]
    (
        grad_query, grad_key, grad_value, grad_out_w, grad_up, grad_down, small_out, own_out,
        left_own, left_far, active_far, rise_own, rise_far, mixed_far, qkv_own, qkv_far,
    ) = refs[19:35]
    (
        left_buf, right_buf, stage, x_land, plane_land, out_buf, tile_buf, wide_buf, low_buf, rise_buf,
        slope_buf, acc_buf, hidden_land, send_buf, qkv_buf, turn_buf, input_land, row_buf, inverse_buf,
        sums_buf, small_land,
        left_sem, right_sem, out_sem, core_send, core_recv, left_send, left_recv, x_send, x_recv,
        plane_send, plane_recv, small_send, small_recv, tile_sem, wide_sem, slope_sem, load_sem, store_sem,
        turn_sem, hidden_send, hidden_recv, input_send, input_recv, row_sem,
    ) = refs[35:]
    plane, across, core, tensor = place()
    far = [lax.rem(plane + k, planes) for k in range(planes)]
    x_peer = device_of(plane, 1 - across, core, tensor)
    core_peer = device_of(plane, across, 1 - core, tensor)
    y_peer = device_of(plane, across, core, 1 - tensor)
    plane_peers = [device_of(far[k], across, core, tensor) for k in range(planes)]
    tokens, features = low_buf.shape
    half = tokens // 2
    head_cols = mixed_in.shape[1]
    heads = head_cols // HEAD_DIM
    up_cols = active_in.shape[1]
    block = features // planes
    factor = HEAD_DIM ** (-0.5)
    slots = x_land.shape[0]
    thin = tile_buf.shape[-1]

    jobs = [(0, active_in, active_far, s, grad_down, s) for s in range(0, up_cols, JOB)]
    jobs += [(1, rise_own, rise_far, s, grad_up, s) for s in range(0, up_cols, JOB)]
    jobs += [(2, mixed_in, mixed_far, s, grad_out_w, s) for s in range(0, head_cols, JOB)]
    for which, result in enumerate((grad_query, grad_key, grad_value)):
        jobs += [
            (3, qkv_own, qkv_far, which * head_cols + s, result, s) for s in range(0, head_cols, JOB)
        ]
    total = len(jobs)
    up_first, out_first, qkv_first = (
        [job[0] for job in jobs].index(a) for a in (1, 2, 3)
    )

    def local(source, target, sem):
        return pltpu.make_async_copy(source, target, sem)

    def remote(source, target, send, recv, peer):
        return pltpu.make_async_remote_copy(
            source, target, send, recv, device_id=peer, device_id_type=MESH
        )

    def left_out(a):
        return remote(
            turn_buf.at[:, :, 1 - core], left_far.at[a], left_send.at[a], left_recv.at[a], core_peer
        )

    def left_keep(a):
        return local(turn_buf.at[:, :, core], left_own.at[a], turn_sem.at[0])

    kept = set()

    def left_kept(a):
        if a not in kept:
            kept.add(a)
            left_keep(a).wait()

    def turn(a, source):
        if a > 0:
            left_out(a - 1).wait_send()
            left_kept(a - 1)

        @pl.loop(0, planes)
        def _(p):
            cols = pl.ds(pl.multiple_of(p * block, block), block)
            turn_buf[p] = source[:, cols].T.reshape(turn_buf.shape[1:])

        left_keep(a).start()
        left_out(a).start()

    def right_out(c, source=None):
        _, own, other, start, _, _ = jobs[c]
        cols = pl.ds(start, JOB)
        return remote(
            (own if source is None else source).at[:, cols], other.at[:, cols], core_send.at[c],
            core_recv.at[c], core_peer,
        )

    def left_load(a):
        slot = a % 2
        copies = []
        for side in range(2):
            copies.append(
                local(left_own.at[a, :, side], left_buf.at[slot, side, :, :, pl.ds(0, tokens)], left_sem.at[slot, 0, side])
            )
            copies.append(
                local(left_far.at[a, :, side], left_buf.at[slot, side, :, :, pl.ds(tokens, tokens)], left_sem.at[slot, 1, side])
            )
        return copies

    def right_load(c):
        _, own, other, start, _, _ = jobs[c]
        slot, cols = c % 2, pl.ds(start, JOB)
        return [
            local(own.at[:, cols], right_buf.at[slot, pl.ds(0, tokens)], right_sem.at[slot, 0]),
            local(other.at[:, cols], right_buf.at[slot, pl.ds(tokens, tokens)], right_sem.at[slot, 1]),
        ]

    def x_out(c):
        return remote(
            stage.at[c % 3, 1 - across], x_land.at[c % slots], x_send.at[c], x_recv.at[c], x_peer
        )

    def plane_out(c, k):
        return remote(
            x_land.at[c % slots, far[k]], plane_land.at[c % slots, k - 1], plane_send.at[c, k - 1],
            plane_recv.at[c, k - 1], plane_peers[k],
        )

    def grad_out(c):
        _, _, _, _, result, start = jobs[c]
        return local(out_buf.at[c % 2], result.at[:, pl.ds(start, JOB)], out_sem.at[c % 2])

    def new_left(c):
        return c == 0 or jobs[c - 1][0] != jobs[c][0]

    def fetch(c):
        a = jobs[c][0]
        if new_left(c):
            left_kept(a)
            left_out(a).wait_recv()
            for copy in left_load(a):
                copy.start()
        right_out(c).wait_recv()
        for copy in right_load(c):
            copy.start()

    def multiply(c):
        a = jobs[c][0]
        if new_left(c):
            for copy in left_load(a):
                copy.wait()
        for copy in right_load(c):
            copy.wait()
        if c + 1 < total:
            fetch(c + 1)
        if c >= 3:
            x_out(c - 3).wait_send()

        @pl.loop(0, JOB // 256)
        def _(n):
            cols = pl.ds(pl.multiple_of(n * 256, 256), 256)
            left = left_buf[a % 2]
            result = jnp.dot(
                left.reshape(-1, left.shape[-1]), right_buf[c % 2, :, cols],
                preferred_element_type=jnp.float32,
            ).astype(jnp.bfloat16)
            stage[c % 3, :, :, :, cols] = result.reshape(*left.shape[:-1], 256)

        x_out(c).start()

    def fold(c):
        x_out(c).wait_recv()
        slot = c % slots

        @pl.loop(0, planes)
        def _(p):
            x_land[slot, p] = (
                x_land[slot, p].astype(jnp.float32) + stage[c % 3, across, p].astype(jnp.float32)
            ).astype(jnp.bfloat16)

        for k in range(1, planes):
            plane_out(c, k).start()

    def finish(c):
        for k in range(1, planes):
            plane_out(c, k).wait()
        if c >= 2:
            grad_out(c - 2).wait()
        value = x_land[c % slots, plane].astype(jnp.float32)
        for k in range(1, planes):
            value += plane_land[c % slots, k - 1].astype(jnp.float32)
        out_buf[c % 2] = value
        grad_out(c).start()

    def small_copy(step, peer, slot):
        return remote(
            small_land.at[0], small_land.at[slot], small_send.at[step], small_recv.at[step], peer
        )

    def small_begin(step):
        if step < 3:
            small_copy(step, (core_peer, x_peer, y_peer)[step], 1 + step).start()
        else:
            for k in range(1, planes):
                small_copy(2 + k, plane_peers[k], 3 + k).start()

    def small_end(step):
        if step < 3:
            small_copy(step, core_peer, 1 + step).wait()
            small_land[0] = small_land[0] + small_land[1 + step]
        else:
            for k in range(1, planes):
                small_copy(2 + k, core_peer, 3 + k).wait()
            value = jnp.zeros(small_land.shape[1:], jnp.float32)
            for p in range(planes):
                back = lax.rem(plane + planes - p, planes)
                value += small_land[jnp.where(back == 0, 0, 3 + back)]
            small_land[1] = value
            local(small_land.at[1], small_out, load_sem.at[0]).start()

    def total_row(value):
        return jnp.sum(value, axis=0, keepdims=True)

    def tile_copy(weight, start, slot):
        return [
            local(weight.at[p, :, :, :, pl.ds(start, thin)], tile_buf.at[slot, p], tile_sem.at[slot, p])
            for p in range(planes)
        ]

    def slope_copy(start, slot):
        return local(slope_in.at[:, pl.ds(start, thin)], slope_buf.at[slot], slope_sem.at[slot])

    def flat(value):
        return value.reshape(-1, value.shape[-1])

    def rise_start(i):
        for copy in tile_copy(down_w, i * thin, i % 2):
            copy.start()
        slope_copy(i * thin, i % 2).start()

    def rise_store(g):
        cols = pl.ds(g * 2 * JOB, 2 * JOB)
        return local(rise_buf.at[:, cols], rise_own.at[:, cols], store_sem.at[g])

    def rise(g):
        per = 2 * JOB // thin
        for i in range(g * per, (g + 1) * per):
            for copy in tile_copy(down_w, i * thin, i % 2):
                copy.wait()
            slope_copy(i * thin, i % 2).wait()
            value = jnp.dot(low_buf[...], flat(tile_buf[i % 2]), preferred_element_type=jnp.float32)
            value = (value * slope_buf[i % 2].astype(jnp.float32)).astype(jnp.bfloat16)
            rise_buf[:, i * thin : (i + 1) * thin] = value
            if i + 2 < up_cols // thin:
                rise_start(i + 2)
            row = 3 + tensor * (up_cols // features) + (i * thin) // features
            col = (i * thin) % features
            small_land[0, pl.ds(row, 1), col : col + thin] = total_row(value.astype(jnp.float32))
        rise_store(g).start()
        for c in (up_first + 2 * g, up_first + 2 * g + 1):
            right_out(c, rise_buf).start()

    def block_cols(p):
        return pl.ds(pl.multiple_of(p * block, block), block)

    def wide_copy(p, side):
        return local(
            up_w.at[p, :, :, :, pl.ds(side * features, features)], wide_buf.at[side], wide_sem.at[side, 0]
        )

    def hidden_share(p):
        return remote(
            send_buf.at[:, block_cols(p)], hidden_land.at[:, block_cols(p)], hidden_send.at[p],
            hidden_recv.at[p], y_peer,
        )

    def hidden_start():
        for side in range(2):
            wide_copy(0, side).start()

    def hidden_back(first, last):
        @pl.loop(first, last)
        def _(p):
            value = None
            for side in range(2):
                wide_copy(p, side).wait()
                part = contract_cols(
                    rise_buf[:, side * features : (side + 1) * features], flat(wide_buf[side])
                )
                value = part if value is None else value + part

                @pl.when(p + 1 < planes)
                def _():
                    wide_copy(p + 1, side).start()

            acc_buf[:, block_cols(p)] = value
            send_buf[:, block_cols(p)] = value.astype(jnp.bfloat16)
            hidden_share(p).start()

    strip = row_buf.shape[2]

    def row_start(which, i):
        base = tensor if which == 0 else 1 - tensor
        return pl.multiple_of(base * half + i * strip, strip)

    def row_copies(which, i):
        rows = pl.ds(row_start(which, i), strip)
        slot = (which * (half // strip) + i) % 2
        return [
            local(normed_in.at[rows], row_buf.at[slot, 0], row_sem.at[slot, 0]),
            local(second_in.at[rows], row_buf.at[slot, 1], row_sem.at[slot, 1]),
        ]

    strips = [(which, i) for which in range(2) for i in range(half // strip)]

    def norm_start():
        for pair in strips[:2]:
            for copy in row_copies(*pair):
                copy.start()
        local(inverse_in, inverse_buf, load_sem.at[1]).start()

    def norm_back():
        @pl.loop(0, planes)
        def _(p):
            hidden_share(p).wait()

        local(inverse_in, inverse_buf, load_sem.at[1]).wait()
        sums_buf[...] = jnp.zeros_like(sums_buf)
        for at, (which, i) in enumerate(strips):
            for copy in row_copies(which, i):
                copy.wait()

            @pl.loop(0, strip // 16)
            def _(r):
                local_rows = pl.ds(pl.multiple_of(r * 16, 16), 16)
                rows = pl.ds(pl.multiple_of(row_start(which, i) + r * 16, 16), 16)
                normed = row_buf[at % 2, 0, local_rows, :]
                grad_hidden = row_buf[at % 2, 1, local_rows, :] + (
                    acc_buf[rows, :] + hidden_land[rows, :].astype(jnp.float32)
                )
                scaled = grad_hidden * gain_ref[...]
                grad = inverse_buf[rows, 0:1] * (
                    scaled
                    - jnp.mean(scaled, axis=-1, keepdims=True)
                    - normed * jnp.mean(scaled * normed, axis=-1, keepdims=True)
                )
                acc_buf[rows, :] = grad
                low = grad.astype(jnp.bfloat16)
                low_buf[rows, :] = low
                if which == 0:
                    sums_buf[0] += grad_hidden * normed
                    sums_buf[1] += grad_hidden
                    sums_buf[2] += low.astype(jnp.float32)

            if at + 2 < len(strips):
                for copy in row_copies(*strips[at + 2]):
                    copy.start()
        small_land[0, 8:9, :] = total_row(sums_buf[0])
        small_land[0, 9:10, :] = total_row(sums_buf[1])
        small_land[0, 2:3, :] = total_row(sums_buf[2])

    def mixed_start():
        for i in range(2):
            for copy in tile_copy(out_w, i * thin, i):
                copy.start()
        for g in range(up_cols // (2 * JOB)):
            for c in (up_first + 2 * g, up_first + 2 * g + 1):
                right_out(c, rise_buf).wait_send()
        local(qkv_in, rise_buf.at[:, pl.ds(0, 3 * head_cols)], load_sem.at[2]).start()

    def mixed_back():
        for i in range(head_cols // thin):
            for copy in tile_copy(out_w, i * thin, i % 2):
                copy.wait()
            value = jnp.dot(low_buf[...], flat(tile_buf[i % 2]), preferred_element_type=jnp.float32)
            start = 3 * head_cols + i * thin
            rise_buf[:, start : start + thin] = value.astype(jnp.bfloat16)
            if i + 2 < head_cols // thin:
                for copy in tile_copy(out_w, (i + 2) * thin, i % 2):
                    copy.start()

    def attend_back(first, last):
        @pl.loop(first, last)
        def _(h):
            def cols(which):
                return pl.ds(pl.multiple_of(which * head_cols + h * HEAD_DIM, HEAD_DIM), HEAD_DIM)

            key, value = rise_buf[:, cols(1)], rise_buf[:, cols(2)]
            key_sum = value_sum = None
            query_total = jnp.zeros((1, HEAD_DIM), jnp.float32)
            for part in range(2):
                rows = slice(part * half, (part + 1) * half)
                query, grad_mixed = rise_buf[rows, cols(0)], rise_buf[rows, cols(3)]
                scores = contract_cols(query, key) * factor
                scores = jnp.where(mask_ref[0:1, :] > 0.0, scores, MASKED)
                expanded = jnp.exp(scores - jnp.max(scores, axis=1, keepdims=True))
                weight = expanded / jnp.sum(expanded, axis=1, keepdims=True)
                grad_weight = contract_cols(grad_mixed, value)
                inner = jnp.sum(weight * grad_weight, axis=1, keepdims=True)
                grad_scores = (weight * (grad_weight - inner)).astype(jnp.bfloat16)
                grad_value = contract_rows(weight.astype(jnp.bfloat16), grad_mixed)
                grad_key = contract_rows(grad_scores, query)
                grad_query = (
                    jnp.dot(grad_scores, key, preferred_element_type=jnp.float32) * factor
                ).astype(jnp.bfloat16)
                qkv_buf[rows, cols(0)] = grad_query
                query_total += total_row(grad_query.astype(jnp.float32))
                key_sum = grad_key if key_sum is None else key_sum + grad_key
                value_sum = grad_value if value_sum is None else value_sum + grad_value
            qkv_buf[:, cols(1)] = (key_sum * factor).astype(jnp.bfloat16)
            value_low = value_sum.astype(jnp.bfloat16)
            qkv_buf[:, cols(2)] = value_low
            at = pl.ds(pl.multiple_of(tensor * head_cols + h * HEAD_DIM, HEAD_DIM), HEAD_DIM)
            small_land[0, 0:1, at] = query_total
            small_land[0, 1:2, at] = total_row(value_low.astype(jnp.float32))

    def attend_done():
        local(qkv_buf, qkv_own, store_sem.at[4]).start()
        for c in range(qkv_first, total):
            right_out(c, qkv_buf).start()
        input_start(0)

    def input_copies(p):
        return [
            local(query_w.at[p], wide_buf.at[0, :, :, :, pl.ds(0, head_cols)], wide_sem.at[0, 0]),
            local(key_w.at[p], wide_buf.at[0, :, :, :, pl.ds(head_cols, head_cols)], wide_sem.at[0, 1]),
            local(value_w.at[p], wide_buf.at[1, :, :, :, pl.ds(0, head_cols)], wide_sem.at[1, 0]),
        ]

    def input_start(p):
        for copy in input_copies(p):
            copy.start()

    own_rows = pl.ds(pl.multiple_of(tensor * half, half), half)
    other_rows = pl.ds(pl.multiple_of((1 - tensor) * half, half), half)

    def input_share(p):
        return remote(
            send_buf.at[pl.ds(0, half), block_cols(p)], input_land.at[:, block_cols(p)], input_send.at[p],
            input_recv.at[p], y_peer,
        )

    def input_back(first, last):
        @pl.loop(first, last)
        def _(p):
            for copy in input_copies(p):
                copy.wait()
            pair = flat(wide_buf[0])
            single = flat(wide_buf[1, :, :, :, 0:head_cols])

            def share(rows):
                return contract_cols(qkv_buf[rows, 0 : 2 * head_cols], pair) + contract_cols(
                    qkv_buf[rows, 2 * head_cols : 3 * head_cols], single
                )

            send_buf[0:half, block_cols(p)] = share(other_rows).astype(jnp.bfloat16)
            input_share(p).start()
            acc_buf[own_rows, block_cols(p)] += share(own_rows)

            @pl.when(p + 1 < planes)
            def _():
                input_start(p + 1)

    def input_done():
        @pl.loop(0, planes)
        def _(p):
            input_share(p).wait()

        @pl.loop(0, half // 16)
        def _(i):
            rows = pl.ds(pl.multiple_of(tensor * half + i * 16, 16), 16)
            land = pl.ds(pl.multiple_of(i * 16, 16), 16)
            send_buf[pl.ds(pl.multiple_of(half + i * 16, 16), 16), :] = (
                acc_buf[rows, :] + input_land[land, :].astype(jnp.float32)
            ).astype(jnp.bfloat16)

        local(send_buf.at[pl.ds(half, half)], own_out, load_sem.at[3]).start()

    local(down_in, low_buf, load_sem.at[0]).start()
    local(hidden_in, send_buf, load_sem.at[1]).start()
    local(sums_in, sums_buf, load_sem.at[2]).start()
    rise_start(0)
    rise_start(1)
    enter(plane_peers[1:] + [x_peer, core_peer, y_peer])
    for c in range(up_first):
        right_out(c).start()
    local(down_in, low_buf, load_sem.at[0]).wait()
    turn(0, low_buf)
    small_land[0] = jnp.zeros(small_land.shape[1:], jnp.float32)
    local(sums_in, sums_buf, load_sem.at[2]).wait()
    for i, row in enumerate((10, 11, 7)):
        small_land[0, row : row + 1, :] = total_row(sums_buf[i])
    fetch(0)

    def turn_hidden():
        local(hidden_in, send_buf, load_sem.at[1]).wait()
        turn(1, send_buf)

    def stored():
        for g in range(up_cols // (2 * JOB)):
            rise_store(g).wait()

    def load_input():
        local(x_in, low_buf, load_sem.at[1]).start()

    def turn_input():
        local(x_in, low_buf, load_sem.at[1]).wait()
        turn(3, low_buf)

    def start_out():
        for c in range(out_first, qkv_first):
            right_out(c).start()

    def wait_qkv():
        local(qkv_in, rise_buf.at[:, pl.ds(0, 3 * head_cols)], load_sem.at[2]).wait()

    def store_qkv_wait():
        local(qkv_buf, qkv_own, store_sem.at[4]).wait()

    plan = {
        0: [(rise, 0)],
        1: [(rise, 1)],
        2: [(rise, 2)],
        3: [(rise, 3), (turn_hidden,), (hidden_start,)],
        4: [(hidden_back, 0, planes // 2)],
        5: [(hidden_back, planes // 2, planes), (norm_start,), (start_out,), (stored,)],
        10: [(norm_back,), (mixed_start,)],
        11: [(turn, 2, low_buf), (mixed_back,), (load_input,)],
        12: [(wait_qkv,), (attend_back, 0, heads // 4), (turn_input,)],
        13: [(attend_back, heads // 4, heads // 2)],
        14: [(attend_back, heads // 2, 3 * heads // 4)],
        15: [(attend_back, 3 * heads // 4, heads), (attend_done,)],
        16: [(input_back, 0, planes // 2), (small_begin, 0), (store_qkv_wait,)],
        17: [(input_back, planes // 2, planes), (small_end, 0), (small_begin, 1)],
        18: [(small_end, 1), (small_begin, 2)],
        19: [(small_end, 2), (small_begin, 3)],
        20: [(input_done,), (small_end, 3)],
    }
    for n in range(total + 4):
        if n < total:
            multiply(n)
        for step in plan.get(n, []):
            step[0](*step[1:])
        if 2 <= n < total + 2:
            fold(n - 2)
        if n >= 4:
            finish(n - 4)
    local(small_land.at[1], small_out, load_sem.at[0]).wait()
    local(send_buf.at[pl.ds(half, half)], own_out, load_sem.at[3]).wait()
    left_out(3).wait_send()
    for c in range(total):
        if not up_first <= c < out_first:
            right_out(c).wait_send()
        if c >= total - 3:
            x_out(c).wait_send()
    for c in range(total - 2, total):
        grad_out(c).wait()


def backward(weights, saved, mask, gain):
    planes, _, _, rows, head_cols = weights[0].shape
    up_cols = weights[4].shape[-1]
    tokens, features = saved[0].shape
    total = (2 * up_cols + 4 * head_cols) // JOB
    slots = 8
    thin, strip = 256, 64
    sem, low, high = pltpu.SemaphoreType.DMA, jnp.bfloat16, jnp.float32
    hbm, vmem = pl.BlockSpec(memory_space=pl.ANY), pl.BlockSpec(memory_space=pltpu.VMEM)
    small_rows = 16
    shapes = (
        [((rows, head_cols), high)] * 4 + [((rows, up_cols), high)] * 2
        + [((small_rows, features), high), ((tokens // 2, features), low)]
        + [((4, planes, 2, rows, tokens), low)] * 2
        + [((tokens, up_cols), low)] * 3 + [((tokens, head_cols), low)] + [((tokens, 3 * head_cols), low)] * 2
    )
    scratch = [
        ((2, 2, planes, rows, 2 * tokens), low), ((2, 2 * tokens, JOB), low), ((3, 2, planes, rows, JOB), low),
        ((slots, planes, rows, JOB), low), ((slots, planes - 1, rows, JOB), low), ((2, rows, JOB), high),
        ((2, planes, 2, 2, rows, thin), low), ((2, 2, 2, rows, features), low), ((tokens, features), low),
        ((tokens, up_cols), low), ((2, tokens, thin), low), ((tokens, features), high),
        ((tokens, features), low), ((tokens, features), low), ((tokens, 3 * head_cols), low),
        ((planes, 2, 2, rows, tokens), low), ((tokens // 2, features), low), ((2, 2, strip, features), high),
        ((tokens, 128), high), ((3, 16, features), high), ((3 + planes, small_rows, features), high),
    ]
    sems = [
        (2, 2, 2), (2, 2), (2,), (total,), (total,), (4,), (4,), (total,), (total,),
        (total, planes - 1), (total, planes - 1), (2 + planes,), (2 + planes,), (2, planes), (2, 2), (2,),
        (4,), (5,), (1,), (planes,), (planes,), (planes,), (planes,), (2, 2),
    ]
    results = pl.pallas_call(
        partial(backward_kernel, planes),
        out_shape=[jax.ShapeDtypeStruct(*shape) for shape in shapes],
        in_specs=[hbm] * 17 + [vmem] * 2,
        out_specs=[hbm] * len(shapes),
        scratch_shapes=[pltpu.VMEM(*shape) for shape in scratch] + [sem(shape) for shape in sems],
        compiler_params=pltpu.CompilerParams(
            collective_id=1, has_side_effects=True, vmem_limit_bytes=62 * 2**20
        ),
        name="backward_scatter",
    )(*weights, *saved, mask, gain)
    return results[:6], results[6], results[7]


def shards(
    inputs,
    lengths,
    dealing,
    w_query,
    w_key,
    w_value,
    b_query,
    b_value,
    w_out,
    b_out,
    gain_first,
    shift_first,
    w_up,
    b_up,
    w_down,
    b_down,
    gain_second,
    shift_second,
    cotangent,
):
    group_index = lax.axis_index("dp")
    tensor_index = lax.axis_index("tensor")
    ordered = jnp.take(inputs, dealing, axis=0)
    arrived = lax.all_to_all(ordered, "dp", split_axis=0, concat_axis=2, tiled=True)
    features = arrived.shape[3]
    half_rows = arrived.shape[2]
    own_rows = arrived.reshape(half_rows, features)
    seq_len = half_rows * lax.axis_size("tensor")
    length = lengths[dealing[group_index]]
    key_valid = jnp.arange(seq_len) < length
    head_cols = w_query.shape[1]
    up_cols = w_up.shape[1]
    query_bias = lax.dynamic_slice_in_dim(b_query, tensor_index * head_cols, head_cols)
    value_bias = lax.dynamic_slice_in_dim(b_value, tensor_index * head_cols, head_cols)
    up_bias = lax.dynamic_slice_in_dim(b_up, tensor_index * up_cols, up_cols)
    vectors = jnp.concatenate(
        (query_bias, value_bias, b_out, gain_first, shift_first, up_bias, b_down, gain_second, shift_second)
    ).reshape(1, -1)
    mask = jnp.broadcast_to(key_valid.astype(jnp.float32), (8, seq_len))
    weights, saved = forward(
        [w_query, w_key, w_value, w_out.T, w_up, w_down.T],
        own_rows, cotangent.reshape(half_rows, features), mask, vectors,
    )
    (
        full_in, _, qkv, mixed_heads, normed_full, inverse_full, full_hidden, active, slope,
        result, full_grad_down, second_full, second_sums,
    ) = saved
    output = result.reshape(cotangent.shape)
    grads, small_total, grad_own = backward(
        weights,
        [
            full_in, qkv, mixed_heads, normed_full, inverse_full, full_hidden, active, slope,
            full_grad_down, second_full, second_sums,
        ],
        mask, gain_first.reshape(1, -1),
    )
    grad_sent = grad_own.reshape(1, 1, half_rows, features)
    returned = lax.all_to_all(grad_sent, "dp", split_axis=2, concat_axis=0, tiled=True)
    grad_inputs = jnp.zeros_like(returned).at[dealing].set(returned)
    weight_sums = (grads[0], grads[1], grads[2], grads[3].T, grads[4], grads[5].T)
    up_rows = b_up.shape[0] // features
    small_sums = (
        small_total[0], small_total[1], small_total[2], small_total[3 : 3 + up_rows].reshape(-1),
        small_total[7], small_total[8], small_total[9], small_total[10], small_total[11],
    )
    return (
        output,
        grad_inputs,
        weight_sums[0],
        weight_sums[1],
        weight_sums[2],
        small_sums[0],
        small_sums[1],
        weight_sums[3],
        small_sums[2],
        small_sums[5],
        small_sums[6],
        weight_sums[4],
        small_sums[3],
        weight_sums[5],
        small_sums[4],
        small_sums[7],
        small_sums[8],
    )


def solution(mesh):
    in_specs = (
        P(None, "tensor", "dp", None),
        P(),
        P(),
        P("dp", "tensor"),
        P("dp", "tensor"),
        P("dp", "tensor"),
        P(),
        P(),
        P("tensor", "dp"),
        P(),
        P(),
        P(),
        P("dp", "tensor"),
        P(),
        P("tensor", "dp"),
        P(),
        P(),
        P(),
        P("dp", "tensor", None),
    )
    out_specs = (
        P("dp", "tensor", None),
        P(None, "tensor", "dp", None),
        P("dp", "tensor"),
        P("dp", "tensor"),
        P("dp", "tensor"),
        P(),
        P(),
        P("tensor", "dp"),
        P(),
        P(),
        P(),
        P("dp", "tensor"),
        P(),
        P("tensor", "dp"),
        P(),
        P(),
        P(),
    )
    return jax.shard_map(shards, mesh=mesh, in_specs=in_specs, out_specs=out_specs, check_vma=False)
```

```python
from functools import partial

import jax
import jax.numpy as jnp
from jax import lax
from jax.experimental import pallas as pl
from jax.experimental.pallas import tpu as pltpu
from jax.sharding import PartitionSpec as P

HEAD_DIM = 128


EPSILON = 1e-05
MASKED = -1e30


def norm_forward(values, scale_gain, bias_shift):
    center = values - jnp.mean(values, axis=-1, keepdims=True)
    inverse = lax.rsqrt(jnp.mean(center * center, axis=-1, keepdims=True) + EPSILON)
    normed = center * inverse
    return (normed * scale_gain + bias_shift, normed, inverse)


def contract_rows(left, right):
    return lax.dot_general(
        left, right, (((0,), (0,)), ((), ())), preferred_element_type=jnp.float32
    )


def contract_cols(left, right):
    return lax.dot_general(
        left, right, (((1,), (1,)), ((), ())), preferred_element_type=jnp.float32
    )


MESH = pl.DeviceIdType.MESH
TILE = 1024
SLOPE = 0.7978845608028654


def place():
    dp, tensor = lax.axis_index("dp"), lax.axis_index("tensor")
    return dp // 4, (dp // 2) % 2, dp % 2, tensor


def device_of(plane, across, core, tensor):
    return ((plane * 2 + across) * 2 + core, tensor)


def enter(peers):
    barrier = pltpu.get_barrier_semaphore()
    for peer in peers:
        pl.semaphore_signal(barrier, inc=1, device_id=peer, device_id_type=MESH)
    pl.semaphore_wait(barrier, len(peers))


LAG, EARLY, X_FIRST, DEALT = 3, 3, (7,), 7


def rest_shape(count):
    whole = count // 16 * 16
    rest = count - whole
    padded = 4 if rest <= 4 else 8 if rest <= 8 else 16
    return whole, rest, padded, 16 // padded

def gather_tiles(widths):
    return [(i, start) for i, width in enumerate(widths) for start in range(0, width, TILE)]


def forward_kernel(planes, widths, *refs):
    count = len(widths)
    shard_refs = refs[:count]
    deal_refs = refs[count : count + 2]
    cot_ref, mask_ref, vec_ref = refs[count + 2 : count + 5]
    outs = refs[count + 5 :]
    full_refs = outs[:count]
    (
        x_full, cot_full, qkv_out, mixed_out, normed_out, inverse_out, hidden_out, active_out, slope_out,
        result_out, down_out, second_out, sums_out,
    ) = outs[count : count + 13]
    (
        w_buf, x_buf, qkv_buf, mixed_buf, attn_acc, attn_land, send_buf, hidden_buf, active_buf, slope_buf,
        down_acc, down_land, inverse_buf, result_buf, sums_buf, whole_land, rest_land,
        plane_send, plane_recv, x_send, x_recv, core_send, core_recv, w_sem, in_send, in_recv,
        attn_send, attn_recv, down_send, down_recv, load_sem, store_sem,
        deal_send, deal_recv,
    ) = outs[count + 13 :]
    plane, across, core, tensor = place()
    far = [lax.rem(plane + k, planes) for k in range(planes)]
    x_peer = device_of(plane, 1 - across, core, tensor)
    core_peer = device_of(plane, across, 1 - core, tensor)
    y_peer = device_of(plane, across, core, 1 - tensor)
    plane_peers = [device_of(far[k], across, core, tensor) for k in range(planes)]
    tiles = gather_tiles(widths)
    half, features = cot_ref.shape
    tokens = 2 * half
    block = features // planes
    head_cols = mixed_buf.shape[1]
    factor = HEAD_DIM ** (-0.5)
    own_rows = pl.ds(pl.multiple_of(tensor * half, half), half)

    vec_at = {}
    at = 0
    for key, size in (
        ("b_query", head_cols), ("b_value", head_cols), ("b_out", features), ("gain_first", features),
        ("shift_first", features), ("b_up", widths[4]), ("b_down", features), ("gain_second", features),
        ("shift_second", features),
    ):
        vec_at[key] = at
        at += size

    def vector(key, start, size):
        return vec_ref[:, pl.ds(vec_at[key] + start, size)]

    first_down = len(tiles) - widths[5] // TILE
    units = [(c, j) for c in range(first_down) for j in range(planes)]
    units += [(c, j) for j in range(planes) for c in range(first_down, len(tiles))]
    lag, early = LAG, EARLY
    relayed = planes == 4
    across_first = X_FIRST if relayed else ()
    low_side = plane < planes // 2
    origins = [
        jnp.where(low_side, lax.rem(plane + j, planes), lax.rem(plane + planes - j, planes)) for j in range(planes)
    ]

    def view(c, *where):
        i, start = tiles[c]
        return full_refs[i].at[(*where, slice(None), pl.ds(start, TILE))]

    def own(c):
        i, start = tiles[c]
        return shard_refs[i].at[:, pl.ds(start, TILE)]

    def own_load(c):
        return pltpu.make_async_copy(own(c), w_buf.at[1, c // 4, (c // 2) % 2, c % 2], plane_recv.at[c, 0])

    def own_store(c):
        return pltpu.make_async_copy(
            w_buf.at[1, c // 4, (c // 2) % 2, c % 2], view(c, plane, across, core), plane_recv.at[c, 0]
        )

    def both(c):
        return slice(None) if c in across_first else across

    def z_copy(c, origin, target, send):
        part = view(c, origin, both(c), core)
        if c not in across_first and send > 0:
            part = own(c)
        place_there = jnp.where(
            target < planes // 2, lax.rem(origin + planes - target, planes), lax.rem(target + planes - origin, planes)
        )
        return pltpu.make_async_remote_copy(
            part, view(c, origin, both(c), core), plane_send.at[c, send], plane_recv.at[c, place_there],
            device_id=device_of(target, across, core, tensor), device_id_type=MESH,
        )

    def z_each(c, offsets, act):
        for k in offsets:
            copy = z_copy(c, plane, far[k], k)
            if relayed and k != 2:
                @pl.when((plane < planes - 1) if k == 1 else (plane > 0))
                def _():
                    act(copy)
            else:
                act(copy)

    def z_relay(c, act):
        if relayed:
            @pl.when(jnp.logical_and(plane > 0, plane < planes - 1))
            def _():
                act(z_copy(c, origins[2], jnp.where(plane == 1, 0, planes - 1), 0))

    def z_arrival(c, j):
        part = view(c, origins[j], both(c), core)
        return pltpu.make_async_remote_copy(
            part, part, plane_send.at[c, j], plane_recv.at[c, j], device_id=x_peer, device_id_type=MESH
        )

    def x_copy(c, j, side):
        part = view(c, origins[j], side, core)
        return pltpu.make_async_remote_copy(
            own(c) if j == 0 else part, part, x_send.at[c, j], x_recv.at[c, j], device_id=x_peer,
            device_id_type=MESH,
        )

    def unit_core(u, side):
        c, j = units[u]
        part = view(c, origins[j], slice(None), side)
        return pltpu.make_async_remote_copy(
            part, part, core_send.at[c, j], core_recv.at[c, j], device_id=core_peer, device_id_type=MESH
        )

    z_items = [(planes * max(c - early, 0), c, range(1, planes)) for c in range(first_down)]
    near_by = [k for k in range(1, planes) if k in (1, planes - 1)]
    at = planes * (first_down - early)
    for offsets in (near_by, [k for k in range(1, planes) if k not in near_by]):
        for c in range(first_down, len(tiles)):
            z_items.append((at, c, offsets))
            at += 2
    z_items.sort(key=lambda item: item[0])

    def z_begin(n):
        for when, c, offsets in z_items:
            if when == n:
                if c in across_first:
                    x_copy(c, 0, 1 - across).wait_recv()
                z_each(c, offsets, lambda copy: copy.start())

    def pump(n):
        if n < len(units):
            if n > 0:
                z_begin(n)
            c, j = units[n]
            if j > 0:
                z_arrival(c, j).wait_recv()
            if j == 2:
                z_relay(c, lambda copy: copy.start())
            if c not in across_first:
                x_copy(c, j, across).start()
        if n >= lag:
            c, j = units[n - lag]
            if c not in across_first:
                x_copy(c, j, 1 - across).wait_recv()
            unit_core(n - lag, core).start()

    def landed(u):
        unit_core(u, 1 - core).wait_recv()

    def tile_copies(c):
        i, start = tiles[c]
        return [
            pltpu.make_async_copy(
                full_refs[i].at[p, :, :, :, pl.ds(start, TILE)], w_buf.at[c % 2, p], w_sem.at[c % 2, p]
            )
            for p in range(planes)
        ]

    def load_tile(c):
        for u, (tile, _) in enumerate(units):
            if tile == c:
                landed(u)
        for copy in tile_copies(c):
            copy.start()

    def wait_tile(c):
        for copy in tile_copies(c):
            copy.wait()

    def down_copy(k, j):
        c = first_down + j
        return pltpu.make_async_copy(
            view(c, origins[k], slice(None), slice(None)), w_buf.at[k % 2, j], w_sem.at[k % 2, j]
        )

    down_parts = widths[5] // TILE

    def load_down(k):
        for j in range(down_parts):
            landed(units.index((first_down + j, k)))
            down_copy(k, j).start()

    def flat(value):
        return value.reshape(-1, value.shape[-1])

    groups = planes * 4
    index = (plane * 2 + across) * 2 + core
    group = half // groups
    whole, rest, padded, chunks = rest_shape(group)
    rest_width = features // chunks
    deal_parts = ((0, whole_land), (1, rest_land)) if whole else ((1, rest_land),)

    def deal(which, land, k):
        target = lax.rem(index + k, groups)
        return pltpu.make_async_remote_copy(
            deal_refs[which].at[target], land.at[index], deal_send.at[which, k], deal_recv.at[which, k],
            device_id=(target, tensor), device_id_type=MESH,
        )

    def deal_own(which, land):
        return pltpu.make_async_copy(deal_refs[which].at[index], land.at[index], deal_recv.at[which, 0])

    def dealt():
        for which, land in deal_parts:
            deal_own(which, land).wait()
            for k in range(1, groups):
                deal(which, land, k).wait_recv()
        for s in range(groups):
            start = s * group
            if whole:
                attn_acc[start : start + whole, :] = whole_land[s].astype(jnp.float32)
            tail = rest_land[s].astype(jnp.float32)
            for q in range(chunks):
                attn_acc[start + whole : start + group, q * rest_width : (q + 1) * rest_width] = tail[
                    q * padded : q * padded + rest, :
                ]

        @pl.loop(0, half // 16)
        def _(i):
            rows = pl.ds(pl.multiple_of(tensor * half + i * 16, 16), 16)
            x_buf[rows, :] = attn_acc[pl.ds(pl.multiple_of(i * 16, 16), 16), :].astype(jnp.bfloat16)

        exchange(0, x_buf.at[own_rows], x_buf).start()

    def load_x():
        exchange(0, x_buf.at[own_rows], x_buf).wait_recv()
        store(11, x_buf, x_full).start()

    def cot_load():
        other_rows = pl.ds(pl.multiple_of((1 - tensor) * half, half), half)
        return [
            pltpu.make_async_copy(cot_ref, x_buf.at[own_rows], load_sem.at[1]),
            pltpu.make_async_copy(cot_full.at[other_rows], x_buf.at[other_rows], load_sem.at[2]),
        ]

    def exchange(which, source, target):
        return pltpu.make_async_remote_copy(
            source, target.at[own_rows], in_send.at[which], in_recv.at[which],
            device_id=y_peer, device_id_type=MESH,
        )

    def start_cot():
        exchange(1, cot_ref, cot_full).start()

    def project(c, bias):
        wait_tile(c)

        @pl.loop(0, TILE // 512)
        def _(n):
            cols = pl.ds(pl.multiple_of(n * 512, 512), 512)
            value = jnp.dot(
                x_buf[...], flat(w_buf[c % 2, :, :, :, :, cols]), preferred_element_type=jnp.float32
            )
            if bias is not None:
                value += vec_ref[:, pl.ds(pl.multiple_of(vec_at[bias] + n * 512, 128), 512)]
            qkv_buf[:, pl.ds(pl.multiple_of(c * TILE + n * 512, 512), 512)] = value.astype(jnp.bfloat16)

    def attend(first, last):
        @pl.loop(first, last)
        def _(h):
            def cols(which):
                return pl.ds(pl.multiple_of(which * head_cols + h * HEAD_DIM, HEAD_DIM), HEAD_DIM)

            scores = contract_cols(qkv_buf[:, cols(0)], qkv_buf[:, cols(1)]) * factor
            scores = jnp.where(mask_ref[0:1, :] > 0.0, scores, MASKED)
            expanded = jnp.exp(scores - jnp.max(scores, axis=1, keepdims=True))
            weight = (expanded / jnp.sum(expanded, axis=1, keepdims=True)).astype(jnp.bfloat16)
            mixed_buf[:, cols(0)] = jnp.dot(
                weight, qkv_buf[:, cols(2)], preferred_element_type=jnp.float32
            ).astype(jnp.bfloat16)

    def block_cols(p):
        return pl.ds(pl.multiple_of(p * block, block), block)

    def attn_share(p):
        return pltpu.make_async_remote_copy(
            send_buf.at[:, block_cols(p)], attn_land.at[:, block_cols(p)], attn_send.at[p], attn_recv.at[p],
            device_id=y_peer, device_id_type=MESH,
        )

    def project_out():
        wait_tile(3)

        @pl.loop(0, planes)
        def _(p):
            value = contract_cols(mixed_buf[...], flat(w_buf[1, p]))
            attn_acc[:, block_cols(p)] = value
            send_buf[:, block_cols(p)] = value.astype(jnp.bfloat16)
            attn_share(p).start()

    def first_norm():
        @pl.loop(0, planes)
        def _(p):
            attn_share(p).wait()

        @pl.loop(0, tokens // 16)
        def _(i):
            rows = pl.ds(pl.multiple_of(i * 16, 16), 16)
            value = (
                x_buf[rows, :].astype(jnp.float32)
                + (attn_acc[rows, :] + attn_land[rows, :].astype(jnp.float32))
                + vector("b_out", 0, features)
            )
            hidden, normed, inverse = norm_forward(
                value, vector("gain_first", 0, features), vector("shift_first", 0, features)
            )
            attn_acc[rows, :] = normed
            inverse_buf[rows, :] = jnp.broadcast_to(inverse, (16, 128))
            hidden_buf[rows, :] = hidden.astype(jnp.bfloat16)

        store(0, attn_acc, normed_out).start()
        store(1, inverse_buf, inverse_out).start()
        store(2, hidden_buf, hidden_out).start()
        exchange(1, cot_ref, cot_full).wait_recv()
        store(11, x_buf, x_full).wait()
        exchange(0, x_buf.at[own_rows], x_buf).wait_send()
        for copy in cot_load():
            copy.start()

    def store(which, source, target):
        return pltpu.make_async_copy(source, target, store_sem.at[which])

    def slope_store(j):
        return pltpu.make_async_copy(
            slope_buf.at[j % 2], slope_out.at[:, pl.ds(j * TILE, TILE)], store_sem.at[5 + j % 2]
        )

    def raise_up(j):
        c = 4 + j
        wait_tile(c)
        if j >= 2:
            slope_store(j - 2).wait()

        @pl.loop(0, TILE // 256)
        def _(n):
            cols = pl.ds(pl.multiple_of(n * 256, 256), 256)
            value = jnp.dot(
                hidden_buf[...], flat(w_buf[c % 2, :, :, :, :, cols]), preferred_element_type=jnp.float32
            )
            value += vec_ref[:, pl.ds(pl.multiple_of(vec_at["b_up"] + j * TILE + n * 256, 128), 256)]
            square = value * value
            bend = jnp.tanh(SLOPE * value * (1.0 + 0.044715 * square))
            rise = 0.5 * (1.0 + bend)
            active_buf[:, pl.ds(pl.multiple_of(j * TILE + n * 256, 256), 256)] = (value * rise).astype(
                jnp.bfloat16
            )
            slope_buf[j % 2, :, cols] = (
                rise + 0.5 * value * (1.0 - bend * bend) * (SLOPE * (1.0 + 3.0 * 0.044715 * square))
            ).astype(jnp.bfloat16)

        slope_store(j).start()

    def down_share(k):
        cols = block_cols(origins[k])
        return pltpu.make_async_remote_copy(
            send_buf.at[:, cols], down_land.at[:, cols], down_send.at[k], down_recv.at[k],
            device_id=y_peer, device_id_type=MESH,
        )

    def lower(k):
        cols = block_cols(origins[k])
        value = None
        for j in range(down_parts):
            down_copy(k, j).wait()
            part = contract_cols(active_buf[:, j * TILE : (j + 1) * TILE], flat(w_buf[k % 2, j]))
            value = part if value is None else value + part
        down_acc[:, cols] = value
        send_buf[:, cols] = value.astype(jnp.bfloat16)
        down_share(k).start()

    def second_norm():
        for k in range(planes):
            down_share(k).wait()
        for copy in cot_load():
            copy.wait()
        store(2, hidden_buf, hidden_out).wait()
        sums_buf[...] = jnp.zeros_like(sums_buf)
        gain = vector("gain_second", 0, features)

        def rows_of(which, i):
            base = tensor if which == 0 else 1 - tensor
            return pl.ds(pl.multiple_of(base * half + i * 16, 16), 16)

        for which in (0, 1):
            @pl.loop(0, half // 16)
            def _(i):
                rows = rows_of(which, i)
                hidden = attn_acc[rows, :] * vector("gain_first", 0, features) + vector(
                    "shift_first", 0, features
                )
                value = (
                    hidden
                    + (down_acc[rows, :] + down_land[rows, :].astype(jnp.float32))
                    + vector("b_down", 0, features)
                )
                result, normed, inverse = norm_forward(value, gain, vector("shift_second", 0, features))
                grad_out = x_buf[rows, :].astype(jnp.float32)
                scaled = grad_out * gain
                grad = inverse * (
                    scaled
                    - jnp.mean(scaled, axis=-1, keepdims=True)
                    - normed * jnp.mean(scaled * normed, axis=-1, keepdims=True)
                )
                down_acc[rows, :] = grad
                low = grad.astype(jnp.bfloat16)
                hidden_buf[rows, :] = low
                if which == 0:
                    result_buf[pl.ds(pl.multiple_of(i * 16, 16), 16), :] = result.astype(jnp.bfloat16)
                    sums_buf[0] += grad_out * normed
                    sums_buf[1] += grad_out
                    sums_buf[2] += low.astype(jnp.float32)

        for which, source, target in (
            (2, hidden_buf, down_out), (3, down_acc, second_out), (4, result_buf, result_out), (9, sums_buf, sums_out),
        ):
            store(which, source, target).start()

    for c in range(len(tiles)):
        own_load(c).start()
    for which, land in deal_parts:
        deal_own(which, land).start()
    enter([(lax.rem(index + k, groups), tensor) for k in range(1, groups)] + [y_peer])
    for k in range(1, groups):
        for which, land in deal_parts:
            deal(which, land, k).start()
    for c in across_first:
        x_copy(c, 0, across).start()
    z_begin(0)
    for c in range(len(tiles)):
        own_load(c).wait()
        own_store(c).start()
    for c in range(len(tiles)):
        own_store(c).wait()

    plan = {}

    def at_slot(n, step, *args):
        plan.setdefault(n, []).append((step, args))

    def ready(c):
        return planes * (c + 1) + lag

    heads = head_cols // HEAD_DIM
    at_slot(DEALT, dealt)
    at_slot(ready(0), load_tile, 0)
    at_slot(ready(1), load_tile, 1)
    at_slot(ready(2) - 2, load_x)
    at_slot(ready(2) - 2, project, 0, "b_query")
    at_slot(ready(2) - 2, start_cot)
    at_slot(ready(2) - 1, project, 1, None)
    at_slot(ready(2), load_tile, 2)
    at_slot(ready(2) + 1, project, 2, "b_value")
    begin = ready(2) + 2
    for q in range(4):
        at_slot(begin + q, attend, q * heads // 4, (q + 1) * heads // 4)
    at_slot(begin + 3, load_tile, 3)
    at_slot(begin + 4, project_out)
    norm_slot = begin + 4 + 10 * planes // 4
    at_slot(norm_slot, first_norm)
    at_slot(max(ready(4), begin), load_tile, 4)
    at_slot(max(ready(5), begin + 4), load_tile, 5)
    for j in range(4):
        slot = max(norm_slot + 1 + j, ready(4 + j) + 1)
        at_slot(slot, raise_up, j)
        if j >= 2:
            plan.setdefault(max(norm_slot + 1 + j - 2, ready(4 + j)), []).append((load_tile, (4 + j,)))
    for k in range(planes):
        slot = planes * first_down + down_parts * (k + 1) + lag
        at_slot(slot, load_down, k)
        at_slot(slot + 1, lower, k)
    last = max(max(plan), len(units) + lag - 1)
    for n in range(last + 1):
        if n < len(units) + lag:
            pump(n)
        for step, args in plan.get(n, []):
            step(*args)
        if n == begin + 3:
            store(7, qkv_buf, qkv_out).start()
            store(8, mixed_buf, mixed_out).start()
    store(10, active_buf, active_out).start()
    second_norm()
    for which, source, target in (
        (0, attn_acc, normed_out), (1, inverse_buf, inverse_out), (2, hidden_buf, down_out),
        (3, down_acc, second_out), (4, result_buf, result_out), (7, qkv_buf, qkv_out),
        (8, mixed_buf, mixed_out), (9, sums_buf, sums_out), (10, active_buf, active_out),
    ):
        store(which, source, target).wait()
    for j in range(2, 4):
        slope_store(j).wait()
    exchange(1, cot_ref, cot_full).wait_send()
    for which, land in deal_parts:
        for k in range(1, groups):
            deal(which, land, k).wait_send()
    for c in range(len(tiles)):
        z_each(c, range(1, planes), lambda copy: copy.wait_send())
        z_relay(c, lambda copy: copy.wait_send())
    for u, (c, j) in enumerate(units):
        if c not in across_first or j == 0:
            x_copy(c, j, across).wait_send()
        unit_core(u, core).wait_send()


def forward(shard_list, dealt_rows, cot, mask, vectors):
    planes = lax.axis_size("dp") // 4
    widths = [shard.shape[1] for shard in shard_list]
    total = sum(width // TILE for width in widths)
    half, features = cot.shape
    tokens, rows = 2 * half, shard_list[0].shape[0]
    head_cols, up_cols = widths[0], widths[4]
    groups = planes * 4
    whole, rest, padded, chunks = rest_shape(half // groups)
    whole_rows = dealt_rows[:, : max(whole, 16)] if whole else jnp.zeros((groups, 16, 128), jnp.bfloat16)
    rest_rows = jnp.pad(dealt_rows[:, whole:], ((0, 0), (0, padded - rest), (0, 0)))
    rest_rows = rest_rows.reshape(groups, padded, chunks, features // chunks)
    rest_rows = rest_rows.transpose(0, 2, 1, 3).reshape(groups, 16, features // chunks)
    sem, low, high = pltpu.SemaphoreType.DMA, jnp.bfloat16, jnp.float32
    hbm, vmem = pl.BlockSpec(memory_space=pl.ANY), pl.BlockSpec(memory_space=pltpu.VMEM)
    shapes = [((planes, 2, 2, *shard.shape), low) for shard in shard_list] + [
        ((tokens, features), low), ((tokens, features), low), ((tokens, 3 * head_cols), low),
        ((tokens, head_cols), low), ((tokens, features), high), ((tokens, 128), high),
        ((tokens, features), low), ((tokens, up_cols), low), ((tokens, up_cols), low),
        ((half, features), low), ((tokens, features), low), ((tokens, features), high),
        ((3, 16, features), high),
    ]
    results = pl.pallas_call(
        partial(forward_kernel, planes, widths),
        out_shape=[jax.ShapeDtypeStruct(*shape) for shape in shapes],
        in_specs=[hbm] * (len(shard_list) + 3) + [vmem] * 2,
        out_specs=[hbm] * len(shapes),
        scratch_shapes=[
            pltpu.VMEM((2, planes, 2, 2, rows, TILE), low),
            pltpu.VMEM((tokens, features), low),
            pltpu.VMEM((tokens, 3 * head_cols), low),
            pltpu.VMEM((tokens, head_cols), low),
            pltpu.VMEM((tokens, features), high),
            pltpu.VMEM((tokens, features), low),
            pltpu.VMEM((tokens, features), low),
            pltpu.VMEM((tokens, features), low),
            pltpu.VMEM((tokens, up_cols), low),
            pltpu.VMEM((2, tokens, TILE), low),
            pltpu.VMEM((tokens, features), high),
            pltpu.VMEM((tokens, features), low),
            pltpu.VMEM((tokens, 128), high),
            pltpu.VMEM((half, features), low),
            pltpu.VMEM((3, 16, features), high),
            pltpu.VMEM(whole_rows.shape, low),
            pltpu.VMEM(rest_rows.shape, low),
            *[sem((total, planes))] * 6,
            sem((2, max(planes, 4))), sem((2,)), sem((2,)),
            sem((planes,)), sem((planes,)), sem((planes,)), sem((planes,)), sem((3,)), sem((12,)),
            sem((2, groups)), sem((2, groups)),
        ],
        compiler_params=pltpu.CompilerParams(
            collective_id=0, has_side_effects=True, vmem_limit_bytes=62 * 2**20
        ),
        name="forward_gather",
    )(*shard_list, whole_rows, rest_rows, cot, mask, vectors)
    return results[: len(shard_list)], results[len(shard_list) :]


JOB = 512


def backward_kernel(planes, *refs):
    (
        query_w, key_w, value_w, out_w, up_w, down_w,
        x_in, qkv_in, mixed_in, normed_in, inverse_in, hidden_in, active_in, slope_in, down_in, second_in,
        sums_in, mask_ref, gain_ref,
    ) = refs[:19]
    (
        grad_query, grad_key, grad_value, grad_out_w, grad_up, grad_down, small_out, whole_out, rest_out,
        left_own, left_far, active_far, rise_own, rise_far, mixed_far, qkv_own, qkv_far,
    ) = refs[19:36]
    (
        left_buf, right_buf, stage, x_land, plane_land, out_buf, tile_buf, wide_buf, low_buf, rise_buf,
        slope_buf, acc_buf, hidden_land, send_buf, qkv_buf, turn_buf, input_land, row_buf, inverse_buf,
        sums_buf, small_land, whole_buf, rest_buf, rest_wide,
        left_sem, right_sem, out_sem, core_send, core_recv, left_send, left_recv, x_send, x_recv,
        plane_send, plane_recv, small_send, small_recv, tile_sem, wide_sem, slope_sem, load_sem, store_sem,
        turn_sem, hidden_send, hidden_recv, input_send, input_recv, row_sem, back_send, back_recv,
    ) = refs[36:]
    plane, across, core, tensor = place()
    far = [lax.rem(plane + k, planes) for k in range(planes)]
    x_peer = device_of(plane, 1 - across, core, tensor)
    core_peer = device_of(plane, across, 1 - core, tensor)
    y_peer = device_of(plane, across, core, 1 - tensor)
    plane_peers = [device_of(far[k], across, core, tensor) for k in range(planes)]
    tokens, features = low_buf.shape
    half = tokens // 2
    head_cols = mixed_in.shape[1]
    heads = head_cols // HEAD_DIM
    up_cols = active_in.shape[1]
    block = features // planes
    factor = HEAD_DIM ** (-0.5)
    slots = x_land.shape[0]
    thin = tile_buf.shape[-1]

    jobs = [(0, active_in, active_far, s, grad_down, s) for s in range(0, up_cols, JOB)]
    jobs += [(1, rise_own, rise_far, s, grad_up, s) for s in range(0, up_cols, JOB)]
    jobs += [(2, mixed_in, mixed_far, s, grad_out_w, s) for s in range(0, head_cols, JOB)]
    for which, result in enumerate((grad_query, grad_key, grad_value)):
        jobs += [
            (3, qkv_own, qkv_far, which * head_cols + s, result, s) for s in range(0, head_cols, JOB)
        ]
    total = len(jobs)
    up_first, out_first, qkv_first = (
        [job[0] for job in jobs].index(a) for a in (1, 2, 3)
    )

    def local(source, target, sem):
        return pltpu.make_async_copy(source, target, sem)

    def remote(source, target, send, recv, peer):
        return pltpu.make_async_remote_copy(
            source, target, send, recv, device_id=peer, device_id_type=MESH
        )

    def left_out(a):
        return remote(
            turn_buf.at[:, :, 1 - core], left_far.at[a], left_send.at[a], left_recv.at[a], core_peer
        )

    def left_keep(a):
        return local(turn_buf.at[:, :, core], left_own.at[a], turn_sem.at[0])

    kept = set()

    def left_kept(a):
        if a not in kept:
            kept.add(a)
            left_keep(a).wait()

    def turn(a, source):
        if a > 0:
            left_out(a - 1).wait_send()
            left_kept(a - 1)

        @pl.loop(0, planes)
        def _(p):
            cols = pl.ds(pl.multiple_of(p * block, block), block)
            turn_buf[p] = source[:, cols].T.reshape(turn_buf.shape[1:])

        left_keep(a).start()
        left_out(a).start()

    def right_out(c, source=None):
        _, own, other, start, _, _ = jobs[c]
        cols = pl.ds(start, JOB)
        return remote(
            (own if source is None else source).at[:, cols], other.at[:, cols], core_send.at[c],
            core_recv.at[c], core_peer,
        )

    def left_load(a):
        slot = a % 2
        copies = []
        for side in range(2):
            copies.append(
                local(left_own.at[a, :, side], left_buf.at[slot, side, :, :, pl.ds(0, tokens)], left_sem.at[slot, 0, side])
            )
            copies.append(
                local(left_far.at[a, :, side], left_buf.at[slot, side, :, :, pl.ds(tokens, tokens)], left_sem.at[slot, 1, side])
            )
        return copies

    def right_load(c):
        _, own, other, start, _, _ = jobs[c]
        slot, cols = c % 2, pl.ds(start, JOB)
        return [
            local(own.at[:, cols], right_buf.at[slot, pl.ds(0, tokens)], right_sem.at[slot, 0]),
            local(other.at[:, cols], right_buf.at[slot, pl.ds(tokens, tokens)], right_sem.at[slot, 1]),
        ]

    def x_out(c):
        return remote(
            stage.at[c % 3, 1 - across], x_land.at[c % slots], x_send.at[c], x_recv.at[c], x_peer
        )

    def plane_out(c, k):
        return remote(
            x_land.at[c % slots, far[k]], plane_land.at[c % slots, k - 1], plane_send.at[c, k - 1],
            plane_recv.at[c, k - 1], plane_peers[k],
        )

    def grad_out(c):
        _, _, _, _, result, start = jobs[c]
        return local(out_buf.at[c % 2], result.at[:, pl.ds(start, JOB)], out_sem.at[c % 2])

    def new_left(c):
        return c == 0 or jobs[c - 1][0] != jobs[c][0]

    def fetch(c):
        a = jobs[c][0]
        if new_left(c):
            left_kept(a)
            left_out(a).wait_recv()
            for copy in left_load(a):
                copy.start()
        right_out(c).wait_recv()
        for copy in right_load(c):
            copy.start()

    def multiply(c):
        a = jobs[c][0]
        if new_left(c):
            for copy in left_load(a):
                copy.wait()
        for copy in right_load(c):
            copy.wait()
        if c + 1 < total:
            fetch(c + 1)
        if c >= 3:
            x_out(c - 3).wait_send()

        @pl.loop(0, JOB // 256)
        def _(n):
            cols = pl.ds(pl.multiple_of(n * 256, 256), 256)
            left = left_buf[a % 2]
            result = jnp.dot(
                left.reshape(-1, left.shape[-1]), right_buf[c % 2, :, cols],
                preferred_element_type=jnp.float32,
            ).astype(jnp.bfloat16)
            stage[c % 3, :, :, :, cols] = result.reshape(*left.shape[:-1], 256)

        x_out(c).start()

    def fold(c):
        x_out(c).wait_recv()
        slot = c % slots

        @pl.loop(0, planes)
        def _(p):
            x_land[slot, p] = (
                x_land[slot, p].astype(jnp.float32) + stage[c % 3, across, p].astype(jnp.float32)
            ).astype(jnp.bfloat16)

        for k in range(1, planes):
            plane_out(c, k).start()

    def finish(c):
        for k in range(1, planes):
            plane_out(c, k).wait()
        if c >= 2:
            grad_out(c - 2).wait()
        value = x_land[c % slots, plane].astype(jnp.float32)
        for k in range(1, planes):
            value += plane_land[c % slots, k - 1].astype(jnp.float32)
        out_buf[c % 2] = value
        grad_out(c).start()

    def small_copy(step, peer, slot):
        return remote(
            small_land.at[0], small_land.at[slot], small_send.at[step], small_recv.at[step], peer
        )

    def small_begin(step):
        if step < 3:
            small_copy(step, (core_peer, x_peer, y_peer)[step], 1 + step).start()
        else:
            for k in range(1, planes):
                small_copy(2 + k, plane_peers[k], 3 + k).start()

    def small_end(step):
        if step < 3:
            small_copy(step, core_peer, 1 + step).wait()
            small_land[0] = small_land[0] + small_land[1 + step]
        else:
            for k in range(1, planes):
                small_copy(2 + k, core_peer, 3 + k).wait()
            value = jnp.zeros(small_land.shape[1:], jnp.float32)
            for p in range(planes):
                back = lax.rem(plane + planes - p, planes)
                value += small_land[jnp.where(back == 0, 0, 3 + back)]
            small_land[1] = value
            local(small_land.at[1], small_out, load_sem.at[0]).start()

    def total_row(value):
        return jnp.sum(value, axis=0, keepdims=True)

    def tile_copy(weight, start, slot):
        return [
            local(weight.at[p, :, :, :, pl.ds(start, thin)], tile_buf.at[slot, p], tile_sem.at[slot, p])
            for p in range(planes)
        ]

    def slope_copy(start, slot):
        return local(slope_in.at[:, pl.ds(start, thin)], slope_buf.at[slot], slope_sem.at[slot])

    def flat(value):
        return value.reshape(-1, value.shape[-1])

    def rise_start(i):
        for copy in tile_copy(down_w, i * thin, i % 2):
            copy.start()
        slope_copy(i * thin, i % 2).start()

    def rise_store(g):
        cols = pl.ds(g * 2 * JOB, 2 * JOB)
        return local(rise_buf.at[:, cols], rise_own.at[:, cols], store_sem.at[g])

    def rise(g):
        per = 2 * JOB // thin
        for i in range(g * per, (g + 1) * per):
            for copy in tile_copy(down_w, i * thin, i % 2):
                copy.wait()
            slope_copy(i * thin, i % 2).wait()
            value = jnp.dot(low_buf[...], flat(tile_buf[i % 2]), preferred_element_type=jnp.float32)
            value = (value * slope_buf[i % 2].astype(jnp.float32)).astype(jnp.bfloat16)
            rise_buf[:, i * thin : (i + 1) * thin] = value
            if i + 2 < up_cols // thin:
                rise_start(i + 2)
            row = 3 + tensor * (up_cols // features) + (i * thin) // features
            col = (i * thin) % features
            small_land[0, pl.ds(row, 1), col : col + thin] = total_row(value.astype(jnp.float32))
        rise_store(g).start()
        for c in (up_first + 2 * g, up_first + 2 * g + 1):
            right_out(c, rise_buf).start()

    def block_cols(p):
        return pl.ds(pl.multiple_of(p * block, block), block)

    def wide_copy(p, side):
        return local(
            up_w.at[p, :, :, :, pl.ds(side * features, features)], wide_buf.at[side], wide_sem.at[side, 0]
        )

    def hidden_share(p):
        return remote(
            send_buf.at[:, block_cols(p)], hidden_land.at[:, block_cols(p)], hidden_send.at[p],
            hidden_recv.at[p], y_peer,
        )

    def hidden_start():
        for side in range(2):
            wide_copy(0, side).start()

    def hidden_back(first, last):
        @pl.loop(first, last)
        def _(p):
            value = None
            for side in range(2):
                wide_copy(p, side).wait()
                part = contract_cols(
                    rise_buf[:, side * features : (side + 1) * features], flat(wide_buf[side])
                )
                value = part if value is None else value + part

                @pl.when(p + 1 < planes)
                def _():
                    wide_copy(p + 1, side).start()

            acc_buf[:, block_cols(p)] = value
            send_buf[:, block_cols(p)] = value.astype(jnp.bfloat16)
            hidden_share(p).start()

    strip = row_buf.shape[2]

    def row_start(which, i):
        base = tensor if which == 0 else 1 - tensor
        return pl.multiple_of(base * half + i * strip, strip)

    def row_copies(which, i):
        rows = pl.ds(row_start(which, i), strip)
        slot = (which * (half // strip) + i) % 2
        return [
            local(normed_in.at[rows], row_buf.at[slot, 0], row_sem.at[slot, 0]),
            local(second_in.at[rows], row_buf.at[slot, 1], row_sem.at[slot, 1]),
        ]

    strips = [(which, i) for which in range(2) for i in range(half // strip)]

    def norm_start():
        for pair in strips[:2]:
            for copy in row_copies(*pair):
                copy.start()
        local(inverse_in, inverse_buf, load_sem.at[1]).start()

    def norm_back():
        @pl.loop(0, planes)
        def _(p):
            hidden_share(p).wait()

        local(inverse_in, inverse_buf, load_sem.at[1]).wait()
        sums_buf[...] = jnp.zeros_like(sums_buf)
        for at, (which, i) in enumerate(strips):
            for copy in row_copies(which, i):
                copy.wait()

            @pl.loop(0, strip // 16)
            def _(r):
                local_rows = pl.ds(pl.multiple_of(r * 16, 16), 16)
                rows = pl.ds(pl.multiple_of(row_start(which, i) + r * 16, 16), 16)
                normed = row_buf[at % 2, 0, local_rows, :]
                grad_hidden = row_buf[at % 2, 1, local_rows, :] + (
                    acc_buf[rows, :] + hidden_land[rows, :].astype(jnp.float32)
                )
                scaled = grad_hidden * gain_ref[...]
                grad = inverse_buf[rows, 0:1] * (
                    scaled
                    - jnp.mean(scaled, axis=-1, keepdims=True)
                    - normed * jnp.mean(scaled * normed, axis=-1, keepdims=True)
                )
                acc_buf[rows, :] = grad
                low = grad.astype(jnp.bfloat16)
                low_buf[rows, :] = low
                if which == 0:
                    sums_buf[0] += grad_hidden * normed
                    sums_buf[1] += grad_hidden
                    sums_buf[2] += low.astype(jnp.float32)

            if at + 2 < len(strips):
                for copy in row_copies(*strips[at + 2]):
                    copy.start()
        small_land[0, 8:9, :] = total_row(sums_buf[0])
        small_land[0, 9:10, :] = total_row(sums_buf[1])
        small_land[0, 2:3, :] = total_row(sums_buf[2])

    def mixed_start():
        for i in range(2):
            for copy in tile_copy(out_w, i * thin, i):
                copy.start()
        for g in range(up_cols // (2 * JOB)):
            for c in (up_first + 2 * g, up_first + 2 * g + 1):
                right_out(c, rise_buf).wait_send()
        local(qkv_in, rise_buf.at[:, pl.ds(0, 3 * head_cols)], load_sem.at[2]).start()

    def mixed_back():
        for i in range(head_cols // thin):
            for copy in tile_copy(out_w, i * thin, i % 2):
                copy.wait()
            value = jnp.dot(low_buf[...], flat(tile_buf[i % 2]), preferred_element_type=jnp.float32)
            start = 3 * head_cols + i * thin
            rise_buf[:, start : start + thin] = value.astype(jnp.bfloat16)
            if i + 2 < head_cols // thin:
                for copy in tile_copy(out_w, (i + 2) * thin, i % 2):
                    copy.start()

    def attend_back(first, last):
        @pl.loop(first, last)
        def _(h):
            def cols(which):
                return pl.ds(pl.multiple_of(which * head_cols + h * HEAD_DIM, HEAD_DIM), HEAD_DIM)

            key, value = rise_buf[:, cols(1)], rise_buf[:, cols(2)]
            key_sum = value_sum = None
            query_total = jnp.zeros((1, HEAD_DIM), jnp.float32)
            for part in range(2):
                rows = slice(part * half, (part + 1) * half)
                query, grad_mixed = rise_buf[rows, cols(0)], rise_buf[rows, cols(3)]
                scores = contract_cols(query, key) * factor
                scores = jnp.where(mask_ref[0:1, :] > 0.0, scores, MASKED)
                expanded = jnp.exp(scores - jnp.max(scores, axis=1, keepdims=True))
                weight = expanded / jnp.sum(expanded, axis=1, keepdims=True)
                grad_weight = contract_cols(grad_mixed, value)
                inner = jnp.sum(weight * grad_weight, axis=1, keepdims=True)
                grad_scores = (weight * (grad_weight - inner)).astype(jnp.bfloat16)
                grad_value = contract_rows(weight.astype(jnp.bfloat16), grad_mixed)
                grad_key = contract_rows(grad_scores, query)
                grad_query = (
                    jnp.dot(grad_scores, key, preferred_element_type=jnp.float32) * factor
                ).astype(jnp.bfloat16)
                qkv_buf[rows, cols(0)] = grad_query
                query_total += total_row(grad_query.astype(jnp.float32))
                key_sum = grad_key if key_sum is None else key_sum + grad_key
                value_sum = grad_value if value_sum is None else value_sum + grad_value
            qkv_buf[:, cols(1)] = (key_sum * factor).astype(jnp.bfloat16)
            value_low = value_sum.astype(jnp.bfloat16)
            qkv_buf[:, cols(2)] = value_low
            at = pl.ds(pl.multiple_of(tensor * head_cols + h * HEAD_DIM, HEAD_DIM), HEAD_DIM)
            small_land[0, 0:1, at] = query_total
            small_land[0, 1:2, at] = total_row(value_low.astype(jnp.float32))

    def attend_done():
        local(qkv_buf, qkv_own, store_sem.at[4]).start()
        for c in range(qkv_first, total):
            right_out(c, qkv_buf).start()
        input_start(0)

    def input_copies(p):
        return [
            local(query_w.at[p], wide_buf.at[0, :, :, :, pl.ds(0, head_cols)], wide_sem.at[0, 0]),
            local(key_w.at[p], wide_buf.at[0, :, :, :, pl.ds(head_cols, head_cols)], wide_sem.at[0, 1]),
            local(value_w.at[p], wide_buf.at[1, :, :, :, pl.ds(0, head_cols)], wide_sem.at[1, 0]),
        ]

    def input_start(p):
        for copy in input_copies(p):
            copy.start()

    own_rows = pl.ds(pl.multiple_of(tensor * half, half), half)
    other_rows = pl.ds(pl.multiple_of((1 - tensor) * half, half), half)

    def input_share(p):
        return remote(
            send_buf.at[pl.ds(0, half), block_cols(p)], input_land.at[:, block_cols(p)], input_send.at[p],
            input_recv.at[p], y_peer,
        )

    def input_back(first, last):
        @pl.loop(first, last)
        def _(p):
            for copy in input_copies(p):
                copy.wait()
            pair = flat(wide_buf[0])
            single = flat(wide_buf[1, :, :, :, 0:head_cols])

            def share(rows):
                return contract_cols(qkv_buf[rows, 0 : 2 * head_cols], pair) + contract_cols(
                    qkv_buf[rows, 2 * head_cols : 3 * head_cols], single
                )

            send_buf[0:half, block_cols(p)] = share(other_rows).astype(jnp.bfloat16)
            input_share(p).start()
            acc_buf[own_rows, block_cols(p)] += share(own_rows)

            @pl.when(p + 1 < planes)
            def _():
                input_start(p + 1)

    def input_done():
        @pl.loop(0, planes)
        def _(p):
            input_share(p).wait()

        @pl.loop(0, half // 16)
        def _(i):
            rows = pl.ds(pl.multiple_of(tensor * half + i * 16, 16), 16)
            land = pl.ds(pl.multiple_of(i * 16, 16), 16)
            acc_buf[land, :] = acc_buf[rows, :] + input_land[land, :].astype(jnp.float32)

    groups = planes * 4
    index = (plane * 2 + across) * 2 + core
    group = half // groups
    whole, rest, padded, chunks = rest_shape(group)
    rest_width = features // chunks
    back_parts = ((0, whole_buf, whole_out), (1, rest_buf, rest_out))[0 if whole else 1 :]

    def back(which, source, target, k):
        peer = lax.rem(index + k, groups)
        return remote(
            source.at[peer], target.at[index], back_send.at[which, k], back_recv.at[which, k], (peer, tensor)
        )

    def back_own(which, source, target):
        return local(source.at[index], target.at[index], back_recv.at[which, 0])

    def send_back():
        rest_wide[...] = jnp.zeros_like(rest_wide)
        for s in range(groups):
            start = s * group
            if whole:
                whole_buf[s] = acc_buf[start : start + whole, :].astype(jnp.bfloat16)
            for q in range(chunks):
                rest_wide[q * padded : q * padded + rest, :] = acc_buf[
                    start + whole : start + group, q * rest_width : (q + 1) * rest_width
                ]
            rest_buf[s] = rest_wide[...].astype(jnp.bfloat16)
        for part in back_parts:
            back_own(*part).start()
            for k in range(1, groups):
                back(*part, k).start()

    def back_wait():
        for part in back_parts:
            back_own(*part).wait()
            for k in range(1, groups):
                back(*part, k).wait()

    local(down_in, low_buf, load_sem.at[0]).start()
    local(hidden_in, send_buf, load_sem.at[1]).start()
    local(sums_in, sums_buf, load_sem.at[2]).start()
    rise_start(0)
    rise_start(1)
    enter([(lax.rem(index + k, groups), tensor) for k in range(1, groups)] + [y_peer])
    for c in range(up_first):
        right_out(c).start()
    local(down_in, low_buf, load_sem.at[0]).wait()
    turn(0, low_buf)
    small_land[0] = jnp.zeros(small_land.shape[1:], jnp.float32)
    local(sums_in, sums_buf, load_sem.at[2]).wait()
    for i, row in enumerate((10, 11, 7)):
        small_land[0, row : row + 1, :] = total_row(sums_buf[i])
    fetch(0)

    def turn_hidden():
        local(hidden_in, send_buf, load_sem.at[1]).wait()
        turn(1, send_buf)

    def stored():
        for g in range(up_cols // (2 * JOB)):
            rise_store(g).wait()

    def load_input():
        local(x_in, low_buf, load_sem.at[1]).start()

    def turn_input():
        local(x_in, low_buf, load_sem.at[1]).wait()
        turn(3, low_buf)

    def start_out():
        for c in range(out_first, qkv_first):
            right_out(c).start()

    def wait_qkv():
        local(qkv_in, rise_buf.at[:, pl.ds(0, 3 * head_cols)], load_sem.at[2]).wait()

    def store_qkv_wait():
        local(qkv_buf, qkv_own, store_sem.at[4]).wait()

    plan = {
        0: [(rise, 0)],
        1: [(rise, 1)],
        2: [(rise, 2)],
        3: [(rise, 3), (turn_hidden,), (hidden_start,)],
        4: [(hidden_back, 0, planes // 2)],
        5: [(hidden_back, planes // 2, planes), (norm_start,), (start_out,), (stored,)],
        10: [(norm_back,), (mixed_start,)],
        11: [(turn, 2, low_buf), (mixed_back,), (load_input,)],
        12: [(wait_qkv,), (attend_back, 0, heads // 4), (turn_input,)],
        13: [(attend_back, heads // 4, heads // 2)],
        14: [(attend_back, heads // 2, 3 * heads // 4)],
        15: [(attend_back, 3 * heads // 4, heads), (attend_done,)],
        16: [(input_back, 0, planes // 2), (small_begin, 0), (store_qkv_wait,)],
        17: [(input_back, planes // 2, planes), (small_end, 0), (small_begin, 1)],
        18: [(small_end, 1), (small_begin, 2)],
        19: [(small_end, 2), (small_begin, 3)],
        20: [(input_done,), (send_back,), (small_end, 3)],
    }
    for n in range(total + 4):
        if n < total:
            multiply(n)
        for step in plan.get(n, []):
            step[0](*step[1:])
        if 2 <= n < total + 2:
            fold(n - 2)
        if n >= 4:
            finish(n - 4)
    local(small_land.at[1], small_out, load_sem.at[0]).wait()
    back_wait()
    left_out(3).wait_send()
    for c in range(total):
        if not up_first <= c < out_first:
            right_out(c).wait_send()
        if c >= total - 3:
            x_out(c).wait_send()
    for c in range(total - 2, total):
        grad_out(c).wait()


def backward(weights, saved, mask, gain):
    planes, _, _, rows, head_cols = weights[0].shape
    up_cols = weights[4].shape[-1]
    tokens, features = saved[0].shape
    total = (2 * up_cols + 4 * head_cols) // JOB
    slots = 8
    thin, strip = 256, 64
    sem, low, high = pltpu.SemaphoreType.DMA, jnp.bfloat16, jnp.float32
    hbm, vmem = pl.BlockSpec(memory_space=pl.ANY), pl.BlockSpec(memory_space=pltpu.VMEM)
    small_rows = 16
    groups = planes * 4
    whole, rest, padded, chunks = rest_shape(tokens // 2 // groups)
    whole_shape = ((groups, whole, features) if whole else (groups, 16, 128), low)
    rest_rows = ((groups, 16, features // chunks), low)
    shapes = (
        [((rows, head_cols), high)] * 4 + [((rows, up_cols), high)] * 2
        + [((small_rows, features), high), whole_shape, rest_rows]
        + [((4, planes, 2, rows, tokens), low)] * 2
        + [((tokens, up_cols), low)] * 3 + [((tokens, head_cols), low)] + [((tokens, 3 * head_cols), low)] * 2
    )
    scratch = [
        ((2, 2, planes, rows, 2 * tokens), low), ((2, 2 * tokens, JOB), low), ((3, 2, planes, rows, JOB), low),
        ((slots, planes, rows, JOB), low), ((slots, planes - 1, rows, JOB), low), ((2, rows, JOB), high),
        ((2, planes, 2, 2, rows, thin), low), ((2, 2, 2, rows, features), low), ((tokens, features), low),
        ((tokens, up_cols), low), ((2, tokens, thin), low), ((tokens, features), high),
        ((tokens, features), low), ((tokens, features), low), ((tokens, 3 * head_cols), low),
        ((planes, 2, 2, rows, tokens), low), ((tokens // 2, features), low), ((2, 2, strip, features), high),
        ((tokens, 128), high), ((3, 16, features), high), ((3 + planes, small_rows, features), high),
        whole_shape, rest_rows, ((16, features // chunks), high),
    ]
    sems = [
        (2, 2, 2), (2, 2), (2,), (total,), (total,), (4,), (4,), (total,), (total,),
        (total, planes - 1), (total, planes - 1), (2 + planes,), (2 + planes,), (2, planes), (2, 2), (2,),
        (4,), (5,), (1,), (planes,), (planes,), (planes,), (planes,), (2, 2), (2, groups), (2, groups),
    ]
    results = pl.pallas_call(
        partial(backward_kernel, planes),
        out_shape=[jax.ShapeDtypeStruct(*shape) for shape in shapes],
        in_specs=[hbm] * 17 + [vmem] * 2,
        out_specs=[hbm] * len(shapes),
        scratch_shapes=[pltpu.VMEM(*shape) for shape in scratch] + [sem(shape) for shape in sems],
        compiler_params=pltpu.CompilerParams(
            collective_id=1, has_side_effects=True, vmem_limit_bytes=62 * 2**20
        ),
        name="backward_scatter",
    )(*weights, *saved, mask, gain)
    whole_rows, rest_rows = results[7], results[8]
    rest_rows = rest_rows.reshape(groups, chunks, padded, features // chunks).transpose(0, 2, 1, 3)
    returned = rest_rows.reshape(groups, padded, features)[:, :rest]
    if whole:
        returned = jnp.concatenate((whole_rows, returned), axis=1)
    return results[:6], results[6], returned


def shards(
    inputs,
    lengths,
    dealing,
    w_query,
    w_key,
    w_value,
    b_query,
    b_value,
    w_out,
    b_out,
    gain_first,
    shift_first,
    w_up,
    b_up,
    w_down,
    b_down,
    gain_second,
    shift_second,
    cotangent,
):
    group_index = lax.axis_index("dp")
    tensor_index = lax.axis_index("tensor")
    ordered = jnp.take(inputs, dealing, axis=0)
    features = cotangent.shape[-1]
    half_rows = cotangent.shape[1]
    seq_len = half_rows * lax.axis_size("tensor")
    length = lengths[dealing[group_index]]
    key_valid = jnp.arange(seq_len) < length
    head_cols = w_query.shape[1]
    up_cols = w_up.shape[1]
    query_bias = lax.dynamic_slice_in_dim(b_query, tensor_index * head_cols, head_cols)
    value_bias = lax.dynamic_slice_in_dim(b_value, tensor_index * head_cols, head_cols)
    up_bias = lax.dynamic_slice_in_dim(b_up, tensor_index * up_cols, up_cols)
    vectors = jnp.concatenate(
        (query_bias, value_bias, b_out, gain_first, shift_first, up_bias, b_down, gain_second, shift_second)
    ).reshape(1, -1)
    mask = jnp.broadcast_to(key_valid.astype(jnp.float32), (8, seq_len))
    weights, saved = forward(
        [w_query, w_key, w_value, w_out.T, w_up, w_down.T],
        ordered.reshape(ordered.shape[0], -1, features), cotangent.reshape(half_rows, features), mask, vectors,
    )
    (
        full_in, _, qkv, mixed_heads, normed_full, inverse_full, full_hidden, active, slope,
        result, full_grad_down, second_full, second_sums,
    ) = saved
    output = result.reshape(cotangent.shape)
    grads, small_total, grad_own = backward(
        weights,
        [
            full_in, qkv, mixed_heads, normed_full, inverse_full, full_hidden, active, slope,
            full_grad_down, second_full, second_sums,
        ],
        mask, gain_first.reshape(1, -1),
    )
    returned = grad_own.reshape(inputs.shape)
    grad_inputs = jnp.zeros_like(returned).at[dealing].set(returned)
    weight_sums = (grads[0], grads[1], grads[2], grads[3].T, grads[4], grads[5].T)
    up_rows = b_up.shape[0] // features
    small_sums = (
        small_total[0], small_total[1], small_total[2], small_total[3 : 3 + up_rows].reshape(-1),
        small_total[7], small_total[8], small_total[9], small_total[10], small_total[11],
    )
    return (
        output,
        grad_inputs,
        weight_sums[0],
        weight_sums[1],
        weight_sums[2],
        small_sums[0],
        small_sums[1],
        weight_sums[3],
        small_sums[2],
        small_sums[5],
        small_sums[6],
        weight_sums[4],
        small_sums[3],
        weight_sums[5],
        small_sums[4],
        small_sums[7],
        small_sums[8],
    )


def solution(mesh):
    in_specs = (
        P(None, "tensor", "dp", None),
        P(),
        P(),
        P("dp", "tensor"),
        P("dp", "tensor"),
        P("dp", "tensor"),
        P(),
        P(),
        P("tensor", "dp"),
        P(),
        P(),
        P(),
        P("dp", "tensor"),
        P(),
        P("tensor", "dp"),
        P(),
        P(),
        P(),
        P("dp", "tensor", None),
    )
    out_specs = (
        P("dp", "tensor", None),
        P(None, "tensor", "dp", None),
        P("dp", "tensor"),
        P("dp", "tensor"),
        P("dp", "tensor"),
        P(),
        P(),
        P("tensor", "dp"),
        P(),
        P(),
        P(),
        P("dp", "tensor"),
        P(),
        P("tensor", "dp"),
        P(),
        P(),
        P(),
    )
    return jax.shard_map(shards, mesh=mesh, in_specs=in_specs, out_specs=out_specs, check_vma=False)
```

```python
from functools import partial

import jax
import jax.numpy as jnp
from jax import lax
from jax.experimental import pallas as pl
from jax.experimental.pallas import tpu as pltpu
from jax.sharding import PartitionSpec as P

HEAD_DIM = 128


EPSILON = 1e-05
MASKED = -1e30


def norm_forward(values, scale_gain, bias_shift):
    center = values - jnp.mean(values, axis=-1, keepdims=True)
    inverse = lax.rsqrt(jnp.mean(center * center, axis=-1, keepdims=True) + EPSILON)
    normed = center * inverse
    return (normed * scale_gain + bias_shift, normed, inverse)


def contract_rows(left, right):
    return lax.dot_general(
        left, right, (((0,), (0,)), ((), ())), preferred_element_type=jnp.float32
    )


def contract_cols(left, right):
    return lax.dot_general(
        left, right, (((1,), (1,)), ((), ())), preferred_element_type=jnp.float32
    )


MESH = pl.DeviceIdType.MESH
TILE = 1024
SLOPE = 0.7978845608028654


def place():
    dp, tensor = lax.axis_index("dp"), lax.axis_index("tensor")
    return dp // 4, (dp // 2) % 2, dp % 2, tensor


def device_of(plane, across, core, tensor):
    return ((plane * 2 + across) * 2 + core, tensor)


def enter(peers):
    barrier = pltpu.get_barrier_semaphore()
    for peer in peers:
        pl.semaphore_signal(barrier, inc=1, device_id=peer, device_id_type=MESH)
    pl.semaphore_wait(barrier, len(peers))


LAG, LEAD, X_FIRST, DEALT, X_LEAD, NORM = 4, (3, 2, 1), (3, 7), 7, 6, 14


def rest_shape(count):
    whole = count // 16 * 16
    rest = count - whole
    padded = 4 if rest <= 4 else 8 if rest <= 8 else 16
    return whole, rest, padded, 16 // padded

def gather_tiles(widths):
    return [(i, start) for i, width in enumerate(widths) for start in range(0, width, TILE)]


def forward_kernel(planes, widths, *refs):
    count = len(widths)
    shard_refs = refs[:count]
    deal_refs = refs[count : count + 2]
    cot_ref, mask_ref, vec_ref = refs[count + 2 : count + 5]
    outs = refs[count + 5 :]
    full_refs = outs[:count]
    (
        x_full, cot_full, qkv_out, mixed_out, normed_out, inverse_out, hidden_out, active_out, slope_out,
        result_out, down_out, second_out, sums_out,
    ) = outs[count : count + 13]
    (
        w_buf, x_buf, qkv_buf, mixed_buf, attn_acc, attn_land, send_buf, hidden_buf, active_buf, slope_buf,
        down_acc, down_land, inverse_buf, result_buf, sums_buf, whole_land, rest_land,
        plane_send, plane_recv, x_send, x_recv, core_send, core_recv, w_sem, in_send, in_recv,
        attn_send, attn_recv, down_send, down_recv, load_sem, store_sem,
        deal_send, deal_recv,
    ) = outs[count + 13 :]
    plane, across, core, tensor = place()
    far = [lax.rem(plane + k, planes) for k in range(planes)]
    x_peer = device_of(plane, 1 - across, core, tensor)
    core_peer = device_of(plane, across, 1 - core, tensor)
    y_peer = device_of(plane, across, core, 1 - tensor)
    plane_peers = [device_of(far[k], across, core, tensor) for k in range(planes)]
    tiles = gather_tiles(widths)
    half, features = cot_ref.shape
    tokens = 2 * half
    block = features // planes
    head_cols = mixed_buf.shape[1]
    factor = HEAD_DIM ** (-0.5)
    own_rows = pl.ds(pl.multiple_of(tensor * half, half), half)

    vec_at = {}
    at = 0
    for key, size in (
        ("b_query", head_cols), ("b_value", head_cols), ("b_out", features), ("gain_first", features),
        ("shift_first", features), ("b_up", widths[4]), ("b_down", features), ("gain_second", features),
        ("shift_second", features),
    ):
        vec_at[key] = at
        at += size

    def vector(key, start, size):
        return vec_ref[:, pl.ds(vec_at[key] + start, size)]

    first_down = len(tiles) - widths[5] // TILE
    units = [(c, j) for c in range(first_down) for j in range(planes)]
    units += [(c, j) for j in range(planes) for c in range(first_down, len(tiles))]
    lag = LAG
    relayed = planes == 4
    across_first = X_FIRST if relayed else ()
    low_side = plane < planes // 2
    origins = [
        jnp.where(low_side, lax.rem(plane + j, planes), lax.rem(plane + planes - j, planes)) for j in range(planes)
    ]

    def view(c, *where):
        i, start = tiles[c]
        return full_refs[i].at[(*where, slice(None), pl.ds(start, TILE))]

    def own(c):
        i, start = tiles[c]
        return shard_refs[i].at[:, pl.ds(start, TILE)]

    def own_load(c):
        return pltpu.make_async_copy(own(c), w_buf.at[1, c // 4, (c // 2) % 2, c % 2], plane_recv.at[c, 0])

    def own_store(c):
        return pltpu.make_async_copy(
            w_buf.at[1, c // 4, (c // 2) % 2, c % 2], view(c, plane, across, core), plane_recv.at[c, 0]
        )

    def both(c):
        return slice(None) if c in across_first else across

    def z_copy(c, origin, target, send):
        part = view(c, origin, both(c), core)
        if c not in across_first and send <= 3:
            part = own(c)
        place_there = jnp.where(
            target < planes // 2, lax.rem(origin + planes - target, planes), lax.rem(target + planes - origin, planes)
        )
        return pltpu.make_async_remote_copy(
            part, view(c, origin, both(c), core), plane_send.at[c, send], plane_recv.at[c, place_there],
            device_id=device_of(target, across, core, tensor), device_id_type=MESH,
        )

    middle = jnp.logical_and(plane > 0, plane < planes - 1)

    def z_each(c, act):
        for k in range(1, planes):
            if not relayed:
                act(z_copy(c, plane, far[k], k))
            elif k != 2:
                @pl.when((plane < planes - 1) if k == 1 else (plane > 0))
                def _():
                    act(z_copy(c, plane, far[k], k))

    def z_pass(c, j):
        near_end, far_side = jnp.where(plane == 1, 0, planes - 1), jnp.where(plane == 1, 2, 1)
        return z_copy(c, origins[j], far_side if j == 3 else near_end, 3 + j)

    def z_arrival(c, j):
        part = view(c, origins[j], both(c), core)
        return pltpu.make_async_remote_copy(
            part, part, plane_send.at[c, j], plane_recv.at[c, j], device_id=x_peer, device_id_type=MESH
        )

    def x_copy(c, j, side):
        part = view(c, origins[j], side, core)
        return pltpu.make_async_remote_copy(
            own(c) if j == 0 else part, part, x_send.at[c, j], x_recv.at[c, j], device_id=x_peer,
            device_id_type=MESH,
        )

    def unit_core(u, side):
        c, j = units[u]
        part = view(c, origins[j], slice(None), side)
        return pltpu.make_async_remote_copy(
            part, part, core_send.at[c, j], core_recv.at[c, j], device_id=core_peer, device_id_type=MESH
        )

    lead_own, lead_first, lead_second = LEAD
    z_at, first_at, second_at = {}, {}, {}
    for c in range(len(tiles)):
        for lead, table, ramp in ((lead_own, z_at, c - 1), (lead_first, first_at, c + 1), (lead_second, second_at, c + 2)):
            table.setdefault(max(planes * (c - lead), ramp), []).append(c)

    def z_begin(n):
        for c in z_at.get(n, []):
            if c in across_first:
                x_copy(c, 0, 1 - across).wait_recv()
            z_each(c, lambda copy: copy.start())

    def z_forward(n):
        steps = [(c, (1, 3)) for c in first_at.get(n, [])] + [(c, (2,)) for c in second_at.get(n, [])]
        if relayed and steps:
            @pl.when(middle)
            def _():
                for c, positions in steps:
                    for j in positions:
                        z_arrival(c, j).wait_recv()
                        z_pass(c, j).start()

    def pump(n):
        if n < len(units):
            if n > 0:
                z_begin(n)
            c, j = units[n]
            z_forward(n)
            if j > 0:
                if relayed:
                    pl.when(jnp.logical_not(middle))(z_arrival(c, j).wait_recv)
                else:
                    z_arrival(c, j).wait_recv()
            if c not in across_first:
                if j > 0:
                    x_copy(c, j, across).start()
            if j == 0 and c + X_LEAD < len(tiles) and c + X_LEAD not in across_first:
                x_copy(c + X_LEAD, 0, across).start()
        if n >= lag:
            c, j = units[n - lag]
            if c not in across_first:
                x_copy(c, j, 1 - across).wait_recv()
            unit_core(n - lag, core).start()

    def landed(u):
        unit_core(u, 1 - core).wait_recv()

    def tile_copies(c):
        i, start = tiles[c]
        return [
            pltpu.make_async_copy(
                full_refs[i].at[p, :, :, :, pl.ds(start, TILE)], w_buf.at[c % 2, p], w_sem.at[c % 2, p]
            )
            for p in range(planes)
        ]

    def load_tile(c):
        for u, (tile, _) in enumerate(units):
            if tile == c:
                landed(u)
        for copy in tile_copies(c):
            copy.start()

    def wait_tile(c):
        for copy in tile_copies(c):
            copy.wait()

    def down_copy(k, j):
        c = first_down + j
        return pltpu.make_async_copy(
            view(c, origins[k], slice(None), slice(None)), w_buf.at[k % 2, j], w_sem.at[k % 2, j]
        )

    down_parts = widths[5] // TILE

    def load_down(k):
        for j in range(down_parts):
            landed(units.index((first_down + j, k)))
            down_copy(k, j).start()

    def flat(value):
        return value.reshape(-1, value.shape[-1])

    groups = planes * 4
    index = (plane * 2 + across) * 2 + core
    group = half // groups
    whole, rest, padded, chunks = rest_shape(group)
    rest_width = features // chunks
    deal_parts = ((0, whole_land), (1, rest_land)) if whole else ((1, rest_land),)

    def deal(which, land, k):
        target = lax.rem(index + k, groups)
        return pltpu.make_async_remote_copy(
            deal_refs[which].at[target], land.at[index], deal_send.at[which, k], deal_recv.at[which, k],
            device_id=(target, tensor), device_id_type=MESH,
        )

    def deal_own(which, land):
        return pltpu.make_async_copy(deal_refs[which].at[index], land.at[index], deal_recv.at[which, 0])

    def dealt():
        for which, land in deal_parts:
            deal_own(which, land).wait()
            for k in range(1, groups):
                deal(which, land, k).wait_recv()
        for s in range(groups):
            start = s * group
            if whole:
                attn_acc[start : start + whole, :] = whole_land[s].astype(jnp.float32)
            tail = rest_land[s].astype(jnp.float32)
            for q in range(chunks):
                attn_acc[start + whole : start + group, q * rest_width : (q + 1) * rest_width] = tail[
                    q * padded : q * padded + rest, :
                ]

        @pl.loop(0, half // 16)
        def _(i):
            rows = pl.ds(pl.multiple_of(tensor * half + i * 16, 16), 16)
            x_buf[rows, :] = attn_acc[pl.ds(pl.multiple_of(i * 16, 16), 16), :].astype(jnp.bfloat16)

        exchange(0, x_buf.at[own_rows], x_buf).start()

    def load_x():
        exchange(0, x_buf.at[own_rows], x_buf).wait_recv()
        store(11, x_buf, x_full).start()

    def cot_load():
        other_rows = pl.ds(pl.multiple_of((1 - tensor) * half, half), half)
        return [
            pltpu.make_async_copy(cot_ref, x_buf.at[own_rows], load_sem.at[1]),
            pltpu.make_async_copy(cot_full.at[other_rows], x_buf.at[other_rows], load_sem.at[2]),
        ]

    def exchange(which, source, target):
        return pltpu.make_async_remote_copy(
            source, target.at[own_rows], in_send.at[which], in_recv.at[which],
            device_id=y_peer, device_id_type=MESH,
        )

    def load_cot():
        exchange(1, cot_ref, cot_full).wait_recv()
        for copy in cot_load():
            copy.start()

    def project(c, bias):
        wait_tile(c)

        @pl.loop(0, TILE // 512)
        def _(n):
            cols = pl.ds(pl.multiple_of(n * 512, 512), 512)
            value = jnp.dot(
                x_buf[...], flat(w_buf[c % 2, :, :, :, :, cols]), preferred_element_type=jnp.float32
            )
            if bias is not None:
                value += vec_ref[:, pl.ds(pl.multiple_of(vec_at[bias] + n * 512, 128), 512)]
            qkv_buf[:, pl.ds(pl.multiple_of(c * TILE + n * 512, 512), 512)] = value.astype(jnp.bfloat16)

    def attend(first, last):
        @pl.loop(first, last)
        def _(h):
            def cols(which):
                return pl.ds(pl.multiple_of(which * head_cols + h * HEAD_DIM, HEAD_DIM), HEAD_DIM)

            scores = contract_cols(qkv_buf[:, cols(0)], qkv_buf[:, cols(1)]) * factor
            scores = jnp.where(mask_ref[0:1, :] > 0.0, scores, MASKED)
            expanded = jnp.exp(scores - jnp.max(scores, axis=1, keepdims=True))
            weight = (expanded / jnp.sum(expanded, axis=1, keepdims=True)).astype(jnp.bfloat16)
            mixed_buf[:, cols(0)] = jnp.dot(
                weight, qkv_buf[:, cols(2)], preferred_element_type=jnp.float32
            ).astype(jnp.bfloat16)

    def block_cols(p):
        return pl.ds(pl.multiple_of(p * block, block), block)

    def attn_share(p):
        return pltpu.make_async_remote_copy(
            send_buf.at[:, block_cols(p)], attn_land.at[:, block_cols(p)], attn_send.at[p], attn_recv.at[p],
            device_id=y_peer, device_id_type=MESH,
        )

    def project_out():
        wait_tile(3)

        @pl.loop(0, planes)
        def _(p):
            value = contract_cols(mixed_buf[...], flat(w_buf[1, p]))
            attn_acc[:, block_cols(p)] = value
            send_buf[:, block_cols(p)] = value.astype(jnp.bfloat16)
            attn_share(p).start()

    def first_norm():
        @pl.loop(0, planes)
        def _(p):
            attn_share(p).wait()

        @pl.loop(0, tokens // 16, unroll=2)
        def _(i):
            rows = pl.ds(pl.multiple_of(i * 16, 16), 16)
            value = (
                x_buf[rows, :].astype(jnp.float32)
                + (attn_acc[rows, :] + attn_land[rows, :].astype(jnp.float32))
                + vector("b_out", 0, features)
            )
            hidden, normed, inverse = norm_forward(
                value, vector("gain_first", 0, features), vector("shift_first", 0, features)
            )
            attn_acc[rows, :] = normed
            inverse_buf[rows, :] = jnp.broadcast_to(inverse, (16, 128))
            hidden_buf[rows, :] = hidden.astype(jnp.bfloat16)

        store(0, attn_acc, normed_out).start()
        store(1, inverse_buf, inverse_out).start()
        store(2, hidden_buf, hidden_out).start()
        store(11, x_buf, x_full).wait()
        exchange(0, x_buf.at[own_rows], x_buf).wait_send()
        exchange(1, cot_ref, cot_full).start()

    def store(which, source, target):
        return pltpu.make_async_copy(source, target, store_sem.at[which])

    def slope_store(j):
        return pltpu.make_async_copy(
            slope_buf.at[j % 2], slope_out.at[:, pl.ds(j * TILE, TILE)], store_sem.at[5 + j % 2]
        )

    def raise_up(j):
        c = 4 + j
        wait_tile(c)
        if j >= 2:
            slope_store(j - 2).wait()

        @pl.loop(0, TILE // 256)
        def _(n):
            cols = pl.ds(pl.multiple_of(n * 256, 256), 256)
            value = jnp.dot(
                hidden_buf[...], flat(w_buf[c % 2, :, :, :, :, cols]), preferred_element_type=jnp.float32
            )
            value += vec_ref[:, pl.ds(pl.multiple_of(vec_at["b_up"] + j * TILE + n * 256, 128), 256)]
            square = value * value
            bend = jnp.tanh(SLOPE * value * (1.0 + 0.044715 * square))
            rise = 0.5 * (1.0 + bend)
            active_buf[:, pl.ds(pl.multiple_of(j * TILE + n * 256, 256), 256)] = (value * rise).astype(
                jnp.bfloat16
            )
            slope_buf[j % 2, :, cols] = (
                rise + 0.5 * value * (1.0 - bend * bend) * (SLOPE * (1.0 + 3.0 * 0.044715 * square))
            ).astype(jnp.bfloat16)

        slope_store(j).start()

    def down_share(k):
        cols = block_cols(origins[k])
        return pltpu.make_async_remote_copy(
            send_buf.at[:, cols], down_land.at[:, cols], down_send.at[k], down_recv.at[k],
            device_id=y_peer, device_id_type=MESH,
        )

    def lower(k):
        cols = block_cols(origins[k])
        value = None
        for j in range(down_parts):
            down_copy(k, j).wait()
            part = contract_cols(active_buf[:, j * TILE : (j + 1) * TILE], flat(w_buf[k % 2, j]))
            value = part if value is None else value + part
        down_acc[:, cols] = value
        send_buf[:, cols] = value.astype(jnp.bfloat16)
        down_share(k).start()

    def second_norm():
        for k in range(planes):
            down_share(k).wait()
        for copy in cot_load():
            copy.wait()
        store(2, hidden_buf, hidden_out).wait()
        sums_buf[...] = jnp.zeros_like(sums_buf)
        gain = vector("gain_second", 0, features)

        def rows_of(which, i):
            base = tensor if which == 0 else 1 - tensor
            return pl.ds(pl.multiple_of(base * half + i * 16, 16), 16)

        for which in (0, 1):
            @pl.loop(0, half // 16, unroll=2)
            def _(i):
                rows = rows_of(which, i)
                hidden = attn_acc[rows, :] * vector("gain_first", 0, features) + vector(
                    "shift_first", 0, features
                )
                value = (
                    hidden
                    + (down_acc[rows, :] + down_land[rows, :].astype(jnp.float32))
                    + vector("b_down", 0, features)
                )
                result, normed, inverse = norm_forward(value, gain, vector("shift_second", 0, features))
                grad_out = x_buf[rows, :].astype(jnp.float32)
                scaled = grad_out * gain
                grad = inverse * (
                    scaled
                    - jnp.mean(scaled, axis=-1, keepdims=True)
                    - normed * jnp.mean(scaled * normed, axis=-1, keepdims=True)
                )
                down_acc[rows, :] = grad
                low = grad.astype(jnp.bfloat16)
                hidden_buf[rows, :] = low
                if which == 0:
                    result_buf[pl.ds(pl.multiple_of(i * 16, 16), 16), :] = result.astype(jnp.bfloat16)
                    sums_buf[0] += grad_out * normed
                    sums_buf[1] += grad_out
                    sums_buf[2] += low.astype(jnp.float32)

        for which, source, target in (
            (2, hidden_buf, down_out), (3, down_acc, second_out), (4, result_buf, result_out), (9, sums_buf, sums_out),
        ):
            store(which, source, target).start()

    for c in range(len(tiles)):
        own_load(c).start()
    for which, land in deal_parts:
        deal_own(which, land).start()
    enter([(lax.rem(index + k, groups), tensor) for k in range(1, groups)] + [y_peer])
    z_begin(-1)
    for c in sorted({*range(X_LEAD), *across_first}):
        x_copy(c, 0, across).start()
    for k in range(1, groups):
        for which, land in deal_parts:
            deal(which, land, k).start()
    z_begin(0)
    for c in range(len(tiles)):
        own_load(c).wait()
        own_store(c).start()
    for c in range(len(tiles)):
        own_store(c).wait()

    plan = {}

    def at_slot(n, step, *args):
        plan.setdefault(n, []).append((step, args))

    def ready(c):
        return planes * (c + 1) + lag

    heads = head_cols // HEAD_DIM
    at_slot(DEALT, dealt)
    at_slot(ready(0), load_tile, 0)
    at_slot(ready(1), load_tile, 1)
    at_slot(ready(2) - 2, load_x)
    at_slot(ready(2) - 2, project, 0, "b_query")
    at_slot(ready(2) - 1, project, 1, None)
    at_slot(ready(2), load_tile, 2)
    at_slot(ready(2) + 1, project, 2, "b_value")
    begin = ready(2) + 2
    for q in range(4):
        at_slot(begin + q, attend, q * heads // 4, (q + 1) * heads // 4)
    at_slot(begin + 3, load_tile, 3)
    at_slot(begin + 4, project_out)
    norm_slot = begin + 4 + NORM * planes // 4
    at_slot(norm_slot, first_norm)
    at_slot(max(ready(4), begin), load_tile, 4)
    at_slot(max(ready(5), begin + 4), load_tile, 5)
    for j in range(4):
        slot = max(norm_slot + 1 + j, ready(4 + j) + 1)
        at_slot(slot, raise_up, j)
        if j >= 2:
            plan.setdefault(max(norm_slot + 1 + j - 2, ready(4 + j)), []).append((load_tile, (4 + j,)))
    raised = max(norm_slot + 4, ready(7) + 1)
    for k in range(planes):
        slot = planes * first_down + down_parts * (k + 1) + lag
        at_slot(slot, load_down, k)
        at_slot(max(slot + 1, raised), lower, k)
        if k == planes // 2:
            at_slot(slot, load_cot)
    last = max(max(plan), len(units) + lag - 1)
    for n in range(last + 1):
        if n < len(units) + lag:
            pump(n)
        for step, args in plan.get(n, []):
            step(*args)
        if n == begin + 3:
            store(7, qkv_buf, qkv_out).start()
            store(8, mixed_buf, mixed_out).start()
    store(10, active_buf, active_out).start()
    second_norm()
    for which, source, target in (
        (0, attn_acc, normed_out), (1, inverse_buf, inverse_out), (2, hidden_buf, down_out),
        (3, down_acc, second_out), (4, result_buf, result_out), (7, qkv_buf, qkv_out),
        (8, mixed_buf, mixed_out), (9, sums_buf, sums_out), (10, active_buf, active_out),
    ):
        store(which, source, target).wait()
    for j in range(2, 4):
        slope_store(j).wait()
    exchange(1, cot_ref, cot_full).wait_send()
    for which, land in deal_parts:
        for k in range(1, groups):
            deal(which, land, k).wait_send()
    for c in range(len(tiles)):
        z_each(c, lambda copy: copy.wait_send())
        if relayed:
            @pl.when(middle)
            def _():
                for j in range(1, planes):
                    z_pass(c, j).wait_send()
    for u, (c, j) in enumerate(units):
        if c not in across_first or j == 0:
            x_copy(c, j, across).wait_send()
        unit_core(u, core).wait_send()


def forward(shard_list, dealt_rows, cot, mask, vectors):
    planes = lax.axis_size("dp") // 4
    widths = [shard.shape[1] for shard in shard_list]
    total = sum(width // TILE for width in widths)
    half, features = cot.shape
    tokens, rows = 2 * half, shard_list[0].shape[0]
    head_cols, up_cols = widths[0], widths[4]
    groups = planes * 4
    whole, rest, padded, chunks = rest_shape(half // groups)
    whole_rows = dealt_rows[:, : max(whole, 16)] if whole else jnp.zeros((groups, 16, 128), jnp.bfloat16)
    rest_rows = jnp.pad(dealt_rows[:, whole:], ((0, 0), (0, padded - rest), (0, 0)))
    rest_rows = rest_rows.reshape(groups, padded, chunks, features // chunks)
    rest_rows = rest_rows.transpose(0, 2, 1, 3).reshape(groups, 16, features // chunks)
    sem, low, high = pltpu.SemaphoreType.DMA, jnp.bfloat16, jnp.float32
    hbm, vmem = pl.BlockSpec(memory_space=pl.ANY), pl.BlockSpec(memory_space=pltpu.VMEM)
    shapes = [((planes, 2, 2, *shard.shape), low) for shard in shard_list] + [
        ((tokens, features), low), ((tokens, features), low), ((tokens, 3 * head_cols), low),
        ((tokens, head_cols), low), ((tokens, features), high), ((tokens, 128), high),
        ((tokens, features), low), ((tokens, up_cols), low), ((tokens, up_cols), low),
        ((half, features), low), ((tokens, features), low), ((tokens, features), high),
        ((3, 16, features), high),
    ]
    results = pl.pallas_call(
        partial(forward_kernel, planes, widths),
        out_shape=[jax.ShapeDtypeStruct(*shape) for shape in shapes],
        in_specs=[hbm] * (len(shard_list) + 3) + [vmem] * 2,
        out_specs=[hbm] * len(shapes),
        scratch_shapes=[
            pltpu.VMEM((2, planes, 2, 2, rows, TILE), low),
            pltpu.VMEM((tokens, features), low),
            pltpu.VMEM((tokens, 3 * head_cols), low),
            pltpu.VMEM((tokens, head_cols), low),
            pltpu.VMEM((tokens, features), high),
            pltpu.VMEM((tokens, features), low),
            pltpu.VMEM((tokens, features), low),
            pltpu.VMEM((tokens, features), low),
            pltpu.VMEM((tokens, up_cols), low),
            pltpu.VMEM((2, tokens, TILE), low),
            pltpu.VMEM((tokens, features), high),
            pltpu.VMEM((tokens, features), low),
            pltpu.VMEM((tokens, 128), high),
            pltpu.VMEM((half, features), low),
            pltpu.VMEM((3, 16, features), high),
            pltpu.VMEM(whole_rows.shape, low),
            pltpu.VMEM(rest_rows.shape, low),
            sem((total, max(planes, 7))), *[sem((total, planes))] * 5,
            sem((2, max(planes, 4))), sem((2,)), sem((2,)),
            sem((planes,)), sem((planes,)), sem((planes,)), sem((planes,)), sem((3,)), sem((12,)),
            sem((2, groups)), sem((2, groups)),
        ],
        compiler_params=pltpu.CompilerParams(
            collective_id=0, has_side_effects=True, vmem_limit_bytes=62 * 2**20
        ),
        name="forward_gather",
    )(*shard_list, whole_rows, rest_rows, cot, mask, vectors)
    return results[: len(shard_list)], results[len(shard_list) :]


JOB = 512


def backward_kernel(planes, *refs):
    (
        query_w, key_w, value_w, out_w, up_w, down_w,
        x_in, qkv_in, mixed_in, normed_in, inverse_in, hidden_in, active_in, slope_in, down_in, second_in,
        sums_in, mask_ref, gain_ref,
    ) = refs[:19]
    (
        grad_query, grad_key, grad_value, grad_out_w, grad_up, grad_down, small_out, whole_out, rest_out,
        left_own, left_far, active_far, rise_own, rise_far, mixed_far, qkv_own, qkv_far,
    ) = refs[19:36]
    (
        left_buf, right_buf, stage, x_land, plane_land, out_buf, tile_buf, wide_buf, low_buf, rise_buf,
        slope_buf, acc_buf, hidden_land, send_buf, qkv_buf, turn_buf, input_land, row_buf, inverse_buf,
        sums_buf, small_land, whole_buf, rest_buf, rest_wide,
        left_sem, right_sem, out_sem, core_send, core_recv, left_send, left_recv, x_send, x_recv,
        plane_send, plane_recv, small_send, small_recv, tile_sem, wide_sem, slope_sem, load_sem, store_sem,
        turn_sem, hidden_send, hidden_recv, input_send, input_recv, row_sem, back_send, back_recv,
    ) = refs[36:]
    plane, across, core, tensor = place()
    far = [lax.rem(plane + k, planes) for k in range(planes)]
    x_peer = device_of(plane, 1 - across, core, tensor)
    core_peer = device_of(plane, across, 1 - core, tensor)
    y_peer = device_of(plane, across, core, 1 - tensor)
    plane_peers = [device_of(far[k], across, core, tensor) for k in range(planes)]
    tokens, features = low_buf.shape
    half = tokens // 2
    head_cols = mixed_in.shape[1]
    heads = head_cols // HEAD_DIM
    up_cols = active_in.shape[1]
    block = features // planes
    factor = HEAD_DIM ** (-0.5)
    slots = x_land.shape[0]
    thin = tile_buf.shape[-1]

    jobs = [(0, active_in, active_far, s, grad_down, s) for s in range(0, up_cols, JOB)]
    jobs += [(1, rise_own, rise_far, s, grad_up, s) for s in range(0, up_cols, JOB)]
    jobs += [(2, mixed_in, mixed_far, s, grad_out_w, s) for s in range(0, head_cols, JOB)]
    for which, result in enumerate((grad_query, grad_key, grad_value)):
        jobs += [
            (3, qkv_own, qkv_far, which * head_cols + s, result, s) for s in range(0, head_cols, JOB)
        ]
    total = len(jobs)
    up_first, out_first, qkv_first = (
        [job[0] for job in jobs].index(a) for a in (1, 2, 3)
    )

    def local(source, target, sem):
        return pltpu.make_async_copy(source, target, sem)

    def remote(source, target, send, recv, peer):
        return pltpu.make_async_remote_copy(
            source, target, send, recv, device_id=peer, device_id_type=MESH
        )

    def left_out(a):
        return remote(
            turn_buf.at[:, :, 1 - core], left_far.at[a], left_send.at[a], left_recv.at[a], core_peer
        )

    def left_keep(a):
        return local(turn_buf.at[:, :, core], left_own.at[a], turn_sem.at[0])

    kept = set()

    def left_kept(a):
        if a not in kept:
            kept.add(a)
            left_keep(a).wait()

    def turn(a, source):
        if a > 0:
            left_out(a - 1).wait_send()
            left_kept(a - 1)

        @pl.loop(0, planes)
        def _(p):
            cols = pl.ds(pl.multiple_of(p * block, block), block)
            turn_buf[p] = source[:, cols].T.reshape(turn_buf.shape[1:])

        left_keep(a).start()
        left_out(a).start()

    def right_out(c, source=None):
        _, own, other, start, _, _ = jobs[c]
        cols = pl.ds(start, JOB)
        return remote(
            (own if source is None else source).at[:, cols], other.at[:, cols], core_send.at[c],
            core_recv.at[c], core_peer,
        )

    def left_load(a):
        slot = a % 2
        copies = []
        for side in range(2):
            copies.append(
                local(left_own.at[a, :, side], left_buf.at[slot, side, :, :, pl.ds(0, tokens)], left_sem.at[slot, 0, side])
            )
            copies.append(
                local(left_far.at[a, :, side], left_buf.at[slot, side, :, :, pl.ds(tokens, tokens)], left_sem.at[slot, 1, side])
            )
        return copies

    def right_load(c):
        _, own, other, start, _, _ = jobs[c]
        slot, cols = c % 2, pl.ds(start, JOB)
        return [
            local(own.at[:, cols], right_buf.at[slot, pl.ds(0, tokens)], right_sem.at[slot, 0]),
            local(other.at[:, cols], right_buf.at[slot, pl.ds(tokens, tokens)], right_sem.at[slot, 1]),
        ]

    def x_out(c):
        return remote(
            stage.at[c % 3, 1 - across], x_land.at[c % slots], x_send.at[c], x_recv.at[c], x_peer
        )

    relayed = planes == 4
    middle = jnp.logical_and(plane > 0, plane < planes - 1)

    def plane_out(c, k):
        target, block_at, land = far[k], far[k], k - 1
        if relayed and k == 1:
            end = plane == planes - 1
            target, block_at, land = jnp.where(end, plane - 1, plane + 1), jnp.where(end, 0, plane + 1), jnp.where(end, 3, 0)
        if relayed and k == 3:
            end = plane == 0
            target, block_at, land = jnp.where(end, 1, plane - 1), jnp.where(end, planes - 1, plane - 1), jnp.where(end, 3, 2)
        return remote(
            x_land.at[c % slots, block_at], plane_land.at[c % slots, land], plane_send.at[c, k - 1],
            plane_recv.at[c, land], device_of(target, across, core, tensor),
        )

    def plane_in(c, land):
        return remote(
            x_land.at[c % slots, plane], plane_land.at[c % slots, land], plane_send.at[c, 0],
            plane_recv.at[c, land], x_peer,
        )

    def relay(c):
        @pl.when(middle)
        def _():
            plane_in(c, 3).wait_recv()
            x_land[c % slots, far[2]] = (
                x_land[c % slots, far[2]].astype(jnp.float32) + plane_land[c % slots, 3].astype(jnp.float32)
            ).astype(jnp.bfloat16)
            plane_out(c, 2).start()

    def grad_out(c):
        _, _, _, _, result, start = jobs[c]
        return local(out_buf.at[c % 2], result.at[:, pl.ds(start, JOB)], out_sem.at[c % 2])

    def new_left(c):
        return c == 0 or jobs[c - 1][0] != jobs[c][0]

    def fetch(c):
        a = jobs[c][0]
        if new_left(c):
            left_kept(a)
            left_out(a).wait_recv()
            for copy in left_load(a):
                copy.start()
        right_out(c).wait_recv()
        for copy in right_load(c):
            copy.start()

    def multiply(c):
        a = jobs[c][0]
        if new_left(c):
            for copy in left_load(a):
                copy.wait()
        for copy in right_load(c):
            copy.wait()
        if c + 1 < total:
            fetch(c + 1)
        if c >= 3:
            x_out(c - 3).wait_send()

        @pl.loop(0, JOB // 256)
        def _(n):
            cols = pl.ds(pl.multiple_of(n * 256, 256), 256)
            left = left_buf[a % 2]
            result = jnp.dot(
                left.reshape(-1, left.shape[-1]), right_buf[c % 2, :, cols],
                preferred_element_type=jnp.float32,
            ).astype(jnp.bfloat16)
            stage[c % 3, :, :, :, cols] = result.reshape(*left.shape[:-1], 256)

        x_out(c).start()

    def fold(c):
        x_out(c).wait_recv()
        slot = c % slots

        @pl.loop(0, planes)
        def _(p):
            x_land[slot, p] = (
                x_land[slot, p].astype(jnp.float32) + stage[c % 3, across, p].astype(jnp.float32)
            ).astype(jnp.bfloat16)

        for k in range(1, planes):
            if relayed and k == 2:
                @pl.when(jnp.logical_not(middle))
                def _():
                    plane_out(c, 2).start()
            else:
                plane_out(c, k).start()

    def finish(c):
        for k in range(1, planes):
            plane_out(c, k).wait_send()
        if c >= 2:
            grad_out(c - 2).wait()
        out_buf[c % 2] = x_land[c % slots, plane].astype(jnp.float32)
        for land in range(planes - 1):
            def add():
                plane_in(c, land).wait_recv()
                out_buf[c % 2] = out_buf[c % 2] + plane_land[c % slots, land].astype(jnp.float32)

            if relayed and land != 1:
                pl.when((plane > 0) if land == 0 else (plane < planes - 1))(add)
            else:
                add()
        grad_out(c).start()

    def small_copy(step, peer, slot):
        return remote(
            small_land.at[0], small_land.at[slot], small_send.at[step], small_recv.at[step], peer
        )

    def small_begin(step):
        if step < 3:
            small_copy(step, (core_peer, x_peer, y_peer)[step], 1 + step).start()
        else:
            for k in range(1, planes):
                small_copy(2 + k, plane_peers[k], 3 + k).start()

    def small_end(step):
        if step < 3:
            small_copy(step, core_peer, 1 + step).wait()
            small_land[0] = small_land[0] + small_land[1 + step]
        else:
            for k in range(1, planes):
                small_copy(2 + k, core_peer, 3 + k).wait()
            value = jnp.zeros(small_land.shape[1:], jnp.float32)
            for p in range(planes):
                back = lax.rem(plane + planes - p, planes)
                value += small_land[jnp.where(back == 0, 0, 3 + back)]
            small_land[1] = value
            local(small_land.at[1], small_out, load_sem.at[0]).start()

    def total_row(value):
        return jnp.sum(value, axis=0, keepdims=True)

    def tile_copy(weight, start, slot):
        return [
            local(weight.at[p, :, :, :, pl.ds(start, thin)], tile_buf.at[slot, p], tile_sem.at[slot, p])
            for p in range(planes)
        ]

    def slope_copy(start, slot):
        return local(slope_in.at[:, pl.ds(start, thin)], slope_buf.at[slot], slope_sem.at[slot])

    def flat(value):
        return value.reshape(-1, value.shape[-1])

    def rise_start(i):
        for copy in tile_copy(down_w, i * thin, i % 2):
            copy.start()
        slope_copy(i * thin, i % 2).start()

    def rise_store(g):
        cols = pl.ds(g * 2 * JOB, 2 * JOB)
        return local(rise_buf.at[:, cols], rise_own.at[:, cols], store_sem.at[g])

    def rise(g):
        per = 2 * JOB // thin
        for i in range(g * per, (g + 1) * per):
            for copy in tile_copy(down_w, i * thin, i % 2):
                copy.wait()
            slope_copy(i * thin, i % 2).wait()
            value = jnp.dot(low_buf[...], flat(tile_buf[i % 2]), preferred_element_type=jnp.float32)
            value = (value * slope_buf[i % 2].astype(jnp.float32)).astype(jnp.bfloat16)
            rise_buf[:, i * thin : (i + 1) * thin] = value
            if i + 2 < up_cols // thin:
                rise_start(i + 2)
            row = 3 + tensor * (up_cols // features) + (i * thin) // features
            col = (i * thin) % features
            small_land[0, pl.ds(row, 1), col : col + thin] = total_row(value.astype(jnp.float32))
        rise_store(g).start()
        for c in (up_first + 2 * g, up_first + 2 * g + 1):
            right_out(c, rise_buf).start()

    def block_cols(p):
        return pl.ds(pl.multiple_of(p * block, block), block)

    def wide_copy(p, side):
        return local(
            up_w.at[p, :, :, :, pl.ds(side * features, features)], wide_buf.at[side], wide_sem.at[side, 0]
        )

    def hidden_share(p):
        return remote(
            send_buf.at[:, block_cols(p)], hidden_land.at[:, block_cols(p)], hidden_send.at[p],
            hidden_recv.at[p], y_peer,
        )

    def hidden_start():
        for side in range(2):
            wide_copy(0, side).start()

    def hidden_back(first, last):
        @pl.loop(first, last)
        def _(p):
            value = None
            for side in range(2):
                wide_copy(p, side).wait()
                part = contract_cols(
                    rise_buf[:, side * features : (side + 1) * features], flat(wide_buf[side])
                )
                value = part if value is None else value + part

                @pl.when(p + 1 < planes)
                def _():
                    wide_copy(p + 1, side).start()

            acc_buf[:, block_cols(p)] = value
            send_buf[:, block_cols(p)] = value.astype(jnp.bfloat16)
            hidden_share(p).start()

    strip = row_buf.shape[2]

    def row_start(which, i):
        base = tensor if which == 0 else 1 - tensor
        return pl.multiple_of(base * half + i * strip, strip)

    def row_copies(which, i):
        rows = pl.ds(row_start(which, i), strip)
        slot = (which * (half // strip) + i) % 2
        return [
            local(normed_in.at[rows], row_buf.at[slot, 0], row_sem.at[slot, 0]),
            local(second_in.at[rows], row_buf.at[slot, 1], row_sem.at[slot, 1]),
        ]

    strips = [(which, i) for which in range(2) for i in range(half // strip)]

    def norm_start():
        for pair in strips[:2]:
            for copy in row_copies(*pair):
                copy.start()
        local(inverse_in, inverse_buf, load_sem.at[1]).start()

    def norm_back():
        @pl.loop(0, planes)
        def _(p):
            hidden_share(p).wait()

        local(inverse_in, inverse_buf, load_sem.at[1]).wait()
        sums_buf[...] = jnp.zeros_like(sums_buf)
        for at, (which, i) in enumerate(strips):
            for copy in row_copies(which, i):
                copy.wait()

            @pl.loop(0, strip // 16, unroll=2)
            def _(r):
                local_rows = pl.ds(pl.multiple_of(r * 16, 16), 16)
                rows = pl.ds(pl.multiple_of(row_start(which, i) + r * 16, 16), 16)
                normed = row_buf[at % 2, 0, local_rows, :]
                grad_hidden = row_buf[at % 2, 1, local_rows, :] + (
                    acc_buf[rows, :] + hidden_land[rows, :].astype(jnp.float32)
                )
                scaled = grad_hidden * gain_ref[...]
                grad = inverse_buf[rows, 0:1] * (
                    scaled
                    - jnp.mean(scaled, axis=-1, keepdims=True)
                    - normed * jnp.mean(scaled * normed, axis=-1, keepdims=True)
                )
                acc_buf[rows, :] = grad
                low = grad.astype(jnp.bfloat16)
                low_buf[rows, :] = low
                if which == 0:
                    sums_buf[0] += grad_hidden * normed
                    sums_buf[1] += grad_hidden
                    sums_buf[2] += low.astype(jnp.float32)

            if at + 2 < len(strips):
                for copy in row_copies(*strips[at + 2]):
                    copy.start()
        small_land[0, 8:9, :] = total_row(sums_buf[0])
        small_land[0, 9:10, :] = total_row(sums_buf[1])
        small_land[0, 2:3, :] = total_row(sums_buf[2])

    def mixed_start():
        for i in range(2):
            for copy in tile_copy(out_w, i * thin, i):
                copy.start()
        for g in range(up_cols // (2 * JOB)):
            for c in (up_first + 2 * g, up_first + 2 * g + 1):
                right_out(c, rise_buf).wait_send()
        local(qkv_in, rise_buf.at[:, pl.ds(0, 3 * head_cols)], load_sem.at[2]).start()

    def mixed_back():
        for i in range(head_cols // thin):
            for copy in tile_copy(out_w, i * thin, i % 2):
                copy.wait()
            value = jnp.dot(low_buf[...], flat(tile_buf[i % 2]), preferred_element_type=jnp.float32)
            start = 3 * head_cols + i * thin
            rise_buf[:, start : start + thin] = value.astype(jnp.bfloat16)
            if i + 2 < head_cols // thin:
                for copy in tile_copy(out_w, (i + 2) * thin, i % 2):
                    copy.start()

    def attend_back(first, last):
        @pl.loop(first, last)
        def _(h):
            def cols(which):
                return pl.ds(pl.multiple_of(which * head_cols + h * HEAD_DIM, HEAD_DIM), HEAD_DIM)

            key, value = rise_buf[:, cols(1)], rise_buf[:, cols(2)]
            key_sum = value_sum = None
            query_total = jnp.zeros((1, HEAD_DIM), jnp.float32)
            for part in range(2):
                rows = slice(part * half, (part + 1) * half)
                query, grad_mixed = rise_buf[rows, cols(0)], rise_buf[rows, cols(3)]
                scores = contract_cols(query, key) * factor
                scores = jnp.where(mask_ref[0:1, :] > 0.0, scores, MASKED)
                expanded = jnp.exp(scores - jnp.max(scores, axis=1, keepdims=True))
                weight = expanded / jnp.sum(expanded, axis=1, keepdims=True)
                grad_weight = contract_cols(grad_mixed, value)
                inner = jnp.sum(weight * grad_weight, axis=1, keepdims=True)
                grad_scores = (weight * (grad_weight - inner)).astype(jnp.bfloat16)
                grad_value = contract_rows(weight.astype(jnp.bfloat16), grad_mixed)
                grad_key = contract_rows(grad_scores, query)
                grad_query = (
                    jnp.dot(grad_scores, key, preferred_element_type=jnp.float32) * factor
                ).astype(jnp.bfloat16)
                qkv_buf[rows, cols(0)] = grad_query
                query_total += total_row(grad_query.astype(jnp.float32))
                key_sum = grad_key if key_sum is None else key_sum + grad_key
                value_sum = grad_value if value_sum is None else value_sum + grad_value
            qkv_buf[:, cols(1)] = (key_sum * factor).astype(jnp.bfloat16)
            value_low = value_sum.astype(jnp.bfloat16)
            qkv_buf[:, cols(2)] = value_low
            at = pl.ds(pl.multiple_of(tensor * head_cols + h * HEAD_DIM, HEAD_DIM), HEAD_DIM)
            small_land[0, 0:1, at] = query_total
            small_land[0, 1:2, at] = total_row(value_low.astype(jnp.float32))

    def attend_done():
        local(qkv_buf, qkv_own, store_sem.at[4]).start()
        for c in range(qkv_first, total):
            right_out(c, qkv_buf).start()
        input_start(0)

    def input_copies(p):
        return [
            local(query_w.at[p], wide_buf.at[0, :, :, :, pl.ds(0, head_cols)], wide_sem.at[0, 0]),
            local(key_w.at[p], wide_buf.at[0, :, :, :, pl.ds(head_cols, head_cols)], wide_sem.at[0, 1]),
            local(value_w.at[p], wide_buf.at[1, :, :, :, pl.ds(0, head_cols)], wide_sem.at[1, 0]),
        ]

    def input_start(p):
        for copy in input_copies(p):
            copy.start()

    own_rows = pl.ds(pl.multiple_of(tensor * half, half), half)
    other_rows = pl.ds(pl.multiple_of((1 - tensor) * half, half), half)

    def input_share(p):
        return remote(
            send_buf.at[pl.ds(0, half), block_cols(p)], input_land.at[:, block_cols(p)], input_send.at[p],
            input_recv.at[p], y_peer,
        )

    def input_back(first, last):
        @pl.loop(first, last)
        def _(p):
            for copy in input_copies(p):
                copy.wait()
            pair = flat(wide_buf[0])
            single = flat(wide_buf[1, :, :, :, 0:head_cols])

            def share(rows):
                return contract_cols(qkv_buf[rows, 0 : 2 * head_cols], pair) + contract_cols(
                    qkv_buf[rows, 2 * head_cols : 3 * head_cols], single
                )

            send_buf[0:half, block_cols(p)] = share(other_rows).astype(jnp.bfloat16)
            input_share(p).start()
            acc_buf[own_rows, block_cols(p)] += share(own_rows)

            @pl.when(p + 1 < planes)
            def _():
                input_start(p + 1)

    def input_done():
        @pl.loop(0, planes)
        def _(p):
            input_share(p).wait()

        @pl.loop(0, half // 16)
        def _(i):
            rows = pl.ds(pl.multiple_of(tensor * half + i * 16, 16), 16)
            land = pl.ds(pl.multiple_of(i * 16, 16), 16)
            acc_buf[land, :] = acc_buf[rows, :] + input_land[land, :].astype(jnp.float32)

    groups = planes * 4
    index = (plane * 2 + across) * 2 + core
    group = half // groups
    whole, rest, padded, chunks = rest_shape(group)
    rest_width = features // chunks
    back_parts = ((0, whole_buf, whole_out), (1, rest_buf, rest_out))[0 if whole else 1 :]

    def back(which, source, target, k):
        peer = lax.rem(index + k, groups)
        return remote(
            source.at[peer], target.at[index], back_send.at[which, k], back_recv.at[which, k], (peer, tensor)
        )

    def back_own(which, source, target):
        return local(source.at[index], target.at[index], back_recv.at[which, 0])

    def send_back():
        rest_wide[...] = jnp.zeros_like(rest_wide)
        for s in range(groups):
            start = s * group
            if whole:
                whole_buf[s] = acc_buf[start : start + whole, :].astype(jnp.bfloat16)
            for q in range(chunks):
                rest_wide[q * padded : q * padded + rest, :] = acc_buf[
                    start + whole : start + group, q * rest_width : (q + 1) * rest_width
                ]
            rest_buf[s] = rest_wide[...].astype(jnp.bfloat16)
        for part in back_parts:
            back_own(*part).start()
            for k in range(1, groups):
                back(*part, k).start()

    def back_wait():
        for part in back_parts:
            back_own(*part).wait()
            for k in range(1, groups):
                back(*part, k).wait()

    local(down_in, low_buf, load_sem.at[0]).start()
    local(hidden_in, send_buf, load_sem.at[1]).start()
    local(sums_in, sums_buf, load_sem.at[2]).start()
    rise_start(0)
    rise_start(1)
    enter([(lax.rem(index + k, groups), tensor) for k in range(1, groups)] + [y_peer])
    for c in range(up_first):
        right_out(c).start()
    local(down_in, low_buf, load_sem.at[0]).wait()
    turn(0, low_buf)
    small_land[0] = jnp.zeros(small_land.shape[1:], jnp.float32)
    local(sums_in, sums_buf, load_sem.at[2]).wait()
    for i, row in enumerate((10, 11, 7)):
        small_land[0, row : row + 1, :] = total_row(sums_buf[i])
    fetch(0)

    def turn_hidden():
        local(hidden_in, send_buf, load_sem.at[1]).wait()
        turn(1, send_buf)

    def stored():
        for g in range(up_cols // (2 * JOB)):
            rise_store(g).wait()

    def load_input():
        local(x_in, low_buf, load_sem.at[1]).start()

    def turn_input():
        local(x_in, low_buf, load_sem.at[1]).wait()
        turn(3, low_buf)

    def start_out():
        for c in range(out_first, qkv_first):
            right_out(c).start()

    def wait_qkv():
        local(qkv_in, rise_buf.at[:, pl.ds(0, 3 * head_cols)], load_sem.at[2]).wait()

    def store_qkv_wait():
        local(qkv_buf, qkv_own, store_sem.at[4]).wait()

    plan = {
        0: [(rise, 0)],
        1: [(rise, 1)],
        2: [(rise, 2)],
        3: [(rise, 3), (turn_hidden,), (hidden_start,)],
        4: [(hidden_back, 0, planes // 2)],
        5: [(hidden_back, planes // 2, planes), (norm_start,), (start_out,), (stored,)],
        10: [(norm_back,), (mixed_start,)],
        11: [(turn, 2, low_buf), (mixed_back,), (load_input,)],
        12: [(wait_qkv,), (attend_back, 0, heads // 4), (turn_input,)],
        13: [(attend_back, heads // 4, heads // 2)],
        14: [(attend_back, heads // 2, 3 * heads // 4)],
        15: [(attend_back, 3 * heads // 4, heads), (attend_done,)],
        16: [(input_back, 0, planes // 2), (small_begin, 0), (store_qkv_wait,)],
        17: [(input_back, planes // 2, planes), (small_end, 0), (small_begin, 1)],
        18: [(small_end, 1), (small_begin, 2)],
        19: [(small_end, 2), (small_begin, 3)],
        20: [(input_done,), (send_back,), (small_end, 3)],
    }
    for n in range(total + 4):
        if n < total:
            multiply(n)
        for step in plan.get(n, []):
            step[0](*step[1:])
        if 2 <= n < total + 2:
            fold(n - 2)
        if relayed and 3 <= n < total + 3:
            relay(n - 3)
        if n >= 4:
            finish(n - 4)
    local(small_land.at[1], small_out, load_sem.at[0]).wait()
    back_wait()
    left_out(3).wait_send()
    for c in range(total):
        if not up_first <= c < out_first:
            right_out(c).wait_send()
        if c >= total - 3:
            x_out(c).wait_send()
    for c in range(total - 2, total):
        grad_out(c).wait()


def backward(weights, saved, mask, gain):
    planes, _, _, rows, head_cols = weights[0].shape
    up_cols = weights[4].shape[-1]
    tokens, features = saved[0].shape
    total = (2 * up_cols + 4 * head_cols) // JOB
    slots, lands = 8, max(planes - 1, 4)
    thin, strip = 256, 64
    sem, low, high = pltpu.SemaphoreType.DMA, jnp.bfloat16, jnp.float32
    hbm, vmem = pl.BlockSpec(memory_space=pl.ANY), pl.BlockSpec(memory_space=pltpu.VMEM)
    small_rows = 16
    groups = planes * 4
    whole, rest, padded, chunks = rest_shape(tokens // 2 // groups)
    whole_shape = ((groups, whole, features) if whole else (groups, 16, 128), low)
    rest_rows = ((groups, 16, features // chunks), low)
    shapes = (
        [((rows, head_cols), high)] * 4 + [((rows, up_cols), high)] * 2
        + [((small_rows, features), high), whole_shape, rest_rows]
        + [((4, planes, 2, rows, tokens), low)] * 2
        + [((tokens, up_cols), low)] * 3 + [((tokens, head_cols), low)] + [((tokens, 3 * head_cols), low)] * 2
    )
    scratch = [
        ((2, 2, planes, rows, 2 * tokens), low), ((2, 2 * tokens, JOB), low), ((3, 2, planes, rows, JOB), low),
        ((slots, planes, rows, JOB), low), ((slots, lands, rows, JOB), low), ((2, rows, JOB), high),
        ((2, planes, 2, 2, rows, thin), low), ((2, 2, 2, rows, features), low), ((tokens, features), low),
        ((tokens, up_cols), low), ((2, tokens, thin), low), ((tokens, features), high),
        ((tokens, features), low), ((tokens, features), low), ((tokens, 3 * head_cols), low),
        ((planes, 2, 2, rows, tokens), low), ((tokens // 2, features), low), ((2, 2, strip, features), high),
        ((tokens, 128), high), ((3, 16, features), high), ((3 + planes, small_rows, features), high),
        whole_shape, rest_rows, ((16, features // chunks), high),
    ]
    sems = [
        (2, 2, 2), (2, 2), (2,), (total,), (total,), (4,), (4,), (total,), (total,),
        (total, planes - 1), (total, lands), (2 + planes,), (2 + planes,), (2, planes), (2, 2), (2,),
        (4,), (5,), (1,), (planes,), (planes,), (planes,), (planes,), (2, 2), (2, groups), (2, groups),
    ]
    results = pl.pallas_call(
        partial(backward_kernel, planes),
        out_shape=[jax.ShapeDtypeStruct(*shape) for shape in shapes],
        in_specs=[hbm] * 17 + [vmem] * 2,
        out_specs=[hbm] * len(shapes),
        scratch_shapes=[pltpu.VMEM(*shape) for shape in scratch] + [sem(shape) for shape in sems],
        compiler_params=pltpu.CompilerParams(
            collective_id=1, has_side_effects=True, vmem_limit_bytes=62 * 2**20
        ),
        name="backward_scatter",
    )(*weights, *saved, mask, gain)
    whole_rows, rest_rows = results[7], results[8]
    rest_rows = rest_rows.reshape(groups, chunks, padded, features // chunks).transpose(0, 2, 1, 3)
    returned = rest_rows.reshape(groups, padded, features)[:, :rest]
    if whole:
        returned = jnp.concatenate((whole_rows, returned), axis=1)
    return results[:6], results[6], returned


def shards(
    inputs,
    lengths,
    dealing,
    w_query,
    w_key,
    w_value,
    b_query,
    b_value,
    w_out,
    b_out,
    gain_first,
    shift_first,
    w_up,
    b_up,
    w_down,
    b_down,
    gain_second,
    shift_second,
    cotangent,
):
    group_index = lax.axis_index("dp")
    tensor_index = lax.axis_index("tensor")
    ordered = jnp.take(inputs, dealing, axis=0)
    features = cotangent.shape[-1]
    half_rows = cotangent.shape[1]
    seq_len = half_rows * lax.axis_size("tensor")
    length = lengths[dealing[group_index]]
    key_valid = jnp.arange(seq_len) < length
    head_cols = w_query.shape[1]
    up_cols = w_up.shape[1]
    query_bias = lax.dynamic_slice_in_dim(b_query, tensor_index * head_cols, head_cols)
    value_bias = lax.dynamic_slice_in_dim(b_value, tensor_index * head_cols, head_cols)
    up_bias = lax.dynamic_slice_in_dim(b_up, tensor_index * up_cols, up_cols)
    vectors = jnp.concatenate(
        (query_bias, value_bias, b_out, gain_first, shift_first, up_bias, b_down, gain_second, shift_second)
    ).reshape(1, -1)
    mask = jnp.broadcast_to(key_valid.astype(jnp.float32), (8, seq_len))
    weights, saved = forward(
        [w_query, w_key, w_value, w_out.T, w_up, w_down.T],
        ordered.reshape(ordered.shape[0], -1, features), cotangent.reshape(half_rows, features), mask, vectors,
    )
    (
        full_in, _, qkv, mixed_heads, normed_full, inverse_full, full_hidden, active, slope,
        result, full_grad_down, second_full, second_sums,
    ) = saved
    output = result.reshape(cotangent.shape)
    grads, small_total, grad_own = backward(
        weights,
        [
            full_in, qkv, mixed_heads, normed_full, inverse_full, full_hidden, active, slope,
            full_grad_down, second_full, second_sums,
        ],
        mask, gain_first.reshape(1, -1),
    )
    returned = grad_own.reshape(inputs.shape)
    grad_inputs = jnp.zeros_like(returned).at[dealing].set(returned)
    weight_sums = (grads[0], grads[1], grads[2], grads[3].T, grads[4], grads[5].T)
    up_rows = b_up.shape[0] // features
    small_sums = (
        small_total[0], small_total[1], small_total[2], small_total[3 : 3 + up_rows].reshape(-1),
        small_total[7], small_total[8], small_total[9], small_total[10], small_total[11],
    )
    return (
        output,
        grad_inputs,
        weight_sums[0],
        weight_sums[1],
        weight_sums[2],
        small_sums[0],
        small_sums[1],
        weight_sums[3],
        small_sums[2],
        small_sums[5],
        small_sums[6],
        weight_sums[4],
        small_sums[3],
        weight_sums[5],
        small_sums[4],
        small_sums[7],
        small_sums[8],
    )


def solution(mesh):
    in_specs = (
        P(None, "tensor", "dp", None),
        P(),
        P(),
        P("dp", "tensor"),
        P("dp", "tensor"),
        P("dp", "tensor"),
        P(),
        P(),
        P("tensor", "dp"),
        P(),
        P(),
        P(),
        P("dp", "tensor"),
        P(),
        P("tensor", "dp"),
        P(),
        P(),
        P(),
        P("dp", "tensor", None),
    )
    out_specs = (
        P("dp", "tensor", None),
        P(None, "tensor", "dp", None),
        P("dp", "tensor"),
        P("dp", "tensor"),
        P("dp", "tensor"),
        P(),
        P(),
        P("tensor", "dp"),
        P(),
        P(),
        P(),
        P("dp", "tensor"),
        P(),
        P("tensor", "dp"),
        P(),
        P(),
        P(),
    )
    return jax.shard_map(shards, mesh=mesh, in_specs=in_specs, out_specs=out_specs, check_vma=False)
```

```python
from functools import partial

import jax
import jax.numpy as jnp
from jax import lax
from jax.experimental import pallas as pl
from jax.experimental.pallas import tpu as pltpu
from jax.sharding import PartitionSpec as P

HEAD_DIM = 128


EPSILON = 1e-05
MASKED = -1e30


def norm_forward(values, scale_gain, bias_shift):
    center = values - jnp.mean(values, axis=-1, keepdims=True)
    inverse = lax.rsqrt(jnp.mean(center * center, axis=-1, keepdims=True) + EPSILON)
    normed = center * inverse
    return (normed * scale_gain + bias_shift, normed, inverse)


def contract_rows(left, right):
    return lax.dot_general(
        left, right, (((0,), (0,)), ((), ())), preferred_element_type=jnp.float32
    )


def contract_cols(left, right):
    return lax.dot_general(
        left, right, (((1,), (1,)), ((), ())), preferred_element_type=jnp.float32
    )


MESH = pl.DeviceIdType.MESH
TILE = 1024
SLOPE = 0.7978845608028654


def place():
    dp, tensor = lax.axis_index("dp"), lax.axis_index("tensor")
    return dp // 4, (dp // 2) % 2, dp % 2, tensor


def device_of(plane, across, core, tensor):
    return ((plane * 2 + across) * 2 + core, tensor)


def enter(peers):
    barrier = pltpu.get_barrier_semaphore()
    for peer in peers:
        pl.semaphore_signal(barrier, inc=1, device_id=peer, device_id_type=MESH)
    pl.semaphore_wait(barrier, len(peers))


LAG, LEAD, X_FIRST, DEALT, X_LEAD, NORM = 4, (3, 2, 1), (3, 7), 7, 6, 14


def rest_shape(count):
    whole = count // 16 * 16
    rest = count - whole
    padded = 4 if rest <= 4 else 8 if rest <= 8 else 16
    return whole, rest, padded, 16 // padded

def gather_tiles(widths):
    return [(i, start) for i, width in enumerate(widths) for start in range(0, width, TILE)]


def forward_kernel(planes, widths, *refs):
    count = len(widths)
    shard_refs = refs[:count]
    deal_refs = refs[count : count + 2]
    cot_ref, lengths_ref, dealing_ref = refs[count + 2 : count + 5]
    vector_refs = refs[count + 5 : count + 14]
    outs = refs[count + 14 :]
    full_refs = outs[:count]
    (
        x_full, cot_full, qkv_out, mixed_out, normed_out, inverse_out, hidden_out, active_out, slope_out,
        result_out, down_out, second_out, sums_out,
    ) = outs[count : count + 13]
    (
        w_buf, x_buf, qkv_buf, mixed_buf, attn_acc, attn_land, send_buf, hidden_buf, active_buf, slope_buf,
        down_acc, down_land, inverse_buf, result_buf, sums_buf, whole_land, rest_land, vec_buf, mask_buf,
        plane_send, plane_recv, x_send, x_recv, core_send, core_recv, w_sem, in_send, in_recv,
        attn_send, attn_recv, down_send, down_recv, load_sem, store_sem,
        deal_send, deal_recv, vec_sem,
    ) = outs[count + 13 :]
    plane, across, core, tensor = place()
    far = [lax.rem(plane + k, planes) for k in range(planes)]
    x_peer = device_of(plane, 1 - across, core, tensor)
    core_peer = device_of(plane, across, 1 - core, tensor)
    y_peer = device_of(plane, across, core, 1 - tensor)
    plane_peers = [device_of(far[k], across, core, tensor) for k in range(planes)]
    tiles = gather_tiles(widths)
    half, features = cot_ref.shape
    tokens = 2 * half
    block = features // planes
    head_cols = mixed_buf.shape[1]
    factor = HEAD_DIM ** (-0.5)
    own_rows = pl.ds(pl.multiple_of(tensor * half, half), half)

    vec_at, vec_copies = {}, []
    at = 0
    for key, size, part in (
        ("b_query", head_cols, True), ("b_value", head_cols, True), ("b_out", features, False),
        ("gain_first", features, False), ("shift_first", features, False), ("b_up", widths[4], True),
        ("b_down", features, False), ("gain_second", features, False), ("shift_second", features, False),
    ):
        vec_at[key] = at
        start = pl.multiple_of(tensor * size, size) if part else 0
        vec_copies.append(
            pltpu.make_async_copy(
                vector_refs[len(vec_copies)].at[:, pl.ds(start, size)], vec_buf.at[:, pl.ds(at, size)],
                vec_sem.at[len(vec_copies)],
            )
        )
        at += size

    def vector(key, start, size):
        return vec_buf[:, pl.ds(vec_at[key] + start, size)]

    first_down = len(tiles) - widths[5] // TILE
    units = [(c, j) for c in range(first_down) for j in range(planes)]
    units += [(c, j) for j in range(planes) for c in range(first_down, len(tiles))]
    lag = LAG
    relayed = planes == 4
    across_first = X_FIRST if relayed else ()
    low_side = plane < planes // 2
    origins = [
        jnp.where(low_side, lax.rem(plane + j, planes), lax.rem(plane + planes - j, planes)) for j in range(planes)
    ]

    def view(c, *where):
        i, start = tiles[c]
        return full_refs[i].at[(*where, slice(None), pl.ds(start, TILE))]

    def own(c):
        i, start = tiles[c]
        return shard_refs[i].at[:, pl.ds(start, TILE)]

    def own_load(c):
        return pltpu.make_async_copy(own(c), w_buf.at[1, c // 4, (c // 2) % 2, c % 2], plane_recv.at[c, 0])

    def own_store(c):
        return pltpu.make_async_copy(
            w_buf.at[1, c // 4, (c // 2) % 2, c % 2], view(c, plane, across, core), plane_recv.at[c, 0]
        )

    def both(c):
        return slice(None) if c in across_first else across

    def z_copy(c, origin, target, send):
        part = view(c, origin, both(c), core)
        if c not in across_first and send <= 3:
            part = own(c)
        place_there = jnp.where(
            target < planes // 2, lax.rem(origin + planes - target, planes), lax.rem(target + planes - origin, planes)
        )
        return pltpu.make_async_remote_copy(
            part, view(c, origin, both(c), core), plane_send.at[c, send], plane_recv.at[c, place_there],
            device_id=device_of(target, across, core, tensor), device_id_type=MESH,
        )

    middle = jnp.logical_and(plane > 0, plane < planes - 1)

    def z_each(c, act):
        for k in range(1, planes):
            if not relayed:
                act(z_copy(c, plane, far[k], k))
            elif k != 2:
                @pl.when((plane < planes - 1) if k == 1 else (plane > 0))
                def _():
                    act(z_copy(c, plane, far[k], k))

    def z_pass(c, j):
        near_end, far_side = jnp.where(plane == 1, 0, planes - 1), jnp.where(plane == 1, 2, 1)
        return z_copy(c, origins[j], far_side if j == 3 else near_end, 3 + j)

    def z_arrival(c, j):
        part = view(c, origins[j], both(c), core)
        return pltpu.make_async_remote_copy(
            part, part, plane_send.at[c, j], plane_recv.at[c, j], device_id=x_peer, device_id_type=MESH
        )

    def x_copy(c, j, side):
        part = view(c, origins[j], side, core)
        return pltpu.make_async_remote_copy(
            own(c) if j == 0 else part, part, x_send.at[c, j], x_recv.at[c, j], device_id=x_peer,
            device_id_type=MESH,
        )

    def unit_core(u, side):
        c, j = units[u]
        part = view(c, origins[j], slice(None), side)
        return pltpu.make_async_remote_copy(
            part, part, core_send.at[c, j], core_recv.at[c, j], device_id=core_peer, device_id_type=MESH
        )

    lead_own, lead_first, lead_second = LEAD
    z_at, first_at, second_at = {}, {}, {}
    for c in range(len(tiles)):
        for lead, table, ramp in ((lead_own, z_at, c - 1), (lead_first, first_at, c + 1), (lead_second, second_at, c + 2)):
            table.setdefault(max(planes * (c - lead), ramp), []).append(c)

    def z_begin(n):
        for c in z_at.get(n, []):
            if c in across_first:
                x_copy(c, 0, 1 - across).wait_recv()
            z_each(c, lambda copy: copy.start())

    def z_forward(n):
        steps = [(c, (1, 3)) for c in first_at.get(n, [])] + [(c, (2,)) for c in second_at.get(n, [])]
        if relayed and steps:
            @pl.when(middle)
            def _():
                for c, positions in steps:
                    for j in positions:
                        z_arrival(c, j).wait_recv()
                        z_pass(c, j).start()

    def pump(n):
        if n < len(units):
            if n > 0:
                z_begin(n)
            c, j = units[n]
            z_forward(n)
            if j > 0:
                if relayed:
                    pl.when(jnp.logical_not(middle))(z_arrival(c, j).wait_recv)
                else:
                    z_arrival(c, j).wait_recv()
            if c not in across_first:
                if j > 0:
                    x_copy(c, j, across).start()
            if j == 0 and c + X_LEAD < len(tiles) and c + X_LEAD not in across_first:
                x_copy(c + X_LEAD, 0, across).start()
        if n >= lag:
            c, j = units[n - lag]
            if c not in across_first:
                x_copy(c, j, 1 - across).wait_recv()
            unit_core(n - lag, core).start()

    def landed(u):
        unit_core(u, 1 - core).wait_recv()

    def tile_copies(c):
        i, start = tiles[c]
        return [
            pltpu.make_async_copy(
                full_refs[i].at[p, :, :, :, pl.ds(start, TILE)], w_buf.at[c % 2, p], w_sem.at[c % 2, p]
            )
            for p in range(planes)
        ]

    def load_tile(c):
        for u, (tile, _) in enumerate(units):
            if tile == c:
                landed(u)
        for copy in tile_copies(c):
            copy.start()

    def wait_tile(c):
        for copy in tile_copies(c):
            copy.wait()

    def down_copy(k, j):
        c = first_down + j
        return pltpu.make_async_copy(
            view(c, origins[k], slice(None), slice(None)), w_buf.at[k % 2, j], w_sem.at[k % 2, j]
        )

    down_parts = widths[5] // TILE

    def load_down(k):
        for j in range(down_parts):
            landed(units.index((first_down + j, k)))
            down_copy(k, j).start()

    def flat(value):
        return value.reshape(-1, value.shape[-1])

    groups = planes * 4
    index = (plane * 2 + across) * 2 + core
    group = half // groups
    whole, rest, padded, chunks = rest_shape(group)
    rest_width = features // chunks
    deal_parts = ((0, whole_land), (1, rest_land)) if whole else ((1, rest_land),)

    def deal(which, land, k):
        target = lax.rem(index + k, groups)
        return pltpu.make_async_remote_copy(
            deal_refs[which].at[target], land.at[index], deal_send.at[which, k], deal_recv.at[which, k],
            device_id=(target, tensor), device_id_type=MESH,
        )

    def deal_own(which, land):
        return pltpu.make_async_copy(deal_refs[which].at[index], land.at[index], deal_recv.at[which, 0])

    def dealt():
        for which, land in deal_parts:
            deal_own(which, land).wait()
            for k in range(1, groups):
                deal(which, land, k).wait_recv()
        for s in range(groups):
            start = s * group
            if whole:
                attn_acc[start : start + whole, :] = whole_land[s].astype(jnp.float32)
            tail = rest_land[s].astype(jnp.float32)
            for q in range(chunks):
                attn_acc[start + whole : start + group, q * rest_width : (q + 1) * rest_width] = tail[
                    q * padded : q * padded + rest, :
                ]

        @pl.loop(0, half // 16)
        def _(i):
            rows = pl.ds(pl.multiple_of(tensor * half + i * 16, 16), 16)
            x_buf[rows, :] = attn_acc[pl.ds(pl.multiple_of(i * 16, 16), 16), :].astype(jnp.bfloat16)

        exchange(0, x_buf.at[own_rows], x_buf).start()

    def load_x():
        exchange(0, x_buf.at[own_rows], x_buf).wait_recv()
        store(11, x_buf, x_full).start()

    def cot_load():
        other_rows = pl.ds(pl.multiple_of((1 - tensor) * half, half), half)
        return [
            pltpu.make_async_copy(cot_ref, x_buf.at[own_rows], load_sem.at[1]),
            pltpu.make_async_copy(cot_full.at[other_rows], x_buf.at[other_rows], load_sem.at[2]),
        ]

    def exchange(which, source, target):
        return pltpu.make_async_remote_copy(
            source, target.at[own_rows], in_send.at[which], in_recv.at[which],
            device_id=y_peer, device_id_type=MESH,
        )

    def load_cot():
        exchange(1, cot_ref, cot_full).wait_recv()
        for copy in cot_load():
            copy.start()

    def project(c, bias):
        wait_tile(c)

        @pl.loop(0, TILE // 512)
        def _(n):
            cols = pl.ds(pl.multiple_of(n * 512, 512), 512)
            value = jnp.dot(
                x_buf[...], flat(w_buf[c % 2, :, :, :, :, cols]), preferred_element_type=jnp.float32
            )
            if bias is not None:
                value += vec_buf[:, pl.ds(pl.multiple_of(vec_at[bias] + n * 512, 128), 512)]
            qkv_buf[:, pl.ds(pl.multiple_of(c * TILE + n * 512, 512), 512)] = value.astype(jnp.bfloat16)

    def attend(first, last):
        @pl.loop(first, last)
        def _(h):
            def cols(which):
                return pl.ds(pl.multiple_of(which * head_cols + h * HEAD_DIM, HEAD_DIM), HEAD_DIM)

            scores = contract_cols(qkv_buf[:, cols(0)], qkv_buf[:, cols(1)]) * factor
            scores = jnp.where(mask_buf[0:1, :] > 0.0, scores, MASKED)
            expanded = jnp.exp(scores - jnp.max(scores, axis=1, keepdims=True))
            weight = (expanded / jnp.sum(expanded, axis=1, keepdims=True)).astype(jnp.bfloat16)
            mixed_buf[:, cols(0)] = jnp.dot(
                weight, qkv_buf[:, cols(2)], preferred_element_type=jnp.float32
            ).astype(jnp.bfloat16)

    def block_cols(p):
        return pl.ds(pl.multiple_of(p * block, block), block)

    def attn_share(p):
        return pltpu.make_async_remote_copy(
            send_buf.at[:, block_cols(p)], attn_land.at[:, block_cols(p)], attn_send.at[p], attn_recv.at[p],
            device_id=y_peer, device_id_type=MESH,
        )

    def project_out():
        wait_tile(3)

        @pl.loop(0, planes)
        def _(p):
            value = contract_cols(mixed_buf[...], flat(w_buf[1, p]))
            attn_acc[:, block_cols(p)] = value
            send_buf[:, block_cols(p)] = value.astype(jnp.bfloat16)
            attn_share(p).start()

    def first_norm():
        @pl.loop(0, planes)
        def _(p):
            attn_share(p).wait()

        @pl.loop(0, tokens // 16, unroll=4)
        def _(i):
            rows = pl.ds(pl.multiple_of(i * 16, 16), 16)
            value = (
                x_buf[rows, :].astype(jnp.float32)
                + (attn_acc[rows, :] + attn_land[rows, :].astype(jnp.float32))
                + vector("b_out", 0, features)
            )
            hidden, normed, inverse = norm_forward(
                value, vector("gain_first", 0, features), vector("shift_first", 0, features)
            )
            attn_acc[rows, :] = normed
            inverse_buf[rows, :] = jnp.broadcast_to(inverse, (16, 128))
            hidden_buf[rows, :] = hidden.astype(jnp.bfloat16)

        store(0, attn_acc, normed_out).start()
        store(1, inverse_buf, inverse_out).start()
        store(2, hidden_buf, hidden_out).start()
        store(11, x_buf, x_full).wait()
        exchange(0, x_buf.at[own_rows], x_buf).wait_send()
        exchange(1, cot_ref, cot_full).start()

    def store(which, source, target):
        return pltpu.make_async_copy(source, target, store_sem.at[which])

    def slope_store(j):
        return pltpu.make_async_copy(
            slope_buf.at[j % 2], slope_out.at[:, pl.ds(j * TILE, TILE)], store_sem.at[5 + j % 2]
        )

    def raise_up(j):
        c = 4 + j
        wait_tile(c)
        if j >= 2:
            slope_store(j - 2).wait()

        @pl.loop(0, TILE // 256)
        def _(n):
            cols = pl.ds(pl.multiple_of(n * 256, 256), 256)
            value = jnp.dot(
                hidden_buf[...], flat(w_buf[c % 2, :, :, :, :, cols]), preferred_element_type=jnp.float32
            )
            value += vec_buf[:, pl.ds(pl.multiple_of(vec_at["b_up"] + j * TILE + n * 256, 128), 256)]
            square = value * value
            bend = jnp.tanh(SLOPE * value * (1.0 + 0.044715 * square))
            rise = 0.5 * (1.0 + bend)
            active_buf[:, pl.ds(pl.multiple_of(j * TILE + n * 256, 256), 256)] = (value * rise).astype(
                jnp.bfloat16
            )
            slope_buf[j % 2, :, cols] = (
                rise + 0.5 * value * (1.0 - bend * bend) * (SLOPE * (1.0 + 3.0 * 0.044715 * square))
            ).astype(jnp.bfloat16)

        slope_store(j).start()

    def down_share(k):
        cols = block_cols(origins[k])
        return pltpu.make_async_remote_copy(
            send_buf.at[:, cols], down_land.at[:, cols], down_send.at[k], down_recv.at[k],
            device_id=y_peer, device_id_type=MESH,
        )

    def lower(k):
        cols = block_cols(origins[k])
        value = None
        for j in range(down_parts):
            down_copy(k, j).wait()
            part = contract_cols(active_buf[:, j * TILE : (j + 1) * TILE], flat(w_buf[k % 2, j]))
            value = part if value is None else value + part
        down_acc[:, cols] = value
        send_buf[:, cols] = value.astype(jnp.bfloat16)
        down_share(k).start()

    def second_norm():
        for k in range(planes):
            down_share(k).wait()
        for copy in cot_load():
            copy.wait()
        store(2, hidden_buf, hidden_out).wait()
        sums_buf[...] = jnp.zeros_like(sums_buf)
        gain = vector("gain_second", 0, features)

        def rows_of(which, i):
            base = tensor if which == 0 else 1 - tensor
            return pl.ds(pl.multiple_of(base * half + i * 16, 16), 16)

        for which in (0, 1):
            @pl.loop(0, half // 16, unroll=4)
            def _(i):
                rows = rows_of(which, i)
                hidden = attn_acc[rows, :] * vector("gain_first", 0, features) + vector(
                    "shift_first", 0, features
                )
                value = (
                    hidden
                    + (down_acc[rows, :] + down_land[rows, :].astype(jnp.float32))
                    + vector("b_down", 0, features)
                )
                result, normed, inverse = norm_forward(value, gain, vector("shift_second", 0, features))
                grad_out = x_buf[rows, :].astype(jnp.float32)
                scaled = grad_out * gain
                grad = inverse * (
                    scaled
                    - jnp.mean(scaled, axis=-1, keepdims=True)
                    - normed * jnp.mean(scaled * normed, axis=-1, keepdims=True)
                )
                down_acc[rows, :] = grad
                low = grad.astype(jnp.bfloat16)
                hidden_buf[rows, :] = low
                if which == 0:
                    result_buf[pl.ds(pl.multiple_of(i * 16, 16), 16), :] = result.astype(jnp.bfloat16)
                    sums_buf[0] += grad_out * normed
                    sums_buf[1] += grad_out
                    sums_buf[2] += low.astype(jnp.float32)

        for which, source, target in (
            (2, hidden_buf, down_out), (3, down_acc, second_out), (4, result_buf, result_out), (9, sums_buf, sums_out),
        ):
            store(which, source, target).start()

    for c in range(len(tiles)):
        own_load(c).start()
    for copy in vec_copies:
        copy.start()
    for which, land in deal_parts:
        deal_own(which, land).start()
    enter([(lax.rem(index + k, groups), tensor) for k in range(1, groups)] + [y_peer])
    z_begin(-1)
    for c in sorted({*range(X_LEAD), *across_first}):
        x_copy(c, 0, across).start()
    for k in range(1, groups):
        for which, land in deal_parts:
            deal(which, land, k).start()
    z_begin(0)
    for c in range(len(tiles)):
        own_load(c).wait()
        own_store(c).start()
    for c in range(len(tiles)):
        own_store(c).wait()
    for copy in vec_copies:
        copy.wait()
    mask_buf[...] = (
        lax.broadcasted_iota(jnp.int32, mask_buf.shape, 1) < lengths_ref[dealing_ref[index]]
    ).astype(jnp.float32)

    plan = {}

    def at_slot(n, step, *args):
        plan.setdefault(n, []).append((step, args))

    def ready(c):
        return planes * (c + 1) + lag

    heads = head_cols // HEAD_DIM
    at_slot(DEALT, dealt)
    at_slot(ready(0), load_tile, 0)
    at_slot(ready(1), load_tile, 1)
    at_slot(ready(2) - 2, load_x)
    at_slot(ready(2) - 2, project, 0, "b_query")
    at_slot(ready(2) - 1, project, 1, None)
    at_slot(ready(2), load_tile, 2)
    at_slot(ready(2) + 1, project, 2, "b_value")
    begin = ready(2) + 2
    for q in range(4):
        at_slot(begin + q, attend, q * heads // 4, (q + 1) * heads // 4)
    at_slot(begin + 3, load_tile, 3)
    at_slot(begin + 4, project_out)
    norm_slot = begin + 4 + NORM * planes // 4
    at_slot(norm_slot, first_norm)
    at_slot(max(ready(4), begin), load_tile, 4)
    at_slot(max(ready(5), begin + 4), load_tile, 5)
    for j in range(4):
        slot = max(norm_slot + 1 + j, ready(4 + j) + 1)
        at_slot(slot, raise_up, j)
        if j >= 2:
            plan.setdefault(max(norm_slot + 1 + j - 2, ready(4 + j)), []).append((load_tile, (4 + j,)))
    raised = max(norm_slot + 4, ready(7) + 1)
    for k in range(planes):
        slot = planes * first_down + down_parts * (k + 1) + lag
        at_slot(slot, load_down, k)
        at_slot(max(slot + 1, raised), lower, k)
        if k == planes // 2:
            at_slot(slot, load_cot)
    last = max(max(plan), len(units) + lag - 1)
    for n in range(last + 1):
        if n < len(units) + lag:
            pump(n)
        for step, args in plan.get(n, []):
            step(*args)
        if n == begin + 3:
            store(7, qkv_buf, qkv_out).start()
            store(8, mixed_buf, mixed_out).start()
    store(10, active_buf, active_out).start()
    second_norm()
    for which, source, target in (
        (0, attn_acc, normed_out), (1, inverse_buf, inverse_out), (2, hidden_buf, down_out),
        (3, down_acc, second_out), (4, result_buf, result_out), (7, qkv_buf, qkv_out),
        (8, mixed_buf, mixed_out), (9, sums_buf, sums_out), (10, active_buf, active_out),
    ):
        store(which, source, target).wait()
    for j in range(2, 4):
        slope_store(j).wait()
    exchange(1, cot_ref, cot_full).wait_send()
    for which, land in deal_parts:
        for k in range(1, groups):
            deal(which, land, k).wait_send()
    for c in range(len(tiles)):
        z_each(c, lambda copy: copy.wait_send())
        if relayed:
            @pl.when(middle)
            def _():
                for j in range(1, planes):
                    z_pass(c, j).wait_send()
    for u, (c, j) in enumerate(units):
        if c not in across_first or j == 0:
            x_copy(c, j, across).wait_send()
        unit_core(u, core).wait_send()


def forward(shard_list, dealt_rows, cot, lengths, dealing, vectors):
    planes = lax.axis_size("dp") // 4
    widths = [shard.shape[1] for shard in shard_list]
    total = sum(width // TILE for width in widths)
    half, features = cot.shape
    tokens, rows = 2 * half, shard_list[0].shape[0]
    head_cols, up_cols = widths[0], widths[4]
    groups = planes * 4
    whole, rest, padded, chunks = rest_shape(half // groups)
    whole_rows = dealt_rows[:, : max(whole, 16)] if whole else jnp.zeros((groups, 16, 128), jnp.bfloat16)
    rest_rows = jnp.pad(dealt_rows[:, whole:], ((0, 0), (0, padded - rest), (0, 0)))
    rest_rows = rest_rows.reshape(groups, padded, chunks, features // chunks)
    rest_rows = rest_rows.transpose(0, 2, 1, 3).reshape(groups, 16, features // chunks)
    sem, low, high = pltpu.SemaphoreType.DMA, jnp.bfloat16, jnp.float32
    hbm = pl.BlockSpec(memory_space=pl.ANY)
    shapes = [((planes, 2, 2, *shard.shape), low) for shard in shard_list] + [
        ((tokens, features), low), ((tokens, features), low), ((tokens, 3 * head_cols), low),
        ((tokens, head_cols), low), ((tokens, features), high), ((tokens, 128), high),
        ((tokens, features), low), ((tokens, up_cols), low), ((tokens, up_cols), low),
        ((half, features), low), ((tokens, features), low), ((tokens, features), high),
        ((3, 16, features), high),
    ]
    results = pl.pallas_call(
        partial(forward_kernel, planes, widths),
        out_shape=[jax.ShapeDtypeStruct(*shape) for shape in shapes],
        in_specs=[hbm] * (len(shard_list) + 3) + [pl.BlockSpec(memory_space=pltpu.SMEM)] * 2 + [hbm] * len(vectors),
        out_specs=[hbm] * len(shapes),
        scratch_shapes=[
            pltpu.VMEM((2, planes, 2, 2, rows, TILE), low),
            pltpu.VMEM((tokens, features), low),
            pltpu.VMEM((tokens, 3 * head_cols), low),
            pltpu.VMEM((tokens, head_cols), low),
            pltpu.VMEM((tokens, features), high),
            pltpu.VMEM((tokens, features), low),
            pltpu.VMEM((tokens, features), low),
            pltpu.VMEM((tokens, features), low),
            pltpu.VMEM((tokens, up_cols), low),
            pltpu.VMEM((2, tokens, TILE), low),
            pltpu.VMEM((tokens, features), high),
            pltpu.VMEM((tokens, features), low),
            pltpu.VMEM((tokens, 128), high),
            pltpu.VMEM((half, features), low),
            pltpu.VMEM((3, 16, features), high),
            pltpu.VMEM(whole_rows.shape, low),
            pltpu.VMEM(rest_rows.shape, low),
            pltpu.VMEM((1, 2 * head_cols + up_cols + 6 * features), high),
            pltpu.VMEM((8, tokens), high),
            sem((total, max(planes, 7))), *[sem((total, planes))] * 5,
            sem((2, max(planes, 4))), sem((2,)), sem((2,)),
            sem((planes,)), sem((planes,)), sem((planes,)), sem((planes,)), sem((3,)), sem((12,)),
            sem((2, groups)), sem((2, groups)), sem((len(vectors),)),
        ],
        compiler_params=pltpu.CompilerParams(
            collective_id=0, has_side_effects=True, vmem_limit_bytes=62 * 2**20
        ),
        name="forward_gather",
    )(*shard_list, whole_rows, rest_rows, cot, lengths, dealing, *vectors)
    return results[: len(shard_list)], results[len(shard_list) :]


JOB = 512


def backward_kernel(planes, *refs):
    (
        query_w, key_w, value_w, out_w, up_w, down_w,
        x_in, qkv_in, mixed_in, normed_in, inverse_in, hidden_in, active_in, slope_in, down_in, second_in,
        sums_in, lengths_ref, dealing_ref, gain_ref,
    ) = refs[:20]
    (
        grad_query, grad_key, grad_value, grad_out_w, grad_up, grad_down, small_out, whole_out, rest_out,
        left_own, left_far, active_far, rise_own, rise_far, mixed_far, qkv_own, qkv_far,
    ) = refs[20:37]
    (
        left_buf, right_buf, stage, x_land, plane_land, out_buf, tile_buf, wide_buf, low_buf, rise_buf,
        slope_buf, acc_buf, hidden_land, send_buf, qkv_buf, turn_buf, input_land, row_buf, inverse_buf,
        sums_buf, small_land, whole_buf, rest_buf, rest_wide, mask_buf,
        left_sem, right_sem, out_sem, core_send, core_recv, left_send, left_recv, x_send, x_recv,
        plane_send, plane_recv, small_send, small_recv, tile_sem, wide_sem, slope_sem, load_sem, store_sem,
        turn_sem, hidden_send, hidden_recv, input_send, input_recv, row_sem, back_send, back_recv,
    ) = refs[37:]
    plane, across, core, tensor = place()
    far = [lax.rem(plane + k, planes) for k in range(planes)]
    x_peer = device_of(plane, 1 - across, core, tensor)
    core_peer = device_of(plane, across, 1 - core, tensor)
    y_peer = device_of(plane, across, core, 1 - tensor)
    plane_peers = [device_of(far[k], across, core, tensor) for k in range(planes)]
    tokens, features = low_buf.shape
    half = tokens // 2
    head_cols = mixed_in.shape[1]
    heads = head_cols // HEAD_DIM
    up_cols = active_in.shape[1]
    block = features // planes
    factor = HEAD_DIM ** (-0.5)
    slots = x_land.shape[0]
    thin = tile_buf.shape[-1]

    jobs = [(0, active_in, active_far, s, grad_down, s, JOB) for s in range(0, up_cols, JOB)]
    jobs += [(1, rise_own, rise_far, s, grad_up, s, JOB) for s in range(0, up_cols, JOB)]
    jobs += [(2, mixed_in, mixed_far, s, grad_out_w, s, JOB) for s in range(0, head_cols, JOB)]
    for which, result in enumerate((grad_query, grad_key, grad_value)):
        jobs += [
            (3, qkv_own, qkv_far, which * head_cols + s, result, s, JOB) for s in range(0, head_cols, JOB)
        ]
    a, own, other, start, result, at, width = jobs.pop()
    jobs += [(a, own, other, start + s, result, at + s, width // 2) for s in (0, width // 2)]
    total = len(jobs)
    up_first, out_first, qkv_first = (
        [job[0] for job in jobs].index(a) for a in (1, 2, 3)
    )

    def local(source, target, sem):
        return pltpu.make_async_copy(source, target, sem)

    def remote(source, target, send, recv, peer):
        return pltpu.make_async_remote_copy(
            source, target, send, recv, device_id=peer, device_id_type=MESH
        )

    def left_out(a):
        return remote(
            turn_buf.at[:, :, 1 - core], left_far.at[a], left_send.at[a], left_recv.at[a], core_peer
        )

    def left_keep(a):
        return local(turn_buf.at[:, :, core], left_own.at[a], turn_sem.at[0])

    kept = set()

    def left_kept(a):
        if a not in kept:
            kept.add(a)
            left_keep(a).wait()

    def turn(a, source):
        if a > 0:
            left_out(a - 1).wait_send()
            left_kept(a - 1)

        @pl.loop(0, planes)
        def _(p):
            cols = pl.ds(pl.multiple_of(p * block, block), block)
            turn_buf[p] = source[:, cols].T.reshape(turn_buf.shape[1:])

        left_keep(a).start()
        left_out(a).start()

    def right_out(c, source=None):
        _, own, other, start, _, _, width = jobs[c]
        cols = pl.ds(start, width)
        return remote(
            (own if source is None else source).at[:, cols], other.at[:, cols], core_send.at[c],
            core_recv.at[c], core_peer,
        )

    def left_load(a):
        slot = a % 2
        copies = []
        for side in range(2):
            copies.append(
                local(left_own.at[a, :, side], left_buf.at[slot, side, :, :, pl.ds(0, tokens)], left_sem.at[slot, 0, side])
            )
            copies.append(
                local(left_far.at[a, :, side], left_buf.at[slot, side, :, :, pl.ds(tokens, tokens)], left_sem.at[slot, 1, side])
            )
        return copies

    def right_load(c):
        _, own, other, start, _, _, width = jobs[c]
        slot, cols, there = c % 2, pl.ds(start, width), pl.ds(0, width)
        return [
            local(own.at[:, cols], right_buf.at[slot, pl.ds(0, tokens), there], right_sem.at[slot, 0]),
            local(other.at[:, cols], right_buf.at[slot, pl.ds(tokens, tokens), there], right_sem.at[slot, 1]),
        ]

    def used(c):
        return pl.ds(0, jobs[c][-1])

    def x_out(c):
        return remote(
            stage.at[c % 3, 1 - across, :, :, used(c)], x_land.at[c % slots, :, :, used(c)], x_send.at[c], x_recv.at[c], x_peer
        )

    relayed = planes == 4
    middle = jnp.logical_and(plane > 0, plane < planes - 1)

    def plane_out(c, k):
        target, block_at, land = far[k], far[k], k - 1
        if relayed and k == 1:
            end = plane == planes - 1
            target, block_at, land = jnp.where(end, plane - 1, plane + 1), jnp.where(end, 0, plane + 1), jnp.where(end, 3, 0)
        if relayed and k == 3:
            end = plane == 0
            target, block_at, land = jnp.where(end, 1, plane - 1), jnp.where(end, planes - 1, plane - 1), jnp.where(end, 3, 2)
        return remote(
            x_land.at[c % slots, block_at, :, used(c)], plane_land.at[c % slots, land, :, used(c)], plane_send.at[c, k - 1],
            plane_recv.at[c, land], device_of(target, across, core, tensor),
        )

    def plane_in(c, land):
        return remote(
            x_land.at[c % slots, plane, :, used(c)], plane_land.at[c % slots, land, :, used(c)], plane_send.at[c, 0],
            plane_recv.at[c, land], x_peer,
        )

    def relay(c):
        @pl.when(middle)
        def _():
            plane_in(c, 3).wait_recv()
            x_land[c % slots, far[2], :, used(c)] = (
                x_land[c % slots, far[2], :, used(c)].astype(jnp.float32)
                + plane_land[c % slots, 3, :, used(c)].astype(jnp.float32)
            ).astype(jnp.bfloat16)
            plane_out(c, 2).start()

    def grad_out(c):
        _, _, _, _, result, start, width = jobs[c]
        return local(out_buf.at[c % 2, :, used(c)], result.at[:, pl.ds(start, width)], out_sem.at[c % 2])

    def new_left(c):
        return c == 0 or jobs[c - 1][0] != jobs[c][0]

    def fetch(c):
        a = jobs[c][0]
        if new_left(c):
            left_kept(a)
            left_out(a).wait_recv()
            for copy in left_load(a):
                copy.start()
        right_out(c).wait_recv()
        for copy in right_load(c):
            copy.start()

    def multiply(c):
        a = jobs[c][0]
        if new_left(c):
            for copy in left_load(a):
                copy.wait()
        for copy in right_load(c):
            copy.wait()
        if c + 1 < total:
            fetch(c + 1)
        if c >= 3:
            x_out(c - 3).wait_send()

        @pl.loop(0, jobs[c][-1] // 256)
        def _(n):
            cols = pl.ds(pl.multiple_of(n * 256, 256), 256)
            left = left_buf[a % 2]
            result = jnp.dot(
                left.reshape(-1, left.shape[-1]), right_buf[c % 2, :, cols],
                preferred_element_type=jnp.float32,
            ).astype(jnp.bfloat16)
            stage[c % 3, :, :, :, cols] = result.reshape(*left.shape[:-1], 256)

        x_out(c).start()

    def fold(c):
        x_out(c).wait_recv()
        slot = c % slots

        @pl.loop(0, planes)
        def _(p):
            x_land[slot, p, :, used(c)] = (
                x_land[slot, p, :, used(c)].astype(jnp.float32)
                + stage[c % 3, across, p, :, used(c)].astype(jnp.float32)
            ).astype(jnp.bfloat16)

        for k in range(1, planes):
            if relayed and k == 2:
                @pl.when(jnp.logical_not(middle))
                def _():
                    plane_out(c, 2).start()
            else:
                plane_out(c, k).start()

    def finish(c):
        for k in range(1, planes):
            plane_out(c, k).wait_send()
        if c >= 2:
            grad_out(c - 2).wait()
        out_buf[c % 2, :, used(c)] = x_land[c % slots, plane, :, used(c)].astype(jnp.float32)
        for land in range(planes - 1):
            def add():
                plane_in(c, land).wait_recv()
                out_buf[c % 2, :, used(c)] = out_buf[c % 2, :, used(c)] + plane_land[
                    c % slots, land, :, used(c)
                ].astype(jnp.float32)

            if relayed and land != 1:
                pl.when((plane > 0) if land == 0 else (plane < planes - 1))(add)
            else:
                add()
        grad_out(c).start()

    def small_copy(step, peer, slot):
        return remote(
            small_land.at[0], small_land.at[slot], small_send.at[step], small_recv.at[step], peer
        )

    def small_begin(step):
        if step < 3:
            small_copy(step, (core_peer, x_peer, y_peer)[step], 1 + step).start()
        else:
            for k in range(1, planes):
                small_copy(2 + k, plane_peers[k], 3 + k).start()

    def small_end(step):
        if step < 3:
            small_copy(step, core_peer, 1 + step).wait()
            small_land[0] = small_land[0] + small_land[1 + step]
        else:
            for k in range(1, planes):
                small_copy(2 + k, core_peer, 3 + k).wait()
            value = jnp.zeros(small_land.shape[1:], jnp.float32)
            for p in range(planes):
                back = lax.rem(plane + planes - p, planes)
                value += small_land[jnp.where(back == 0, 0, 3 + back)]
            small_land[1] = value
            local(small_land.at[1], small_out, load_sem.at[0]).start()

    def total_row(value):
        return jnp.sum(value, axis=0, keepdims=True)

    def tile_copy(weight, start, slot):
        return [
            local(weight.at[p, :, :, :, pl.ds(start, thin)], tile_buf.at[slot, p], tile_sem.at[slot, p])
            for p in range(planes)
        ]

    def slope_copy(start, slot):
        return local(slope_in.at[:, pl.ds(start, thin)], slope_buf.at[slot], slope_sem.at[slot])

    def flat(value):
        return value.reshape(-1, value.shape[-1])

    def rise_start(i):
        for copy in tile_copy(down_w, i * thin, i % 2):
            copy.start()
        slope_copy(i * thin, i % 2).start()

    def rise_store(g):
        cols = pl.ds(g * 2 * JOB, 2 * JOB)
        return local(rise_buf.at[:, cols], rise_own.at[:, cols], store_sem.at[g])

    def rise(g):
        per = 2 * JOB // thin
        for i in range(g * per, (g + 1) * per):
            for copy in tile_copy(down_w, i * thin, i % 2):
                copy.wait()
            slope_copy(i * thin, i % 2).wait()
            value = jnp.dot(low_buf[...], flat(tile_buf[i % 2]), preferred_element_type=jnp.float32)
            value = (value * slope_buf[i % 2].astype(jnp.float32)).astype(jnp.bfloat16)
            rise_buf[:, i * thin : (i + 1) * thin] = value
            if i + 2 < up_cols // thin:
                rise_start(i + 2)
            row = 3 + tensor * (up_cols // features) + (i * thin) // features
            col = (i * thin) % features
            small_land[0, pl.ds(row, 1), col : col + thin] = total_row(value.astype(jnp.float32))
        rise_store(g).start()
        for c in (up_first + 2 * g, up_first + 2 * g + 1):
            right_out(c, rise_buf).start()

    def block_cols(p):
        return pl.ds(pl.multiple_of(p * block, block), block)

    def wide_copy(p, side):
        return local(
            up_w.at[p, :, :, :, pl.ds(side * features, features)], wide_buf.at[side], wide_sem.at[side, 0]
        )

    def hidden_share(p):
        return remote(
            send_buf.at[:, block_cols(p)], hidden_land.at[:, block_cols(p)], hidden_send.at[p],
            hidden_recv.at[p], y_peer,
        )

    def hidden_start():
        for side in range(2):
            wide_copy(0, side).start()

    def hidden_back(first, last):
        @pl.loop(first, last)
        def _(p):
            value = None
            for side in range(2):
                wide_copy(p, side).wait()
                part = contract_cols(
                    rise_buf[:, side * features : (side + 1) * features], flat(wide_buf[side])
                )
                value = part if value is None else value + part

                @pl.when(p + 1 < planes)
                def _():
                    wide_copy(p + 1, side).start()

            acc_buf[:, block_cols(p)] = value
            send_buf[:, block_cols(p)] = value.astype(jnp.bfloat16)
            hidden_share(p).start()

    strip = row_buf.shape[2]

    def row_start(which, i):
        base = tensor if which == 0 else 1 - tensor
        return pl.multiple_of(base * half + i * strip, strip)

    def row_copies(which, i):
        rows = pl.ds(row_start(which, i), strip)
        slot = (which * (half // strip) + i) % 2
        return [
            local(normed_in.at[rows], row_buf.at[slot, 0], row_sem.at[slot, 0]),
            local(second_in.at[rows], row_buf.at[slot, 1], row_sem.at[slot, 1]),
        ]

    strips = [(which, i) for which in range(2) for i in range(half // strip)]

    def norm_start():
        for pair in strips[:2]:
            for copy in row_copies(*pair):
                copy.start()
        local(inverse_in, inverse_buf, load_sem.at[1]).start()

    def norm_back():
        @pl.loop(0, planes)
        def _(p):
            hidden_share(p).wait()

        local(inverse_in, inverse_buf, load_sem.at[1]).wait()
        sums_buf[...] = jnp.zeros_like(sums_buf)
        for at, (which, i) in enumerate(strips):
            for copy in row_copies(which, i):
                copy.wait()

            @pl.loop(0, strip // 16, unroll=2)
            def _(r):
                local_rows = pl.ds(pl.multiple_of(r * 16, 16), 16)
                rows = pl.ds(pl.multiple_of(row_start(which, i) + r * 16, 16), 16)
                normed = row_buf[at % 2, 0, local_rows, :]
                grad_hidden = row_buf[at % 2, 1, local_rows, :] + (
                    acc_buf[rows, :] + hidden_land[rows, :].astype(jnp.float32)
                )
                scaled = grad_hidden * gain_ref[...]
                grad = inverse_buf[rows, 0:1] * (
                    scaled
                    - jnp.mean(scaled, axis=-1, keepdims=True)
                    - normed * jnp.mean(scaled * normed, axis=-1, keepdims=True)
                )
                acc_buf[rows, :] = grad
                low = grad.astype(jnp.bfloat16)
                low_buf[rows, :] = low
                if which == 0:
                    sums_buf[0] += grad_hidden * normed
                    sums_buf[1] += grad_hidden
                    sums_buf[2] += low.astype(jnp.float32)

            if at + 2 < len(strips):
                for copy in row_copies(*strips[at + 2]):
                    copy.start()
        small_land[0, 8:9, :] = total_row(sums_buf[0])
        small_land[0, 9:10, :] = total_row(sums_buf[1])
        small_land[0, 2:3, :] = total_row(sums_buf[2])

    def mixed_start():
        for i in range(2):
            for copy in tile_copy(out_w, i * thin, i):
                copy.start()
        for g in range(up_cols // (2 * JOB)):
            for c in (up_first + 2 * g, up_first + 2 * g + 1):
                right_out(c, rise_buf).wait_send()
        local(qkv_in, rise_buf.at[:, pl.ds(0, 3 * head_cols)], load_sem.at[2]).start()

    def mixed_back():
        for i in range(head_cols // thin):
            for copy in tile_copy(out_w, i * thin, i % 2):
                copy.wait()
            value = jnp.dot(low_buf[...], flat(tile_buf[i % 2]), preferred_element_type=jnp.float32)
            start = 3 * head_cols + i * thin
            rise_buf[:, start : start + thin] = value.astype(jnp.bfloat16)
            if i + 2 < head_cols // thin:
                for copy in tile_copy(out_w, (i + 2) * thin, i % 2):
                    copy.start()

    def attend_back(first, last):
        @pl.loop(first, last)
        def _(h):
            def cols(which):
                return pl.ds(pl.multiple_of(which * head_cols + h * HEAD_DIM, HEAD_DIM), HEAD_DIM)

            key, value = rise_buf[:, cols(1)], rise_buf[:, cols(2)]
            key_sum = value_sum = None
            query_total = jnp.zeros((1, HEAD_DIM), jnp.float32)
            for part in range(2):
                rows = slice(part * half, (part + 1) * half)
                query, grad_mixed = rise_buf[rows, cols(0)], rise_buf[rows, cols(3)]
                scores = contract_cols(query, key) * factor
                scores = jnp.where(mask_buf[0:1, :] > 0.0, scores, MASKED)
                expanded = jnp.exp(scores - jnp.max(scores, axis=1, keepdims=True))
                weight = expanded / jnp.sum(expanded, axis=1, keepdims=True)
                grad_weight = contract_cols(grad_mixed, value)
                inner = jnp.sum(weight * grad_weight, axis=1, keepdims=True)
                grad_scores = (weight * (grad_weight - inner)).astype(jnp.bfloat16)
                grad_value = contract_rows(weight.astype(jnp.bfloat16), grad_mixed)
                grad_key = contract_rows(grad_scores, query)
                grad_query = (
                    jnp.dot(grad_scores, key, preferred_element_type=jnp.float32) * factor
                ).astype(jnp.bfloat16)
                qkv_buf[rows, cols(0)] = grad_query
                query_total += total_row(grad_query.astype(jnp.float32))
                key_sum = grad_key if key_sum is None else key_sum + grad_key
                value_sum = grad_value if value_sum is None else value_sum + grad_value
            qkv_buf[:, cols(1)] = (key_sum * factor).astype(jnp.bfloat16)
            value_low = value_sum.astype(jnp.bfloat16)
            qkv_buf[:, cols(2)] = value_low
            at = pl.ds(pl.multiple_of(tensor * head_cols + h * HEAD_DIM, HEAD_DIM), HEAD_DIM)
            small_land[0, 0:1, at] = query_total
            small_land[0, 1:2, at] = total_row(value_low.astype(jnp.float32))

    def attend_done():
        local(qkv_buf, qkv_own, store_sem.at[4]).start()
        for c in range(qkv_first, total):
            right_out(c, qkv_buf).start()
        input_start(0)

    def input_copies(p):
        return [
            local(query_w.at[p], wide_buf.at[0, :, :, :, pl.ds(0, head_cols)], wide_sem.at[0, 0]),
            local(key_w.at[p], wide_buf.at[0, :, :, :, pl.ds(head_cols, head_cols)], wide_sem.at[0, 1]),
            local(value_w.at[p], wide_buf.at[1, :, :, :, pl.ds(0, head_cols)], wide_sem.at[1, 0]),
        ]

    def input_start(p):
        for copy in input_copies(p):
            copy.start()

    own_rows = pl.ds(pl.multiple_of(tensor * half, half), half)
    other_rows = pl.ds(pl.multiple_of((1 - tensor) * half, half), half)

    def input_share(p):
        return remote(
            send_buf.at[pl.ds(0, half), block_cols(p)], input_land.at[:, block_cols(p)], input_send.at[p],
            input_recv.at[p], y_peer,
        )

    def input_back(first, last):
        @pl.loop(first, last)
        def _(p):
            for copy in input_copies(p):
                copy.wait()
            pair = flat(wide_buf[0])
            single = flat(wide_buf[1, :, :, :, 0:head_cols])

            def share(rows):
                return contract_cols(qkv_buf[rows, 0 : 2 * head_cols], pair) + contract_cols(
                    qkv_buf[rows, 2 * head_cols : 3 * head_cols], single
                )

            send_buf[0:half, block_cols(p)] = share(other_rows).astype(jnp.bfloat16)
            input_share(p).start()
            acc_buf[own_rows, block_cols(p)] += share(own_rows)

            @pl.when(p + 1 < planes)
            def _():
                input_start(p + 1)

    def input_done():
        @pl.loop(0, planes)
        def _(p):
            input_share(p).wait()

        @pl.loop(0, half // 16)
        def _(i):
            rows = pl.ds(pl.multiple_of(tensor * half + i * 16, 16), 16)
            land = pl.ds(pl.multiple_of(i * 16, 16), 16)
            acc_buf[land, :] = acc_buf[rows, :] + input_land[land, :].astype(jnp.float32)

    groups = planes * 4
    index = (plane * 2 + across) * 2 + core
    group = half // groups
    whole, rest, padded, chunks = rest_shape(group)
    rest_width = features // chunks
    back_parts = ((0, whole_buf, whole_out), (1, rest_buf, rest_out))[0 if whole else 1 :]

    def back(which, source, target, k):
        peer = lax.rem(index + k, groups)
        return remote(
            source.at[peer], target.at[index], back_send.at[which, k], back_recv.at[which, k], (peer, tensor)
        )

    def back_own(which, source, target):
        return local(source.at[index], target.at[index], back_recv.at[which, 0])

    def send_back():
        rest_wide[...] = jnp.zeros_like(rest_wide)
        for s in range(groups):
            start = s * group
            if whole:
                whole_buf[s] = acc_buf[start : start + whole, :].astype(jnp.bfloat16)
            for q in range(chunks):
                rest_wide[q * padded : q * padded + rest, :] = acc_buf[
                    start + whole : start + group, q * rest_width : (q + 1) * rest_width
                ]
            rest_buf[s] = rest_wide[...].astype(jnp.bfloat16)
        for part in back_parts:
            back_own(*part).start()
            for k in range(1, groups):
                back(*part, k).start()

    def back_wait():
        for part in back_parts:
            back_own(*part).wait()
            for k in range(1, groups):
                back(*part, k).wait()

    local(down_in, low_buf, load_sem.at[0]).start()
    local(hidden_in, send_buf, load_sem.at[1]).start()
    local(sums_in, sums_buf, load_sem.at[2]).start()
    rise_start(0)
    rise_start(1)
    enter([(lax.rem(index + k, groups), tensor) for k in range(1, groups)] + [y_peer])
    for c in range(up_first):
        right_out(c).start()
    local(down_in, low_buf, load_sem.at[0]).wait()
    turn(0, low_buf)
    mask_buf[...] = (
        lax.broadcasted_iota(jnp.int32, mask_buf.shape, 1) < lengths_ref[dealing_ref[index]]
    ).astype(jnp.float32)
    small_land[0] = jnp.zeros(small_land.shape[1:], jnp.float32)
    local(sums_in, sums_buf, load_sem.at[2]).wait()
    for i, row in enumerate((10, 11, 7)):
        small_land[0, row : row + 1, :] = total_row(sums_buf[i])
    fetch(0)

    def turn_hidden():
        local(hidden_in, send_buf, load_sem.at[1]).wait()
        turn(1, send_buf)

    def stored():
        for g in range(up_cols // (2 * JOB)):
            rise_store(g).wait()

    def load_input():
        local(x_in, low_buf, load_sem.at[1]).start()

    def turn_input():
        local(x_in, low_buf, load_sem.at[1]).wait()
        turn(3, low_buf)

    def start_out():
        for c in range(out_first, qkv_first):
            right_out(c).start()

    def wait_qkv():
        local(qkv_in, rise_buf.at[:, pl.ds(0, 3 * head_cols)], load_sem.at[2]).wait()

    def store_qkv_wait():
        local(qkv_buf, qkv_own, store_sem.at[4]).wait()

    plan = {
        0: [(rise, 0)],
        1: [(rise, 1)],
        2: [(rise, 2)],
        3: [(rise, 3), (turn_hidden,), (hidden_start,)],
        4: [(hidden_back, 0, planes // 2)],
        5: [(hidden_back, planes // 2, planes), (norm_start,), (start_out,), (stored,)],
        11: [(norm_back,), (mixed_start,)],
        12: [(turn, 2, low_buf), (mixed_back,), (load_input,)],
        13: [(wait_qkv,), (attend_back, 0, heads // 4), (turn_input,)],
        14: [(attend_back, heads // 4, heads // 2)],
        15: [(attend_back, heads // 2, 3 * heads // 4)],
        16: [(attend_back, 3 * heads // 4, heads), (attend_done,), (store_qkv_wait,)],
        17: [(input_back, 0, planes // 2), (small_begin, 0)],
        18: [(input_back, planes // 2, planes), (small_end, 0), (small_begin, 1)],
        19: [(small_end, 1), (small_begin, 2)],
        20: [(small_end, 2), (small_begin, 3)],
        21: [(input_done,), (send_back,), (small_end, 3)],
    }
    for n in range(total + 4):
        if n < total:
            multiply(n)
        for step in plan.get(n, []):
            step[0](*step[1:])
        if 2 <= n < total + 2:
            fold(n - 2)
        if relayed and 3 <= n < total + 3:
            relay(n - 3)
        if n >= 4:
            finish(n - 4)
    local(small_land.at[1], small_out, load_sem.at[0]).wait()
    back_wait()
    left_out(3).wait_send()
    for c in range(total):
        if not up_first <= c < out_first:
            right_out(c).wait_send()
        if c >= total - 3:
            x_out(c).wait_send()
    for c in range(total - 2, total):
        grad_out(c).wait()


def backward(weights, saved, lengths, dealing, gain):
    planes, _, _, rows, head_cols = weights[0].shape
    up_cols = weights[4].shape[-1]
    tokens, features = saved[0].shape
    total = (2 * up_cols + 4 * head_cols) // JOB + 1
    slots, lands = 8, max(planes - 1, 4)
    thin, strip = 256, 64
    sem, low, high = pltpu.SemaphoreType.DMA, jnp.bfloat16, jnp.float32
    hbm, vmem = pl.BlockSpec(memory_space=pl.ANY), pl.BlockSpec(memory_space=pltpu.VMEM)
    small_rows = 16
    groups = planes * 4
    whole, rest, padded, chunks = rest_shape(tokens // 2 // groups)
    whole_shape = ((groups, whole, features) if whole else (groups, 16, 128), low)
    rest_rows = ((groups, 16, features // chunks), low)
    shapes = (
        [((rows, head_cols), high)] * 4 + [((rows, up_cols), high)] * 2
        + [((small_rows, features), high), whole_shape, rest_rows]
        + [((4, planes, 2, rows, tokens), low)] * 2
        + [((tokens, up_cols), low)] * 3 + [((tokens, head_cols), low)] + [((tokens, 3 * head_cols), low)] * 2
    )
    scratch = [
        ((2, 2, planes, rows, 2 * tokens), low), ((2, 2 * tokens, JOB), low), ((3, 2, planes, rows, JOB), low),
        ((slots, planes, rows, JOB), low), ((slots, lands, rows, JOB), low), ((2, rows, JOB), high),
        ((2, planes, 2, 2, rows, thin), low), ((2, 2, 2, rows, features), low), ((tokens, features), low),
        ((tokens, up_cols), low), ((2, tokens, thin), low), ((tokens, features), high),
        ((tokens, features), low), ((tokens, features), low), ((tokens, 3 * head_cols), low),
        ((planes, 2, 2, rows, tokens), low), ((tokens // 2, features), low), ((2, 2, strip, features), high),
        ((tokens, 128), high), ((3, 16, features), high), ((3 + planes, small_rows, features), high),
        whole_shape, rest_rows, ((16, features // chunks), high), ((8, tokens), high),
    ]
    sems = [
        (2, 2, 2), (2, 2), (2,), (total,), (total,), (4,), (4,), (total,), (total,),
        (total, planes - 1), (total, lands), (2 + planes,), (2 + planes,), (2, planes), (2, 2), (2,),
        (4,), (5,), (1,), (planes,), (planes,), (planes,), (planes,), (2, 2), (2, groups), (2, groups),
    ]
    results = pl.pallas_call(
        partial(backward_kernel, planes),
        out_shape=[jax.ShapeDtypeStruct(*shape) for shape in shapes],
        in_specs=[hbm] * 17 + [pl.BlockSpec(memory_space=pltpu.SMEM)] * 2 + [vmem],
        out_specs=[hbm] * len(shapes),
        scratch_shapes=[pltpu.VMEM(*shape) for shape in scratch] + [sem(shape) for shape in sems],
        compiler_params=pltpu.CompilerParams(
            collective_id=1, has_side_effects=True, vmem_limit_bytes=62 * 2**20
        ),
        name="backward_scatter",
    )(*weights, *saved, lengths, dealing, gain)
    whole_rows, rest_rows = results[7], results[8]
    rest_rows = rest_rows.reshape(groups, chunks, padded, features // chunks).transpose(0, 2, 1, 3)
    returned = rest_rows.reshape(groups, padded, features)[:, :rest]
    if whole:
        returned = jnp.concatenate((whole_rows, returned), axis=1)
    return results[:6], results[6], returned


def shards(
    inputs,
    lengths,
    dealing,
    w_query,
    w_key,
    w_value,
    b_query,
    b_value,
    w_out,
    b_out,
    gain_first,
    shift_first,
    w_up,
    b_up,
    w_down,
    b_down,
    gain_second,
    shift_second,
    cotangent,
):
    ordered = inputs.at[dealing].get(mode="promise_in_bounds", unique_indices=True)
    features = cotangent.shape[-1]
    half_rows = cotangent.shape[1]
    vectors = [
        vector.reshape(1, -1)
        for vector in (
            b_query, b_value, b_out, gain_first, shift_first, b_up, b_down, gain_second, shift_second,
        )
    ]
    weights, saved = forward(
        [w_query, w_key, w_value, w_out.T, w_up, w_down.T],
        ordered.reshape(ordered.shape[0], -1, features), cotangent.reshape(half_rows, features), lengths, dealing, vectors,
    )
    (
        full_in, _, qkv, mixed_heads, normed_full, inverse_full, full_hidden, active, slope,
        result, full_grad_down, second_full, second_sums,
    ) = saved
    output = result.reshape(cotangent.shape)
    grads, small_total, grad_own = backward(
        weights,
        [
            full_in, qkv, mixed_heads, normed_full, inverse_full, full_hidden, active, slope,
            full_grad_down, second_full, second_sums,
        ],
        lengths, dealing, gain_first.reshape(1, -1),
    )
    returned = grad_own.reshape(inputs.shape)
    grad_inputs = jnp.zeros_like(returned).at[dealing].set(returned)
    weight_sums = (grads[0], grads[1], grads[2], grads[3].T, grads[4], grads[5].T)
    up_rows = b_up.shape[0] // features
    small_sums = (
        small_total[0], small_total[1], small_total[2], small_total[3 : 3 + up_rows].reshape(-1),
        small_total[7], small_total[8], small_total[9], small_total[10], small_total[11],
    )
    return (
        output,
        grad_inputs,
        weight_sums[0],
        weight_sums[1],
        weight_sums[2],
        small_sums[0],
        small_sums[1],
        weight_sums[3],
        small_sums[2],
        small_sums[5],
        small_sums[6],
        weight_sums[4],
        small_sums[3],
        weight_sums[5],
        small_sums[4],
        small_sums[7],
        small_sums[8],
    )


def solution(mesh):
    in_specs = (
        P(None, "tensor", "dp", None),
        P(),
        P(),
        P("dp", "tensor"),
        P("dp", "tensor"),
        P("dp", "tensor"),
        P(),
        P(),
        P("tensor", "dp"),
        P(),
        P(),
        P(),
        P("dp", "tensor"),
        P(),
        P("tensor", "dp"),
        P(),
        P(),
        P(),
        P("dp", "tensor", None),
    )
    out_specs = (
        P("dp", "tensor", None),
        P(None, "tensor", "dp", None),
        P("dp", "tensor"),
        P("dp", "tensor"),
        P("dp", "tensor"),
        P(),
        P(),
        P("tensor", "dp"),
        P(),
        P(),
        P(),
        P("dp", "tensor"),
        P(),
        P("tensor", "dp"),
        P(),
        P(),
        P(),
    )
    return jax.shard_map(shards, mesh=mesh, in_specs=in_specs, out_specs=out_specs, check_vma=False)
```

```python
from functools import partial

import jax
import jax.numpy as jnp
from jax import lax
from jax.experimental import pallas as pl
from jax.experimental.pallas import tpu as pltpu
from jax.sharding import PartitionSpec as P

HEAD_DIM = 128


EPSILON = 1e-05
MASKED = -1e30


def norm_forward(values, scale_gain, bias_shift):
    center = values - jnp.mean(values, axis=-1, keepdims=True)
    inverse = lax.rsqrt(jnp.mean(center * center, axis=-1, keepdims=True) + EPSILON)
    normed = center * inverse
    return (normed * scale_gain + bias_shift, normed, inverse)


def contract_rows(left, right):
    return lax.dot_general(
        left, right, (((0,), (0,)), ((), ())), preferred_element_type=jnp.float32
    )


def contract_cols(left, right):
    return lax.dot_general(
        left, right, (((1,), (1,)), ((), ())), preferred_element_type=jnp.float32
    )


MESH = pl.DeviceIdType.MESH
TILE = 1024
SLOPE = 0.7978845608028654


def place():
    dp, tensor = lax.axis_index("dp"), lax.axis_index("tensor")
    return dp // 4, (dp // 2) % 2, dp % 2, tensor


def device_of(plane, across, core, tensor):
    return ((plane * 2 + across) * 2 + core, tensor)


def enter(peers):
    barrier = pltpu.get_barrier_semaphore()
    for peer in peers:
        pl.semaphore_signal(barrier, inc=1, device_id=peer, device_id_type=MESH)
    pl.semaphore_wait(barrier, len(peers))


LAG, LEAD, X_FIRST, DEALT, X_LEAD, NORM = 4, (3, 2, 1), (3, 7), 8, 6, 14


def rest_shape(count):
    whole = count // 16 * 16
    rest = count - whole
    padded = 4 if rest <= 4 else 8 if rest <= 8 else 16
    return whole, rest, padded, 16 // padded

def gather_tiles(widths):
    return [(i, start) for i, width in enumerate(widths) for start in range(0, width, TILE)]


def forward_kernel(planes, widths, *refs):
    count = len(widths)
    shard_refs = refs[:count]
    deal_refs = refs[count : count + 2]
    cot_ref, lengths_ref, dealing_ref = refs[count + 2 : count + 5]
    vector_refs = refs[count + 5 : count + 14]
    outs = refs[count + 14 :]
    full_refs = outs[:count]
    (
        x_full, cot_full, qkv_out, mixed_out, normed_out, inverse_out, hidden_out, active_out, slope_out,
        result_out, down_out, second_out, sums_out,
    ) = outs[count : count + 13]
    (
        w_buf, x_buf, qkv_buf, mixed_buf, attn_acc, attn_land, send_buf, hidden_buf, active_buf, slope_buf,
        down_acc, down_land, inverse_buf, result_buf, sums_buf, whole_land, rest_land, vec_buf, mask_buf,
        plane_send, plane_recv, x_send, x_recv, core_send, core_recv, w_sem, in_send, in_recv,
        attn_send, attn_recv, down_send, down_recv, load_sem, store_sem,
        deal_send, deal_recv, vec_sem,
    ) = outs[count + 13 :]
    plane, across, core, tensor = place()
    far = [lax.rem(plane + k, planes) for k in range(planes)]
    x_peer = device_of(plane, 1 - across, core, tensor)
    core_peer = device_of(plane, across, 1 - core, tensor)
    y_peer = device_of(plane, across, core, 1 - tensor)
    plane_peers = [device_of(far[k], across, core, tensor) for k in range(planes)]
    tiles = gather_tiles(widths)
    half, features = cot_ref.shape
    tokens = 2 * half
    block = features // planes
    head_cols = mixed_buf.shape[1]
    factor = HEAD_DIM ** (-0.5)
    own_rows = pl.ds(pl.multiple_of(tensor * half, half), half)

    vec_at, vec_copies = {}, []
    at = 0
    for key, size, part in (
        ("b_query", head_cols, True), ("b_value", head_cols, True), ("b_out", features, False),
        ("gain_first", features, False), ("shift_first", features, False), ("b_up", widths[4], True),
        ("b_down", features, False), ("gain_second", features, False), ("shift_second", features, False),
    ):
        vec_at[key] = at
        start = pl.multiple_of(tensor * size, size) if part else 0
        vec_copies.append(
            pltpu.make_async_copy(
                vector_refs[len(vec_copies)].at[:, pl.ds(start, size)], vec_buf.at[:, pl.ds(at, size)],
                vec_sem.at[len(vec_copies)],
            )
        )
        at += size

    def vector(key, start, size):
        return vec_buf[:, pl.ds(vec_at[key] + start, size)]

    first_down = len(tiles) - widths[5] // TILE
    units = [(c, j) for c in range(first_down) for j in range(planes)]
    units += [(c, j) for j in range(planes) for c in range(first_down, len(tiles))]
    lag = LAG
    relayed = planes == 4
    across_first = X_FIRST if relayed else ()
    low_side = plane < planes // 2
    origins = [
        jnp.where(low_side, lax.rem(plane + j, planes), lax.rem(plane + planes - j, planes)) for j in range(planes)
    ]

    def view(c, *where):
        i, start = tiles[c]
        return full_refs[i].at[(*where, slice(None), pl.ds(start, TILE))]

    def own(c):
        i, start = tiles[c]
        return shard_refs[i].at[:, pl.ds(start, TILE)]

    def own_load(c):
        return pltpu.make_async_copy(own(c), w_buf.at[1, c // 4, (c // 2) % 2, c % 2], plane_recv.at[c, 0])

    def own_store(c):
        return pltpu.make_async_copy(
            w_buf.at[1, c // 4, (c // 2) % 2, c % 2], view(c, plane, across, core), plane_recv.at[c, 0]
        )

    def both(c):
        return slice(None) if c in across_first else across

    def z_copy(c, origin, target, send):
        part = view(c, origin, both(c), core)
        if c not in across_first and send <= 3:
            part = own(c)
        place_there = jnp.where(
            target < planes // 2, lax.rem(origin + planes - target, planes), lax.rem(target + planes - origin, planes)
        )
        return pltpu.make_async_remote_copy(
            part, view(c, origin, both(c), core), plane_send.at[c, send], plane_recv.at[c, place_there],
            device_id=device_of(target, across, core, tensor), device_id_type=MESH,
        )

    middle = jnp.logical_and(plane > 0, plane < planes - 1)

    def z_each(c, act):
        for k in range(1, planes):
            if not relayed:
                act(z_copy(c, plane, far[k], k))
            elif k != 2:
                @pl.when((plane < planes - 1) if k == 1 else (plane > 0))
                def _():
                    act(z_copy(c, plane, far[k], k))

    def z_pass(c, j):
        near_end, far_side = jnp.where(plane == 1, 0, planes - 1), jnp.where(plane == 1, 2, 1)
        return z_copy(c, origins[j], far_side if j == 3 else near_end, 3 + j)

    def z_arrival(c, j):
        part = view(c, origins[j], both(c), core)
        return pltpu.make_async_remote_copy(
            part, part, plane_send.at[c, j], plane_recv.at[c, j], device_id=x_peer, device_id_type=MESH
        )

    def x_copy(c, j, side):
        part = view(c, origins[j], side, core)
        return pltpu.make_async_remote_copy(
            own(c) if j == 0 else part, part, x_send.at[c, j], x_recv.at[c, j], device_id=x_peer,
            device_id_type=MESH,
        )

    def unit_core(u, side):
        c, j = units[u]
        part = view(c, origins[j], slice(None), side)
        return pltpu.make_async_remote_copy(
            part, part, core_send.at[c, j], core_recv.at[c, j], device_id=core_peer, device_id_type=MESH
        )

    lead_own, lead_first, lead_second = LEAD
    z_at, first_at, second_at = {}, {}, {}
    for c in range(len(tiles)):
        for lead, table, ramp in ((lead_own, z_at, c - 1), (lead_first, first_at, c + 1), (lead_second, second_at, c + 2)):
            table.setdefault(max(planes * (c - lead), ramp), []).append(c)

    def z_begin(n):
        for c in z_at.get(n, []):
            if c in across_first:
                x_copy(c, 0, 1 - across).wait_recv()
            z_each(c, lambda copy: copy.start())

    def z_forward(n):
        steps = [(c, (1, 3)) for c in first_at.get(n, [])] + [(c, (2,)) for c in second_at.get(n, [])]
        if relayed and steps:
            @pl.when(middle)
            def _():
                for c, positions in steps:
                    for j in positions:
                        z_arrival(c, j).wait_recv()
                        z_pass(c, j).start()

    def pump(n):
        if n < len(units):
            if n > 0:
                z_begin(n)
            c, j = units[n]
            z_forward(n)
            if j > 0:
                if relayed:
                    pl.when(jnp.logical_not(middle))(z_arrival(c, j).wait_recv)
                else:
                    z_arrival(c, j).wait_recv()
            if c not in across_first:
                if j > 0:
                    x_copy(c, j, across).start()
            if j == 0 and c + X_LEAD < len(tiles) and c + X_LEAD not in across_first:
                x_copy(c + X_LEAD, 0, across).start()
        if n >= lag:
            c, j = units[n - lag]
            if c not in across_first:
                x_copy(c, j, 1 - across).wait_recv()
            unit_core(n - lag, core).start()

    def landed(u):
        unit_core(u, 1 - core).wait_recv()

    def tile_copies(c):
        i, start = tiles[c]
        return [
            pltpu.make_async_copy(
                full_refs[i].at[p, :, :, :, pl.ds(start, TILE)], w_buf.at[c % 2, p], w_sem.at[c % 2, p]
            )
            for p in range(planes)
        ]

    def load_tile(c):
        for u, (tile, _) in enumerate(units):
            if tile == c:
                landed(u)
        for copy in tile_copies(c):
            copy.start()

    def wait_tile(c):
        for copy in tile_copies(c):
            copy.wait()

    def down_copy(k, j):
        c = first_down + j
        return pltpu.make_async_copy(
            view(c, origins[k], slice(None), slice(None)), w_buf.at[k % 2, j], w_sem.at[k % 2, j]
        )

    down_parts = widths[5] // TILE

    def load_down(k):
        for j in range(down_parts):
            landed(units.index((first_down + j, k)))
            down_copy(k, j).start()

    def flat(value):
        return value.reshape(-1, value.shape[-1])

    groups = planes * 4
    index = (plane * 2 + across) * 2 + core
    group = half // groups
    whole, rest, padded, chunks = rest_shape(group)
    rest_width = features // chunks
    deal_parts = ((0, whole_land), (1, rest_land)) if whole else ((1, rest_land),)

    def deal(which, land, k):
        target = lax.rem(index + k, groups)
        return pltpu.make_async_remote_copy(
            deal_refs[which].at[target], land.at[index], deal_send.at[which, k], deal_recv.at[which, k],
            device_id=(target, tensor), device_id_type=MESH,
        )

    def deal_own(which, land):
        return pltpu.make_async_copy(deal_refs[which].at[index], land.at[index], deal_recv.at[which, 0])

    def deal_some(i):
        for k in range(1 + i, groups, 5):
            for which, land in deal_parts:
                deal(which, land, k).start()

    def dealt():
        for which, land in deal_parts:
            deal_own(which, land).wait()
            for k in range(1, groups):
                deal(which, land, k).wait_recv()
        for s in range(groups):
            start = s * group
            if whole:
                attn_acc[start : start + whole, :] = whole_land[s].astype(jnp.float32)
            tail = rest_land[s].astype(jnp.float32)
            for q in range(chunks):
                attn_acc[start + whole : start + group, q * rest_width : (q + 1) * rest_width] = tail[
                    q * padded : q * padded + rest, :
                ]

        @pl.loop(0, half // 16)
        def _(i):
            rows = pl.ds(pl.multiple_of(tensor * half + i * 16, 16), 16)
            x_buf[rows, :] = attn_acc[pl.ds(pl.multiple_of(i * 16, 16), 16), :].astype(jnp.bfloat16)

        exchange(0, x_buf.at[own_rows], x_buf).start()

    def load_x():
        exchange(0, x_buf.at[own_rows], x_buf).wait_recv()
        store(11, x_buf, x_full).start()

    def cot_load():
        other_rows = pl.ds(pl.multiple_of((1 - tensor) * half, half), half)
        return [
            pltpu.make_async_copy(cot_ref, x_buf.at[own_rows], load_sem.at[1]),
            pltpu.make_async_copy(cot_full.at[other_rows], x_buf.at[other_rows], load_sem.at[2]),
        ]

    def exchange(which, source, target):
        return pltpu.make_async_remote_copy(
            source, target.at[own_rows], in_send.at[which], in_recv.at[which],
            device_id=y_peer, device_id_type=MESH,
        )

    def load_cot():
        exchange(1, cot_ref, cot_full).wait_recv()
        for copy in cot_load():
            copy.start()

    def project(c, bias):
        wait_tile(c)

        @pl.loop(0, TILE // 512)
        def _(n):
            cols = pl.ds(pl.multiple_of(n * 512, 512), 512)
            value = jnp.dot(
                x_buf[...], flat(w_buf[c % 2, :, :, :, :, cols]), preferred_element_type=jnp.float32
            )
            if bias is not None:
                value += vec_buf[:, pl.ds(pl.multiple_of(vec_at[bias] + n * 512, 128), 512)]
            qkv_buf[:, pl.ds(pl.multiple_of(c * TILE + n * 512, 512), 512)] = value.astype(jnp.bfloat16)

    def attend(first, last):
        @pl.loop(first, last)
        def _(h):
            def cols(which):
                return pl.ds(pl.multiple_of(which * head_cols + h * HEAD_DIM, HEAD_DIM), HEAD_DIM)

            scores = contract_cols(qkv_buf[:, cols(0)], qkv_buf[:, cols(1)]) * factor
            scores = jnp.where(mask_buf[0:1, :] > 0.0, scores, MASKED)
            expanded = jnp.exp(scores - jnp.max(scores, axis=1, keepdims=True))
            weight = (expanded / jnp.sum(expanded, axis=1, keepdims=True)).astype(jnp.bfloat16)
            mixed_buf[:, cols(0)] = jnp.dot(
                weight, qkv_buf[:, cols(2)], preferred_element_type=jnp.float32
            ).astype(jnp.bfloat16)

    def block_cols(p):
        return pl.ds(pl.multiple_of(p * block, block), block)

    def attn_share(p):
        return pltpu.make_async_remote_copy(
            send_buf.at[:, block_cols(p)], attn_land.at[:, block_cols(p)], attn_send.at[p], attn_recv.at[p],
            device_id=y_peer, device_id_type=MESH,
        )

    def project_out():
        wait_tile(3)

        @pl.loop(0, planes)
        def _(p):
            value = contract_cols(mixed_buf[...], flat(w_buf[1, p]))
            attn_acc[:, block_cols(p)] = value
            send_buf[:, block_cols(p)] = value.astype(jnp.bfloat16)
            attn_share(p).start()

    def first_norm():
        @pl.loop(0, planes)
        def _(p):
            attn_share(p).wait()

        @pl.loop(0, tokens // 16, unroll=4)
        def _(i):
            rows = pl.ds(pl.multiple_of(i * 16, 16), 16)
            value = (
                x_buf[rows, :].astype(jnp.float32)
                + (attn_acc[rows, :] + attn_land[rows, :].astype(jnp.float32))
                + vector("b_out", 0, features)
            )
            hidden, normed, inverse = norm_forward(
                value, vector("gain_first", 0, features), vector("shift_first", 0, features)
            )
            attn_acc[rows, :] = normed
            inverse_buf[rows, :] = jnp.broadcast_to(inverse, (16, 128))
            hidden_buf[rows, :] = hidden.astype(jnp.bfloat16)

        store(0, attn_acc, normed_out).start()
        store(1, inverse_buf, inverse_out).start()
        store(2, hidden_buf, hidden_out).start()
        store(11, x_buf, x_full).wait()
        exchange(0, x_buf.at[own_rows], x_buf).wait_send()
        exchange(1, cot_ref, cot_full).start()

    def store(which, source, target):
        return pltpu.make_async_copy(source, target, store_sem.at[which])

    def slope_store(j):
        return pltpu.make_async_copy(
            slope_buf.at[j % 2], slope_out.at[:, pl.ds(j * TILE, TILE)], store_sem.at[5 + j % 2]
        )

    def raise_up(j):
        c = 4 + j
        wait_tile(c)
        if j >= 2:
            slope_store(j - 2).wait()

        @pl.loop(0, TILE // 256)
        def _(n):
            cols = pl.ds(pl.multiple_of(n * 256, 256), 256)
            value = jnp.dot(
                hidden_buf[...], flat(w_buf[c % 2, :, :, :, :, cols]), preferred_element_type=jnp.float32
            )
            value += vec_buf[:, pl.ds(pl.multiple_of(vec_at["b_up"] + j * TILE + n * 256, 128), 256)]
            square = value * value
            bend = jnp.tanh(SLOPE * value * (1.0 + 0.044715 * square))
            rise = 0.5 * (1.0 + bend)
            active_buf[:, pl.ds(pl.multiple_of(j * TILE + n * 256, 256), 256)] = (value * rise).astype(
                jnp.bfloat16
            )
            slope_buf[j % 2, :, cols] = (
                rise + 0.5 * value * (1.0 - bend * bend) * (SLOPE * (1.0 + 3.0 * 0.044715 * square))
            ).astype(jnp.bfloat16)

        slope_store(j).start()

    def down_share(k):
        cols = block_cols(origins[k])
        return pltpu.make_async_remote_copy(
            send_buf.at[:, cols], down_land.at[:, cols], down_send.at[k], down_recv.at[k],
            device_id=y_peer, device_id_type=MESH,
        )

    def lower(k):
        cols = block_cols(origins[k])
        value = None
        for j in range(down_parts):
            down_copy(k, j).wait()
            part = contract_cols(active_buf[:, j * TILE : (j + 1) * TILE], flat(w_buf[k % 2, j]))
            value = part if value is None else value + part
        down_acc[:, cols] = value
        send_buf[:, cols] = value.astype(jnp.bfloat16)
        down_share(k).start()

    def second_norm():
        for k in range(planes):
            down_share(k).wait()
        for copy in cot_load():
            copy.wait()
        store(2, hidden_buf, hidden_out).wait()
        sums_buf[...] = jnp.zeros_like(sums_buf)
        gain = vector("gain_second", 0, features)

        def rows_of(which, i):
            base = tensor if which == 0 else 1 - tensor
            return pl.ds(pl.multiple_of(base * half + i * 16, 16), 16)

        for which in (0, 1):
            @pl.loop(0, half // 16, unroll=4)
            def _(i):
                rows = rows_of(which, i)
                hidden = attn_acc[rows, :] * vector("gain_first", 0, features) + vector(
                    "shift_first", 0, features
                )
                value = (
                    hidden
                    + (down_acc[rows, :] + down_land[rows, :].astype(jnp.float32))
                    + vector("b_down", 0, features)
                )
                result, normed, inverse = norm_forward(value, gain, vector("shift_second", 0, features))
                grad_out = x_buf[rows, :].astype(jnp.float32)
                scaled = grad_out * gain
                grad = inverse * (
                    scaled
                    - jnp.mean(scaled, axis=-1, keepdims=True)
                    - normed * jnp.mean(scaled * normed, axis=-1, keepdims=True)
                )
                down_acc[rows, :] = grad
                low = grad.astype(jnp.bfloat16)
                hidden_buf[rows, :] = low
                if which == 0:
                    result_buf[pl.ds(pl.multiple_of(i * 16, 16), 16), :] = result.astype(jnp.bfloat16)
                    sums_buf[0] += grad_out * normed
                    sums_buf[1] += grad_out
                    sums_buf[2] += low.astype(jnp.float32)

        for which, source, target in (
            (2, hidden_buf, down_out), (3, down_acc, second_out), (4, result_buf, result_out), (9, sums_buf, sums_out),
        ):
            store(which, source, target).start()

    for c in range(len(tiles)):
        own_load(c).start()
    for copy in vec_copies:
        copy.start()
    for which, land in deal_parts:
        deal_own(which, land).start()
    enter([(lax.rem(index + k, groups), tensor) for k in range(1, groups)] + [y_peer])
    z_begin(-1)
    for c in sorted({*range(X_LEAD), *across_first}):
        x_copy(c, 0, across).start()
    deal_some(0)
    z_begin(0)
    for c in range(len(tiles)):
        own_load(c).wait()
        own_store(c).start()
    for c in range(len(tiles)):
        own_store(c).wait()
    for copy in vec_copies:
        copy.wait()
    mask_buf[...] = (
        lax.broadcasted_iota(jnp.int32, mask_buf.shape, 1) < lengths_ref[dealing_ref[index]]
    ).astype(jnp.float32)

    plan = {}

    def at_slot(n, step, *args):
        plan.setdefault(n, []).append((step, args))

    def ready(c):
        return planes * (c + 1) + lag

    heads = head_cols // HEAD_DIM
    for i in range(1, 5):
        at_slot(i, deal_some, i)
    at_slot(DEALT, dealt)
    at_slot(ready(0), load_tile, 0)
    at_slot(ready(1), load_tile, 1)
    at_slot(ready(2) - 2, load_x)
    at_slot(ready(2) - 2, project, 0, "b_query")
    at_slot(ready(2) - 1, project, 1, None)
    at_slot(ready(2), load_tile, 2)
    at_slot(ready(2) + 1, project, 2, "b_value")
    begin = ready(2) + 2
    for q in range(4):
        at_slot(begin + q, attend, q * heads // 4, (q + 1) * heads // 4)
    at_slot(begin + 3, load_tile, 3)
    at_slot(begin + 4, project_out)
    norm_slot = begin + 4 + NORM * planes // 4
    at_slot(norm_slot, first_norm)
    at_slot(max(ready(4), begin), load_tile, 4)
    at_slot(max(ready(5), begin + 4), load_tile, 5)
    for j in range(4):
        slot = max(norm_slot + 1 + j, ready(4 + j) + 1)
        at_slot(slot, raise_up, j)
        if j >= 2:
            plan.setdefault(max(norm_slot + 1 + j - 2, ready(4 + j)), []).append((load_tile, (4 + j,)))
    raised = max(norm_slot + 4, ready(7) + 1)
    for k in range(planes):
        slot = planes * first_down + down_parts * (k + 1) + lag
        at_slot(slot, load_down, k)
        at_slot(max(slot + 1, raised), lower, k)
        if k == planes // 2:
            at_slot(slot, load_cot)
    last = max(max(plan), len(units) + lag - 1)
    for n in range(last + 1):
        if n < len(units) + lag:
            pump(n)
        for step, args in plan.get(n, []):
            step(*args)
        if n == begin + 3:
            store(7, qkv_buf, qkv_out).start()
            store(8, mixed_buf, mixed_out).start()
    store(10, active_buf, active_out).start()
    second_norm()
    for which, source, target in (
        (0, attn_acc, normed_out), (1, inverse_buf, inverse_out), (2, hidden_buf, down_out),
        (3, down_acc, second_out), (4, result_buf, result_out), (7, qkv_buf, qkv_out),
        (8, mixed_buf, mixed_out), (9, sums_buf, sums_out), (10, active_buf, active_out),
    ):
        store(which, source, target).wait()
    for j in range(2, 4):
        slope_store(j).wait()
    exchange(1, cot_ref, cot_full).wait_send()
    for which, land in deal_parts:
        for k in range(1, groups):
            deal(which, land, k).wait_send()
    for c in range(len(tiles)):
        z_each(c, lambda copy: copy.wait_send())
        if relayed:
            @pl.when(middle)
            def _():
                for j in range(1, planes):
                    z_pass(c, j).wait_send()
    for u, (c, j) in enumerate(units):
        if c not in across_first or j == 0:
            x_copy(c, j, across).wait_send()
        unit_core(u, core).wait_send()


def forward(shard_list, dealt_rows, cot, lengths, dealing, vectors):
    planes = lax.axis_size("dp") // 4
    widths = [shard.shape[1] for shard in shard_list]
    total = sum(width // TILE for width in widths)
    half, features = cot.shape
    tokens, rows = 2 * half, shard_list[0].shape[0]
    head_cols, up_cols = widths[0], widths[4]
    groups = planes * 4
    whole, rest, padded, chunks = rest_shape(half // groups)
    whole_rows = dealt_rows[:, : max(whole, 16)] if whole else jnp.zeros((groups, 16, 128), jnp.bfloat16)
    rest_rows = jnp.pad(dealt_rows[:, whole:], ((0, 0), (0, padded - rest), (0, 0)))
    rest_rows = rest_rows.reshape(groups, padded, chunks, features // chunks)
    rest_rows = rest_rows.transpose(0, 2, 1, 3).reshape(groups, 16, features // chunks)
    sem, low, high = pltpu.SemaphoreType.DMA, jnp.bfloat16, jnp.float32
    hbm = pl.BlockSpec(memory_space=pl.ANY)
    shapes = [((planes, 2, 2, *shard.shape), low) for shard in shard_list] + [
        ((tokens, features), low), ((tokens, features), low), ((tokens, 3 * head_cols), low),
        ((tokens, head_cols), low), ((tokens, features), high), ((tokens, 128), high),
        ((tokens, features), low), ((tokens, up_cols), low), ((tokens, up_cols), low),
        ((half, features), low), ((tokens, features), low), ((tokens, features), high),
        ((3, 16, features), high),
    ]
    results = pl.pallas_call(
        partial(forward_kernel, planes, widths),
        out_shape=[jax.ShapeDtypeStruct(*shape) for shape in shapes],
        in_specs=[hbm] * (len(shard_list) + 3) + [pl.BlockSpec(memory_space=pltpu.SMEM)] * 2 + [hbm] * len(vectors),
        out_specs=[hbm] * len(shapes),
        scratch_shapes=[
            pltpu.VMEM((2, planes, 2, 2, rows, TILE), low),
            pltpu.VMEM((tokens, features), low),
            pltpu.VMEM((tokens, 3 * head_cols), low),
            pltpu.VMEM((tokens, head_cols), low),
            pltpu.VMEM((tokens, features), high),
            pltpu.VMEM((tokens, features), low),
            pltpu.VMEM((tokens, features), low),
            pltpu.VMEM((tokens, features), low),
            pltpu.VMEM((tokens, up_cols), low),
            pltpu.VMEM((2, tokens, TILE), low),
            pltpu.VMEM((tokens, features), high),
            pltpu.VMEM((tokens, features), low),
            pltpu.VMEM((tokens, 128), high),
            pltpu.VMEM((half, features), low),
            pltpu.VMEM((3, 16, features), high),
            pltpu.VMEM(whole_rows.shape, low),
            pltpu.VMEM(rest_rows.shape, low),
            pltpu.VMEM((1, 2 * head_cols + up_cols + 6 * features), high),
            pltpu.VMEM((8, tokens), high),
            sem((total, max(planes, 7))), *[sem((total, planes))] * 5,
            sem((2, max(planes, 4))), sem((2,)), sem((2,)),
            sem((planes,)), sem((planes,)), sem((planes,)), sem((planes,)), sem((3,)), sem((12,)),
            sem((2, groups)), sem((2, groups)), sem((len(vectors),)),
        ],
        compiler_params=pltpu.CompilerParams(
            collective_id=0, has_side_effects=True, vmem_limit_bytes=62 * 2**20
        ),
        name="forward_gather",
    )(*shard_list, whole_rows, rest_rows, cot, lengths, dealing, *vectors)
    return results[: len(shard_list)], results[len(shard_list) :]


JOB = 512
PLANE_FIRST = ()


def backward_kernel(planes, *refs):
    (
        query_w, key_w, value_w, out_w, up_w, down_w,
        x_in, qkv_in, mixed_in, normed_in, inverse_in, hidden_in, active_in, slope_in, down_in, second_in,
        sums_in, lengths_ref, dealing_ref, gain_ref,
    ) = refs[:20]
    (
        grad_query, grad_key, grad_value, grad_out_w, grad_up, grad_down, small_out, whole_out, rest_out,
        left_own, left_far, active_far, rise_own, rise_far, mixed_far, qkv_own, qkv_far,
    ) = refs[20:37]
    (
        left_buf, right_buf, stage, x_land, plane_land, out_buf, tile_buf, wide_buf, low_buf, rise_buf,
        slope_buf, acc_buf, hidden_land, send_buf, qkv_buf, turn_buf, input_land, row_buf, inverse_buf,
        sums_buf, small_land, whole_buf, rest_buf, rest_wide, mask_buf,
        left_sem, right_sem, out_sem, core_send, core_recv, left_send, left_recv, x_send, x_recv,
        plane_send, plane_recv, small_send, small_recv, tile_sem, wide_sem, slope_sem, load_sem, store_sem,
        turn_sem, hidden_send, hidden_recv, input_send, input_recv, row_sem, back_send, back_recv, first_send, first_recv,
    ) = refs[37:]
    plane, across, core, tensor = place()
    far = [lax.rem(plane + k, planes) for k in range(planes)]
    x_peer = device_of(plane, 1 - across, core, tensor)
    core_peer = device_of(plane, across, 1 - core, tensor)
    y_peer = device_of(plane, across, core, 1 - tensor)
    plane_peers = [device_of(far[k], across, core, tensor) for k in range(planes)]
    tokens, features = low_buf.shape
    half = tokens // 2
    head_cols = mixed_in.shape[1]
    heads = head_cols // HEAD_DIM
    up_cols = active_in.shape[1]
    block = features // planes
    factor = HEAD_DIM ** (-0.5)
    slots = x_land.shape[0]
    thin = tile_buf.shape[-1]

    jobs = [(0, active_in, active_far, s, grad_down, s, JOB) for s in range(0, up_cols, JOB)]
    jobs += [(1, rise_own, rise_far, s, grad_up, s, JOB) for s in range(0, up_cols, JOB)]
    jobs += [(2, mixed_in, mixed_far, s, grad_out_w, s, JOB) for s in range(0, head_cols, JOB)]
    for which, result in enumerate((grad_query, grad_key, grad_value)):
        jobs += [
            (3, qkv_own, qkv_far, which * head_cols + s, result, s, JOB) for s in range(0, head_cols, JOB)
        ]
    a, own, other, start, result, at, width = jobs.pop()
    jobs += [(a, own, other, start + s, result, at + s, width // 2) for s in (0, width // 2)]
    total = len(jobs)
    up_first, out_first, qkv_first = (
        [job[0] for job in jobs].index(a) for a in (1, 2, 3)
    )

    def local(source, target, sem):
        return pltpu.make_async_copy(source, target, sem)

    def remote(source, target, send, recv, peer):
        return pltpu.make_async_remote_copy(
            source, target, send, recv, device_id=peer, device_id_type=MESH
        )

    def left_out(a):
        return remote(
            turn_buf.at[:, :, 1 - core], left_far.at[a], left_send.at[a], left_recv.at[a], core_peer
        )

    def left_keep(a):
        return local(turn_buf.at[:, :, core], left_own.at[a], turn_sem.at[0])

    kept = set()

    def left_kept(a):
        if a not in kept:
            kept.add(a)
            left_keep(a).wait()

    def turn(a, source):
        if a > 0:
            left_out(a - 1).wait_send()
            left_kept(a - 1)

        @pl.loop(0, planes)
        def _(p):
            cols = pl.ds(pl.multiple_of(p * block, block), block)
            turn_buf[p] = source[:, cols].T.reshape(turn_buf.shape[1:])

        left_keep(a).start()
        left_out(a).start()

    def right_out(c, source=None):
        _, own, other, start, _, _, width = jobs[c]
        cols = pl.ds(start, width)
        return remote(
            (own if source is None else source).at[:, cols], other.at[:, cols], core_send.at[c],
            core_recv.at[c], core_peer,
        )

    def left_load(a):
        slot = a % 2
        copies = []
        for side in range(2):
            copies.append(
                local(left_own.at[a, :, side], left_buf.at[slot, side, :, :, pl.ds(0, tokens)], left_sem.at[slot, 0, side])
            )
            copies.append(
                local(left_far.at[a, :, side], left_buf.at[slot, side, :, :, pl.ds(tokens, tokens)], left_sem.at[slot, 1, side])
            )
        return copies

    def right_load(c):
        _, own, other, start, _, _, width = jobs[c]
        slot, cols, there = c % 2, pl.ds(start, width), pl.ds(0, width)
        return [
            local(own.at[:, cols], right_buf.at[slot, pl.ds(0, tokens), there], right_sem.at[slot, 0]),
            local(other.at[:, cols], right_buf.at[slot, pl.ds(tokens, tokens), there], right_sem.at[slot, 1]),
        ]

    def used(c):
        return pl.ds(0, jobs[c][-1])

    def x_out(c):
        return remote(
            stage.at[c % 3, 1 - across, :, :, used(c)], x_land.at[c % slots, :, :, used(c)], x_send.at[c], x_recv.at[c], x_peer
        )

    relayed = planes == 4
    middle = jnp.logical_and(plane > 0, plane < planes - 1)

    plane_first = PLANE_FIRST if relayed else ()

    def route(k):
        target, block_at, land = far[k], far[k], k - 1
        if relayed and k == 1:
            end = plane == planes - 1
            target, block_at, land = jnp.where(end, plane - 1, plane + 1), jnp.where(end, 0, plane + 1), jnp.where(end, 3, 0)
        if relayed and k == 3:
            end = plane == 0
            target, block_at, land = jnp.where(end, 1, plane - 1), jnp.where(end, planes - 1, plane - 1), jnp.where(end, 3, 2)
        return target, block_at, land

    def first_rows(c, side):
        rows = x_land.shape[2]
        return pl.ds(pl.multiple_of((plane_first.index(c) * 2 + side) * rows, rows), rows)

    def first_out(c, k, side):
        target, block_at, land = route(k)
        at = plane_first.index(c)
        return remote(
            stage.at[c % 3, side, block_at],
            qkv_buf.at[first_rows(c, side), pl.ds(pl.multiple_of(land * JOB, JOB), JOB)],
            first_send.at[at, k - 1, side], first_recv.at[at, land, side], device_of(target, across, core, tensor),
        )

    def first_in(c, land, side):
        here = qkv_buf.at[first_rows(c, side), pl.ds(land * JOB, JOB)]
        at = plane_first.index(c)
        return remote(here, here, first_send.at[at, 0, side], first_recv.at[at, land, side], x_peer)

    def first_start(c):
        for side in range(2):
            for k in (1, 3):
                first_out(c, k, side).start()

        @pl.when(jnp.logical_not(middle))
        def _():
            for side in range(2):
                first_out(c, 2, side).start()

    def first_relay(c):
        @pl.when(middle)
        def _():
            for side in range(2):
                first_in(c, 3, side).wait_recv()
                stage[c % 3, side, far[2]] = (
                    stage[c % 3, side, far[2]].astype(jnp.float32)
                    + qkv_buf[first_rows(c, side), 3 * JOB : 4 * JOB].astype(jnp.float32)
                ).astype(jnp.bfloat16)
                first_out(c, 2, side).start()

    def first_x(c):
        slot = c % slots
        return remote(x_land.at[slot, 1], x_land.at[slot, 2], x_send.at[c], x_recv.at[c], x_peer)

    def first_sum(c):
        for side in range(2):
            first_in(c, 1, side).wait_recv()

        @pl.when(plane > 0)
        def _():
            for side in range(2):
                first_in(c, 0, side).wait_recv()

        @pl.when(plane < planes - 1)
        def _():
            for side in range(2):
                first_in(c, 2, side).wait_recv()

        for at, side in enumerate((across, 1 - across)):
            value = stage[c % 3, side, plane].astype(jnp.float32)
            for land, there in ((0, plane > 0), (1, None), (2, plane < planes - 1)):
                part = qkv_buf[first_rows(c, side), land * JOB : (land + 1) * JOB].astype(jnp.float32)
                value += part if there is None else jnp.where(there, part, 0.0)
            x_land[c % slots, at] = value.astype(jnp.bfloat16)
        first_x(c).start()

    def plane_out(c, k):
        target, block_at, land = route(k)
        return remote(
            x_land.at[c % slots, block_at, :, used(c)], plane_land.at[c % slots, land, :, used(c)], plane_send.at[c, k - 1],
            plane_recv.at[c, land], device_of(target, across, core, tensor),
        )

    def plane_in(c, land):
        return remote(
            x_land.at[c % slots, plane, :, used(c)], plane_land.at[c % slots, land, :, used(c)], plane_send.at[c, 0],
            plane_recv.at[c, land], x_peer,
        )

    def relay(c):
        @pl.when(middle)
        def _():
            plane_in(c, 3).wait_recv()
            x_land[c % slots, far[2], :, used(c)] = (
                x_land[c % slots, far[2], :, used(c)].astype(jnp.float32)
                + plane_land[c % slots, 3, :, used(c)].astype(jnp.float32)
            ).astype(jnp.bfloat16)
            plane_out(c, 2).start()

    def grad_out(c):
        _, _, _, _, result, start, width = jobs[c]
        return local(out_buf.at[c % 2, :, used(c)], result.at[:, pl.ds(start, width)], out_sem.at[c % 2])

    def new_left(c):
        return c == 0 or jobs[c - 1][0] != jobs[c][0]

    def fetch(c):
        a = jobs[c][0]
        if new_left(c):
            left_kept(a)
            left_out(a).wait_recv()
            for copy in left_load(a):
                copy.start()
        right_out(c).wait_recv()
        for copy in right_load(c):
            copy.start()

    def multiply(c):
        a = jobs[c][0]
        if new_left(c):
            for copy in left_load(a):
                copy.wait()
        for copy in right_load(c):
            copy.wait()
        if c + 1 < total:
            fetch(c + 1)
        if c >= 3 and c - 3 in plane_first:
            for side in range(2):
                for k in range(1, planes):
                    first_out(c - 3, k, side).wait_send()
        elif c >= 3:
            x_out(c - 3).wait_send()

        @pl.loop(0, jobs[c][-1] // 256)
        def _(n):
            cols = pl.ds(pl.multiple_of(n * 256, 256), 256)
            left = left_buf[a % 2]
            result = jnp.dot(
                left.reshape(-1, left.shape[-1]), right_buf[c % 2, :, cols],
                preferred_element_type=jnp.float32,
            ).astype(jnp.bfloat16)
            stage[c % 3, :, :, :, cols] = result.reshape(*left.shape[:-1], 256)

        if c in plane_first:
            first_start(c)
        else:
            x_out(c).start()

    def fold(c):
        if c in plane_first:
            first_sum(c)
            return
        x_out(c).wait_recv()
        slot = c % slots

        @pl.loop(0, planes)
        def _(p):
            x_land[slot, p, :, used(c)] = (
                x_land[slot, p, :, used(c)].astype(jnp.float32)
                + stage[c % 3, across, p, :, used(c)].astype(jnp.float32)
            ).astype(jnp.bfloat16)

        for k in range(1, planes):
            if relayed and k == 2:
                @pl.when(jnp.logical_not(middle))
                def _():
                    plane_out(c, 2).start()
            else:
                plane_out(c, k).start()

    def finish(c):
        if c in plane_first:
            first_x(c).wait()
            if c >= 2:
                grad_out(c - 2).wait()
            out_buf[c % 2] = x_land[c % slots, 0].astype(jnp.float32) + x_land[c % slots, 2].astype(jnp.float32)
            grad_out(c).start()
            return
        for k in range(1, planes):
            plane_out(c, k).wait_send()
        if c >= 2:
            grad_out(c - 2).wait()
        out_buf[c % 2, :, used(c)] = x_land[c % slots, plane, :, used(c)].astype(jnp.float32)
        for land in range(planes - 1):
            def add():
                plane_in(c, land).wait_recv()
                out_buf[c % 2, :, used(c)] = out_buf[c % 2, :, used(c)] + plane_land[
                    c % slots, land, :, used(c)
                ].astype(jnp.float32)

            if relayed and land != 1:
                pl.when((plane > 0) if land == 0 else (plane < planes - 1))(add)
            else:
                add()
        grad_out(c).start()

    def small_copy(step, peer, slot):
        return remote(
            small_land.at[0], small_land.at[slot], small_send.at[step], small_recv.at[step], peer
        )

    def small_begin(step):
        if step < 3:
            small_copy(step, (core_peer, x_peer, y_peer)[step], 1 + step).start()
        else:
            for k in range(1, planes):
                small_copy(2 + k, plane_peers[k], 3 + k).start()

    def small_end(step):
        if step < 3:
            small_copy(step, core_peer, 1 + step).wait()
            small_land[0] = small_land[0] + small_land[1 + step]
        else:
            for k in range(1, planes):
                small_copy(2 + k, core_peer, 3 + k).wait()
            value = jnp.zeros(small_land.shape[1:], jnp.float32)
            for p in range(planes):
                back = lax.rem(plane + planes - p, planes)
                value += small_land[jnp.where(back == 0, 0, 3 + back)]
            small_land[1] = value
            local(small_land.at[1], small_out, load_sem.at[0]).start()

    def total_row(value):
        return jnp.sum(value, axis=0, keepdims=True)

    def tile_copy(weight, start, slot):
        return [
            local(weight.at[p, :, :, :, pl.ds(start, thin)], tile_buf.at[slot, p], tile_sem.at[slot, p])
            for p in range(planes)
        ]

    def slope_copy(start, slot):
        return local(slope_in.at[:, pl.ds(start, thin)], slope_buf.at[slot], slope_sem.at[slot])

    def flat(value):
        return value.reshape(-1, value.shape[-1])

    def rise_start(i):
        for copy in tile_copy(down_w, i * thin, i % 2):
            copy.start()
        slope_copy(i * thin, i % 2).start()

    def rise_store(g):
        cols = pl.ds(g * 2 * JOB, 2 * JOB)
        return local(rise_buf.at[:, cols], rise_own.at[:, cols], store_sem.at[g])

    def rise(g):
        per = 2 * JOB // thin
        for i in range(g * per, (g + 1) * per):
            for copy in tile_copy(down_w, i * thin, i % 2):
                copy.wait()
            slope_copy(i * thin, i % 2).wait()
            value = jnp.dot(low_buf[...], flat(tile_buf[i % 2]), preferred_element_type=jnp.float32)
            value = (value * slope_buf[i % 2].astype(jnp.float32)).astype(jnp.bfloat16)
            rise_buf[:, i * thin : (i + 1) * thin] = value
            if i + 2 < up_cols // thin:
                rise_start(i + 2)
            row = 3 + tensor * (up_cols // features) + (i * thin) // features
            col = (i * thin) % features
            small_land[0, pl.ds(row, 1), col : col + thin] = total_row(value.astype(jnp.float32))
        rise_store(g).start()
        for c in (up_first + 2 * g, up_first + 2 * g + 1):
            right_out(c, rise_buf).start()

    def block_cols(p):
        return pl.ds(pl.multiple_of(p * block, block), block)

    def wide_copy(p, side):
        return local(
            up_w.at[p, :, :, :, pl.ds(side * features, features)], wide_buf.at[side], wide_sem.at[side, 0]
        )

    def hidden_share(p):
        return remote(
            send_buf.at[:, block_cols(p)], hidden_land.at[:, block_cols(p)], hidden_send.at[p],
            hidden_recv.at[p], y_peer,
        )

    def hidden_start():
        for side in range(2):
            wide_copy(0, side).start()

    def hidden_back(first, last):
        @pl.loop(first, last)
        def _(p):
            value = None
            for side in range(2):
                wide_copy(p, side).wait()
                part = contract_cols(
                    rise_buf[:, side * features : (side + 1) * features], flat(wide_buf[side])
                )
                value = part if value is None else value + part

                @pl.when(p + 1 < planes)
                def _():
                    wide_copy(p + 1, side).start()

            acc_buf[:, block_cols(p)] = value
            send_buf[:, block_cols(p)] = value.astype(jnp.bfloat16)
            hidden_share(p).start()

    strip = row_buf.shape[2]

    def row_start(which, i):
        base = tensor if which == 0 else 1 - tensor
        return pl.multiple_of(base * half + i * strip, strip)

    def row_copies(which, i):
        rows = pl.ds(row_start(which, i), strip)
        slot = (which * (half // strip) + i) % 2
        return [
            local(normed_in.at[rows], row_buf.at[slot, 0], row_sem.at[slot, 0]),
            local(second_in.at[rows], row_buf.at[slot, 1], row_sem.at[slot, 1]),
        ]

    strips = [(which, i) for which in range(2) for i in range(half // strip)]

    def norm_start():
        for pair in strips[:2]:
            for copy in row_copies(*pair):
                copy.start()
        local(inverse_in, inverse_buf, load_sem.at[1]).start()

    def norm_back():
        @pl.loop(0, planes)
        def _(p):
            hidden_share(p).wait()

        local(inverse_in, inverse_buf, load_sem.at[1]).wait()
        sums_buf[...] = jnp.zeros_like(sums_buf)
        for at, (which, i) in enumerate(strips):
            for copy in row_copies(which, i):
                copy.wait()

            @pl.loop(0, strip // 16, unroll=2)
            def _(r):
                local_rows = pl.ds(pl.multiple_of(r * 16, 16), 16)
                rows = pl.ds(pl.multiple_of(row_start(which, i) + r * 16, 16), 16)
                normed = row_buf[at % 2, 0, local_rows, :]
                grad_hidden = row_buf[at % 2, 1, local_rows, :] + (
                    acc_buf[rows, :] + hidden_land[rows, :].astype(jnp.float32)
                )
                scaled = grad_hidden * gain_ref[...]
                grad = inverse_buf[rows, 0:1] * (
                    scaled
                    - jnp.mean(scaled, axis=-1, keepdims=True)
                    - normed * jnp.mean(scaled * normed, axis=-1, keepdims=True)
                )
                acc_buf[rows, :] = grad
                low = grad.astype(jnp.bfloat16)
                low_buf[rows, :] = low
                if which == 0:
                    sums_buf[0] += grad_hidden * normed
                    sums_buf[1] += grad_hidden
                    sums_buf[2] += low.astype(jnp.float32)

            if at + 2 < len(strips):
                for copy in row_copies(*strips[at + 2]):
                    copy.start()
        small_land[0, 8:9, :] = total_row(sums_buf[0])
        small_land[0, 9:10, :] = total_row(sums_buf[1])
        small_land[0, 2:3, :] = total_row(sums_buf[2])

    def mixed_start():
        for i in range(2):
            for copy in tile_copy(out_w, i * thin, i):
                copy.start()
        for g in range(up_cols // (2 * JOB)):
            for c in (up_first + 2 * g, up_first + 2 * g + 1):
                right_out(c, rise_buf).wait_send()
        local(qkv_in, rise_buf.at[:, pl.ds(0, 3 * head_cols)], load_sem.at[2]).start()

    def mixed_back():
        for i in range(head_cols // thin):
            for copy in tile_copy(out_w, i * thin, i % 2):
                copy.wait()
            value = jnp.dot(low_buf[...], flat(tile_buf[i % 2]), preferred_element_type=jnp.float32)
            start = 3 * head_cols + i * thin
            rise_buf[:, start : start + thin] = value.astype(jnp.bfloat16)
            if i + 2 < head_cols // thin:
                for copy in tile_copy(out_w, (i + 2) * thin, i % 2):
                    copy.start()

    def attend_back(first, last):
        @pl.loop(first, last)
        def _(h):
            def cols(which):
                return pl.ds(pl.multiple_of(which * head_cols + h * HEAD_DIM, HEAD_DIM), HEAD_DIM)

            key, value = rise_buf[:, cols(1)], rise_buf[:, cols(2)]
            key_sum = value_sum = None
            query_total = jnp.zeros((1, HEAD_DIM), jnp.float32)
            for part in range(2):
                rows = slice(part * half, (part + 1) * half)
                query, grad_mixed = rise_buf[rows, cols(0)], rise_buf[rows, cols(3)]
                scores = contract_cols(query, key) * factor
                scores = jnp.where(mask_buf[0:1, :] > 0.0, scores, MASKED)
                expanded = jnp.exp(scores - jnp.max(scores, axis=1, keepdims=True))
                weight = expanded / jnp.sum(expanded, axis=1, keepdims=True)
                grad_weight = contract_cols(grad_mixed, value)
                inner = jnp.sum(weight * grad_weight, axis=1, keepdims=True)
                grad_scores = (weight * (grad_weight - inner)).astype(jnp.bfloat16)
                grad_value = contract_rows(weight.astype(jnp.bfloat16), grad_mixed)
                grad_key = contract_rows(grad_scores, query)
                grad_query = (
                    jnp.dot(grad_scores, key, preferred_element_type=jnp.float32) * factor
                ).astype(jnp.bfloat16)
                qkv_buf[rows, cols(0)] = grad_query
                query_total += total_row(grad_query.astype(jnp.float32))
                key_sum = grad_key if key_sum is None else key_sum + grad_key
                value_sum = grad_value if value_sum is None else value_sum + grad_value
            qkv_buf[:, cols(1)] = (key_sum * factor).astype(jnp.bfloat16)
            value_low = value_sum.astype(jnp.bfloat16)
            qkv_buf[:, cols(2)] = value_low
            at = pl.ds(pl.multiple_of(tensor * head_cols + h * HEAD_DIM, HEAD_DIM), HEAD_DIM)
            small_land[0, 0:1, at] = query_total
            small_land[0, 1:2, at] = total_row(value_low.astype(jnp.float32))

    def attend_done():
        local(qkv_buf, qkv_own, store_sem.at[4]).start()
        for c in range(qkv_first, total):
            right_out(c, qkv_buf).start()
        input_start(0)

    def input_copies(p):
        return [
            local(query_w.at[p], wide_buf.at[0, :, :, :, pl.ds(0, head_cols)], wide_sem.at[0, 0]),
            local(key_w.at[p], wide_buf.at[0, :, :, :, pl.ds(head_cols, head_cols)], wide_sem.at[0, 1]),
            local(value_w.at[p], wide_buf.at[1, :, :, :, pl.ds(0, head_cols)], wide_sem.at[1, 0]),
        ]

    def input_start(p):
        for copy in input_copies(p):
            copy.start()

    own_rows = pl.ds(pl.multiple_of(tensor * half, half), half)
    other_rows = pl.ds(pl.multiple_of((1 - tensor) * half, half), half)

    def input_share(p):
        return remote(
            send_buf.at[pl.ds(0, half), block_cols(p)], input_land.at[:, block_cols(p)], input_send.at[p],
            input_recv.at[p], y_peer,
        )

    def input_back(first, last):
        @pl.loop(first, last)
        def _(p):
            for copy in input_copies(p):
                copy.wait()
            pair = flat(wide_buf[0])
            single = flat(wide_buf[1, :, :, :, 0:head_cols])

            def share(rows):
                return contract_cols(qkv_buf[rows, 0 : 2 * head_cols], pair) + contract_cols(
                    qkv_buf[rows, 2 * head_cols : 3 * head_cols], single
                )

            send_buf[0:half, block_cols(p)] = share(other_rows).astype(jnp.bfloat16)
            input_share(p).start()
            acc_buf[own_rows, block_cols(p)] += share(own_rows)

            @pl.when(p + 1 < planes)
            def _():
                input_start(p + 1)

    def input_done():
        @pl.loop(0, planes)
        def _(p):
            input_share(p).wait()

        @pl.loop(0, half // 16)
        def _(i):
            rows = pl.ds(pl.multiple_of(tensor * half + i * 16, 16), 16)
            land = pl.ds(pl.multiple_of(i * 16, 16), 16)
            acc_buf[land, :] = acc_buf[rows, :] + input_land[land, :].astype(jnp.float32)

    groups = planes * 4
    index = (plane * 2 + across) * 2 + core
    group = half // groups
    whole, rest, padded, chunks = rest_shape(group)
    rest_width = features // chunks
    back_parts = ((0, whole_buf, whole_out), (1, rest_buf, rest_out))[0 if whole else 1 :]

    def back(which, source, target, k):
        peer = lax.rem(index + k, groups)
        return remote(
            source.at[peer], target.at[index], back_send.at[which, k], back_recv.at[which, k], (peer, tensor)
        )

    def back_own(which, source, target):
        return local(source.at[index], target.at[index], back_recv.at[which, 0])

    def send_back():
        rest_wide[...] = jnp.zeros_like(rest_wide)
        for s in range(groups):
            start = s * group
            if whole:
                whole_buf[s] = acc_buf[start : start + whole, :].astype(jnp.bfloat16)
            for q in range(chunks):
                rest_wide[q * padded : q * padded + rest, :] = acc_buf[
                    start + whole : start + group, q * rest_width : (q + 1) * rest_width
                ]
            rest_buf[s] = rest_wide[...].astype(jnp.bfloat16)
        for part in back_parts:
            back_own(*part).start()

    def back_some(i):
        for k in range(1 + i, groups, 5):
            for part in back_parts:
                back(*part, k).start()

    def back_wait():
        for part in back_parts:
            back_own(*part).wait()
            for k in range(1, groups):
                back(*part, k).wait()

    local(down_in, low_buf, load_sem.at[0]).start()
    local(hidden_in, send_buf, load_sem.at[1]).start()
    local(sums_in, sums_buf, load_sem.at[2]).start()
    rise_start(0)
    rise_start(1)
    enter([(lax.rem(index + k, groups), tensor) for k in range(1, groups)] + [y_peer])
    for c in range(up_first):
        right_out(c).start()
    local(down_in, low_buf, load_sem.at[0]).wait()
    turn(0, low_buf)
    mask_buf[...] = (
        lax.broadcasted_iota(jnp.int32, mask_buf.shape, 1) < lengths_ref[dealing_ref[index]]
    ).astype(jnp.float32)
    small_land[0] = jnp.zeros(small_land.shape[1:], jnp.float32)
    local(sums_in, sums_buf, load_sem.at[2]).wait()
    for i, row in enumerate((10, 11, 7)):
        small_land[0, row : row + 1, :] = total_row(sums_buf[i])
    fetch(0)

    def turn_hidden():
        local(hidden_in, send_buf, load_sem.at[1]).wait()
        turn(1, send_buf)

    def stored():
        for g in range(up_cols // (2 * JOB)):
            rise_store(g).wait()

    def load_input():
        local(x_in, low_buf, load_sem.at[1]).start()

    def turn_input():
        local(x_in, low_buf, load_sem.at[1]).wait()
        turn(3, low_buf)

    def start_out():
        for c in range(out_first, qkv_first):
            right_out(c).start()

    def wait_qkv():
        local(qkv_in, rise_buf.at[:, pl.ds(0, 3 * head_cols)], load_sem.at[2]).wait()

    def store_qkv_wait():
        local(qkv_buf, qkv_own, store_sem.at[4]).wait()

    plan = {
        0: [(rise, 0)],
        1: [(rise, 1), (rise, 2)],
        2: [(rise, 3), (turn_hidden,), (hidden_start,)],
        3: [(hidden_back, 0, planes // 2)],
        4: [(hidden_back, planes // 2, planes), (norm_start,), (start_out,), (stored,)],
        9: [(norm_back,), (mixed_start,)],
        10: [(turn, 2, low_buf), (mixed_back,), (load_input,)],
        11: [(wait_qkv,), (attend_back, 0, heads // 4), (turn_input,)],
        12: [(attend_back, heads // 4, heads // 2)],
        13: [(attend_back, heads // 2, 3 * heads // 4)],
        14: [(attend_back, 3 * heads // 4, heads), (attend_done,), (store_qkv_wait,)],
        15: [(input_back, 0, planes // 2), (small_begin, 0)],
        16: [(input_back, planes // 2, planes), (small_end, 0), (small_begin, 1)],
        17: [(small_end, 1), (small_begin, 2)],
        18: [(input_done,), (send_back,), (back_some, 0), (small_end, 2), (small_begin, 3)],
        19: [(back_some, 1), (small_end, 3)],
        20: [(back_some, 2)],
        21: [(back_some, 3)],
        22: [(back_some, 4)],
    }
    for n in range(total + 4):
        if n < total:
            multiply(n)
        for step in plan.get(n, []):
            step[0](*step[1:])
        if n - 1 in plane_first:
            first_relay(n - 1)
        if 2 <= n < total + 2:
            fold(n - 2)
        if relayed and 3 <= n < total + 3 and n - 3 not in plane_first:
            relay(n - 3)
        if n >= 4:
            finish(n - 4)
    local(small_land.at[1], small_out, load_sem.at[0]).wait()
    back_wait()
    left_out(3).wait_send()
    for c in range(total):
        if not up_first <= c < out_first:
            right_out(c).wait_send()
        if c >= total - 3:
            x_out(c).wait_send()
    for c in range(total - 2, total):
        grad_out(c).wait()


def backward(weights, saved, lengths, dealing, gain):
    planes, _, _, rows, head_cols = weights[0].shape
    up_cols = weights[4].shape[-1]
    tokens, features = saved[0].shape
    total = (2 * up_cols + 4 * head_cols) // JOB + 1
    slots, lands = 8, max(planes - 1, 4)
    thin, strip = 256, 64
    sem, low, high = pltpu.SemaphoreType.DMA, jnp.bfloat16, jnp.float32
    hbm, vmem = pl.BlockSpec(memory_space=pl.ANY), pl.BlockSpec(memory_space=pltpu.VMEM)
    small_rows = 16
    groups = planes * 4
    whole, rest, padded, chunks = rest_shape(tokens // 2 // groups)
    whole_shape = ((groups, whole, features) if whole else (groups, 16, 128), low)
    rest_rows = ((groups, 16, features // chunks), low)
    shapes = (
        [((rows, head_cols), high)] * 4 + [((rows, up_cols), high)] * 2
        + [((small_rows, features), high), whole_shape, rest_rows]
        + [((4, planes, 2, rows, tokens), low)] * 2
        + [((tokens, up_cols), low)] * 3 + [((tokens, head_cols), low)] + [((tokens, 3 * head_cols), low)] * 2
    )
    scratch = [
        ((2, 2, planes, rows, 2 * tokens), low), ((2, 2 * tokens, JOB), low), ((3, 2, planes, rows, JOB), low),
        ((slots, planes, rows, JOB), low), ((slots, lands, rows, JOB), low), ((2, rows, JOB), high),
        ((2, planes, 2, 2, rows, thin), low), ((2, 2, 2, rows, features), low), ((tokens, features), low),
        ((tokens, up_cols), low), ((2, tokens, thin), low), ((tokens, features), high),
        ((tokens, features), low), ((tokens, features), low), ((tokens, 3 * head_cols), low),
        ((planes, 2, 2, rows, tokens), low), ((tokens // 2, features), low), ((2, 2, strip, features), high),
        ((tokens, 128), high), ((3, 16, features), high), ((3 + planes, small_rows, features), high),
        whole_shape, rest_rows, ((16, features // chunks), high), ((8, tokens), high),
    ]
    sems = [
        (2, 2, 2), (2, 2), (2,), (total,), (total,), (4,), (4,), (total,), (total,),
        (total, planes - 1), (total, lands), (2 + planes,), (2 + planes,), (2, planes), (2, 2), (2,),
        (4,), (5,), (1,), (planes,), (planes,), (planes,), (planes,), (2, 2), (2, groups), (2, groups),
        (2, 3, 2), (2, 4, 2),
    ]
    results = pl.pallas_call(
        partial(backward_kernel, planes),
        out_shape=[jax.ShapeDtypeStruct(*shape) for shape in shapes],
        in_specs=[hbm] * 17 + [pl.BlockSpec(memory_space=pltpu.SMEM)] * 2 + [vmem],
        out_specs=[hbm] * len(shapes),
        scratch_shapes=[pltpu.VMEM(*shape) for shape in scratch] + [sem(shape) for shape in sems],
        compiler_params=pltpu.CompilerParams(
            collective_id=1, has_side_effects=True, vmem_limit_bytes=62 * 2**20
        ),
        name="backward_scatter",
    )(*weights, *saved, lengths, dealing, gain)
    whole_rows, rest_rows = results[7], results[8]
    rest_rows = rest_rows.reshape(groups, chunks, padded, features // chunks).transpose(0, 2, 1, 3)
    returned = rest_rows.reshape(groups, padded, features)[:, :rest]
    if whole:
        returned = jnp.concatenate((whole_rows, returned), axis=1)
    return results[:6], results[6], returned


def shards(
    inputs,
    lengths,
    dealing,
    w_query,
    w_key,
    w_value,
    b_query,
    b_value,
    w_out,
    b_out,
    gain_first,
    shift_first,
    w_up,
    b_up,
    w_down,
    b_down,
    gain_second,
    shift_second,
    cotangent,
):
    ordered = inputs.at[dealing].get(mode="promise_in_bounds", unique_indices=True)
    features = cotangent.shape[-1]
    half_rows = cotangent.shape[1]
    vectors = [
        vector.reshape(1, -1)
        for vector in (
            b_query, b_value, b_out, gain_first, shift_first, b_up, b_down, gain_second, shift_second,
        )
    ]
    weights, saved = forward(
        [w_query, w_key, w_value, w_out.T, w_up, w_down.T],
        ordered.reshape(ordered.shape[0], -1, features), cotangent.reshape(half_rows, features), lengths, dealing, vectors,
    )
    (
        full_in, _, qkv, mixed_heads, normed_full, inverse_full, full_hidden, active, slope,
        result, full_grad_down, second_full, second_sums,
    ) = saved
    output = result.reshape(cotangent.shape)
    grads, small_total, grad_own = backward(
        weights,
        [
            full_in, qkv, mixed_heads, normed_full, inverse_full, full_hidden, active, slope,
            full_grad_down, second_full, second_sums,
        ],
        lengths, dealing, gain_first.reshape(1, -1),
    )
    returned = grad_own.reshape(inputs.shape)
    grad_inputs = jnp.zeros_like(returned).at[dealing].set(returned)
    weight_sums = (grads[0], grads[1], grads[2], grads[3].T, grads[4], grads[5].T)
    up_rows = b_up.shape[0] // features
    small_sums = (
        small_total[0], small_total[1], small_total[2], small_total[3 : 3 + up_rows].reshape(-1),
        small_total[7], small_total[8], small_total[9], small_total[10], small_total[11],
    )
    return (
        output,
        grad_inputs,
        weight_sums[0],
        weight_sums[1],
        weight_sums[2],
        small_sums[0],
        small_sums[1],
        weight_sums[3],
        small_sums[2],
        small_sums[5],
        small_sums[6],
        weight_sums[4],
        small_sums[3],
        weight_sums[5],
        small_sums[4],
        small_sums[7],
        small_sums[8],
    )


def solution(mesh):
    in_specs = (
        P(None, "tensor", "dp", None),
        P(),
        P(),
        P("dp", "tensor"),
        P("dp", "tensor"),
        P("dp", "tensor"),
        P(),
        P(),
        P("tensor", "dp"),
        P(),
        P(),
        P(),
        P("dp", "tensor"),
        P(),
        P("tensor", "dp"),
        P(),
        P(),
        P(),
        P("dp", "tensor", None),
    )
    out_specs = (
        P("dp", "tensor", None),
        P(None, "tensor", "dp", None),
        P("dp", "tensor"),
        P("dp", "tensor"),
        P("dp", "tensor"),
        P(),
        P(),
        P("tensor", "dp"),
        P(),
        P(),
        P(),
        P("dp", "tensor"),
        P(),
        P("tensor", "dp"),
        P(),
        P(),
        P(),
    )
    return jax.shard_map(shards, mesh=mesh, in_specs=in_specs, out_specs=out_specs, check_vma=False)
```
